32 devices in a mesh: samp: 4 (over x, core), win: 8 (over z, y).
Axes of the slice: x: 2, y: 2, z: 4, core: 2. Of those that a mesh axis runs over, the one named last changes fastest.
Arguments:
- atoms: bfloat16 [64, 8192, 128], P('samp', 'win'), may hold values from -6 to 6
- cond: float32 [8, 8192, 128], P('samp', 'win'), may hold values from -6 to 6
- pair: bfloat16 [8, 8192, 16, 128], P('samp', 'win'), may hold values from -6 to 6
- struct_ids: int32 [64], P('samp'), may hold values from 0 to 7, as said below
- cotangent: bfloat16 [64, 8192, 128], P('samp', 'win'), may hold values from -6 to 6
- weights: float32 [17, 128, 128], replicated
- vectors: float32 [7, 128], replicated
- pair_weight: float32 [16, 4], replicated, may hold values from -1.5 to 1.5
- stat_left: float32 [17, 128, 128], P(None, 'win'), as said below
- stat_right: float32 [17, 128, 128], P(None, 'win')
- root_left: float32 [17, 128, 128], P(None, 'win')
- root_right: float32 [17, 128, 128], replicated
- stat_vectors: float32 [7, 128], replicated, may hold values from 47185.92 to 188743.69
- stat_pair: float32 [16, 4], replicated, may hold values from 47185.92 to 188743.69
- ema_weights: float32 [17, 128, 128], P(None, 'win'), may hold values from -0.5 to 0.5
- ema_vectors: float32 [7, 128], replicated, may hold values from -3 to 3
- ema_pair: float32 [16, 4], replicated, may hold values from -1.5 to 1.5
Outputs:
- out: bfloat16 [64, 8192, 128], P('samp', 'win')
- grad_atoms: bfloat16 [64, 8192, 128], P('samp', 'win')
- grad_weights: float32 [17, 128, 128], P(None, 'win')
- grad_vectors: float32 [7, 128], replicated
- grad_pair_weight: float32 [16, 4], replicated
- new_left: float32 [17, 128, 128], P(None, 'win')
- new_right: float32 [17, 128, 128], P(None, 'win')
- new_weights: float32 [17, 128, 128], P(None, 'win')
- new_weights_low: bfloat16 [17, 128, 128], P(None, 'win')
- new_vectors: float32 [7, 128], replicated
- new_pair_weight: float32 [16, 4], replicated
- new_stat_vectors: float32 [7, 128], replicated
- new_stat_pair: float32 [16, 4], replicated
- new_ema_weights: float32 [17, 128, 128], P(None, 'win')
- new_ema_vectors: float32 [7, 128], replicated
- new_ema_pair: float32 [16, 4], replicated
The draws below stay inside these ranges and needn't reach their ends.
Inputs may be any that keep to these rules, and one draw needn't show every extreme that they name: `struct_ids`: sample n names a structure among the 2 structures that start at n // 16 * 2; every structure is named by exactly 8 samples. `stat_left`: each block of the statistics and of the roots is symmetric.
All inputs are finite; a program needn't handle non-finite values.
Results may differ from the reference program's by a relative error of at most 0.015.
The reference program's roundings to bfloat16 on the way count: a program that leaves them out, or rounds other values in their place, can miss the bound.
Values may be sent and summed in bfloat16 or wider, within the bound.
No kernel may reach another device: no remote copies, remote signals or barrier semaphores. Data moves between devices by JAX's collectives and lax.ppermute only.
A program may use at most 576 MiB of HBM per device.

```python
import math
import jax
import jax.numpy as jnp
from jax import lax

C = 128
HEADS = 4
FF = 256
PAIR = 16
QW = 32
HALO = 48
KW = 128
ATOMS = 8192
STRUCTURES_LOCAL = 2
SAMPLES_PER_ITEM = 8
SAMP_DEV = 16
SAMPLES = 64
STRUCTS = 8
NBLK = 17


def grad_size():
    return 0.3 * (SAMPLES * ATOMS) ** 0.5


def spd_draw(key, salt, base_scale):
    key_noise = jax.random.fold_in(key, salt)
    key_diag = jax.random.fold_in(key, salt + 1)
    noise_raw = jax.random.normal(key_noise, (NBLK, C, C), jnp.float32)
    symmetric = (noise_raw + jnp.swapaxes(noise_raw, 1, 2)) * 0.7071
    diagonal = jnp.exp(jax.random.uniform(key_diag, (NBLK, C), jnp.float32, 0.0, math.log(4.0)))
    identity = jnp.eye(C, dtype=jnp.float32)
    return base_scale * (identity * diagonal[:, :, None] + 0.3 * C ** (-0.5) * symmetric * (1.0 - identity))


def draw_stat_left(key, part):
    return spd_draw(key, 101, C * grad_size() ** 2)


def draw_stat_right(key, part):
    return spd_draw(key, 203, C * grad_size() ** 2)


def draw_root_left(key, part):
    return spd_draw(key, 307, (C * grad_size() ** 2) ** (-0.25))


def draw_root_right(key, part):
    return spd_draw(key, 409, (C * grad_size() ** 2) ** (-0.25))


def draw_weights(key, part):
    key_main = jax.random.fold_in(key, 503)
    noise_raw = jax.random.normal(key_main, (NBLK, C, C), jnp.float32)
    block_index = jnp.arange(NBLK)[:, None, None]
    factor = jnp.where(block_index == 6, 8.0 * C ** (-0.5), jnp.where(block_index >= 11 + 2 * FF // C, 4.0 * FF ** (-0.5), C ** (-0.5)))
    return noise_raw * factor


def draw_vectors(key, part):
    key_main = jax.random.fold_in(key, 607)
    noise_raw = jax.random.normal(key_main, (7, C), jnp.float32)
    row_index = jnp.arange(7)[:, None]
    is_gain = (row_index == 0) | (row_index == 4)
    return jnp.where(is_gain, 1.0 + 0.15 * noise_raw, 0.5 * noise_raw)


def draw_struct_ids(key, part):
    count_of_blocks = SAMPLES // SAMP_DEV
    key_main = jax.random.fold_in(key, 709)
    sub_keys = jax.random.split(key_main, count_of_blocks)
    sorting_orders = jax.vmap(lambda sub_key: jax.random.permutation(sub_key, SAMP_DEV))(sub_keys)
    structure_lookup = jnp.arange(count_of_blocks, dtype=jnp.int32)[:, None] * STRUCTURES_LOCAL + sorting_orders.astype(jnp.int32) // SAMPLES_PER_ITEM
    return structure_lookup.reshape(SAMPLES).astype(jnp.int32)


def block_levels(stream_key, shape, pieces, least, largest):
    def one(axis_at, parts):
        heights = jax.random.uniform(jax.random.fold_in(jax.random.fold_in(stream_key, 6), axis_at), (parts,), jnp.float32, least / len(pieces), largest / len(pieces))
        return jnp.repeat(jnp.exp(heights), shape[axis_at] // parts).reshape((-1,) + (1,) * (len(shape) - axis_at - 1))

    gain = one(*pieces[0])
    for cut in pieces[1:]:
        gain = gain * one(*cut)
    return gain


def gaussian(own_key, dims, scale, bound, cuts=(), kind=jnp.bfloat16):
    values = scale * jax.random.normal(own_key, dims, jnp.float32)
    if cuts:
        values = values * block_levels(own_key, dims, cuts, -0.22, 0.18)
    return jnp.clip(values, -bound, bound).astype(kind)


def setup_inputs(seed: int = 0) -> dict:
    arg_keys = jax.random.split(jax.random.key(seed), 18)
    atoms = gaussian(arg_keys[0], (SAMPLES, ATOMS, C), 1.0, 6.0, ((0, 4), (1, 8)))
    cond = gaussian(arg_keys[1], (STRUCTS, ATOMS, C), 1.0, 6.0, ((0, 4), (1, 8)), jnp.float32)
    pair = gaussian(arg_keys[2], (STRUCTS, ATOMS, PAIR, KW), 1.0, 6.0, ((0, 4), (1, 8)))
    struct_ids = draw_struct_ids(jax.random.fold_in(arg_keys[17], 71), 0)
    cotangent = gaussian(arg_keys[4], (SAMPLES, ATOMS, C), 1.0, 6.0, ((0, 4), (1, 8)))
    weights = draw_weights(jax.random.fold_in(arg_keys[17], 71), 0)
    vectors = draw_vectors(jax.random.fold_in(arg_keys[17], 71), 0)
    pair_weight = gaussian(arg_keys[7], (PAIR, HEADS), PAIR ** -0.5, 1.5, (), jnp.float32)
    stat_left = draw_stat_left(jax.random.fold_in(arg_keys[17], 71), 0)
    stat_right = draw_stat_right(jax.random.fold_in(arg_keys[17], 71), 0)
    root_left = draw_root_left(jax.random.fold_in(arg_keys[17], 71), 0)
    root_right = draw_root_right(jax.random.fold_in(arg_keys[17], 71), 0)
    stat_vectors = jnp.clip(jnp.exp(jax.random.uniform(arg_keys[12], (7, C), jnp.float32, math.log(47185.92), math.log(188743.69))), 47185.92, 188743.69)
    stat_pair = jnp.clip(jnp.exp(jax.random.uniform(arg_keys[13], (PAIR, HEADS), jnp.float32, math.log(47185.92), math.log(188743.69))), 47185.92, 188743.69)
    ema_weights = gaussian(arg_keys[14], (NBLK, C, C), C ** -0.5, 0.5, ((1, 8),), jnp.float32)
    ema_vectors = gaussian(arg_keys[15], (7, C), 0.5, 3.0, (), jnp.float32)
    ema_pair = gaussian(arg_keys[16], (PAIR, HEADS), PAIR ** -0.5, 1.5, (), jnp.float32)
    return dict(atoms=atoms, cond=cond, pair=pair, struct_ids=struct_ids, cotangent=cotangent, weights=weights, vectors=vectors, pair_weight=pair_weight, stat_left=stat_left, stat_right=stat_right, root_left=root_left, root_right=root_right, stat_vectors=stat_vectors, stat_pair=stat_pair, ema_weights=ema_weights, ema_vectors=ema_vectors, ema_pair=ema_pair)


@jax.custom_vjp
def low(v):
    return lax.optimization_barrier(v.astype(jnp.bfloat16)).astype(jnp.float32)

@jax.custom_vjp
def low_back(v):
    return v

def low_keep(v):
    return (low(v), None)

def low_pass(kept, grad):
    return (grad,)

def back_keep(v):
    return (v, None)

def back_low(kept, grad):
    return (low(grad),)
low.defvjp(low_keep, low_pass)
low_back.defvjp(back_keep, back_low)
stat_decay = 0.5
ema_decay = 0.8
matrix_rate = 1.0
vector_rate = 0.2

def layer_norm(values, axis=-1):
    center = values - lax.optimization_barrier(jnp.mean(values, axis=axis, keepdims=True))
    spread = lax.optimization_barrier(jnp.mean(center * center, axis=axis, keepdims=True))
    return center * lax.rsqrt(spread + 1e-05)

def matmul_high(left, right):
    return jnp.einsum('...c,cd->...d', left, right, precision=lax.Precision.HIGHEST)

def windows(padded, count):
    blocks = padded.reshape(count + 3, QW, padded.shape[-1])
    return jnp.concatenate([blocks[offset:offset + count] for offset in range(4)], axis=1)

def reference(atoms, cond, pair, struct_ids, cotangent, weights, vectors, pair_weight, stat_left, stat_right, root_left, root_right, stat_vectors, stat_pair, ema_weights, ema_vectors, ema_pair):
    high = lax.Precision.HIGHEST
    count = ATOMS // QW
    in_blocks = 2 * FF // C
    out_base = 11 + in_blocks
    head_dim = C // HEADS
    factor = 1.0 / math.sqrt(head_dim)
    key_pos = jnp.arange(count)[:, None] * QW - HALO + jnp.arange(KW)[None, :]
    key_valid = (key_pos >= 0) & (key_pos < ATOMS)
    cond_norm = layer_norm(cond)
    pair_norm = layer_norm(pair.astype(jnp.float32), axis=2)

    def forward(atom_in, weight_in, vector_in, pair_in):
        low_weights = low(weight_in)
        cond_one = low(cond_norm * vector_in[0])
        cond_two = low(cond_norm * vector_in[4])
        scale_one = jax.nn.sigmoid(low_back(matmul_high(cond_one, low_weights[0]) + vector_in[1]))
        shift_one = low_back(matmul_high(cond_one, low_weights[1]))
        gate_one = jax.nn.sigmoid(low_back(matmul_high(cond_one, low_weights[7]) + vector_in[3]))
        scale_two = jax.nn.sigmoid(low_back(matmul_high(cond_two, low_weights[8]) + vector_in[5]))
        shift_two = low_back(matmul_high(cond_two, low_weights[9]))
        gate_two = jax.nn.sigmoid(low_back(matmul_high(cond_two, low_weights[10]) + vector_in[6]))
        bias = jnp.einsum('sack,ch->shak', pair_norm, pair_in, precision=high)
        bias = bias.reshape(STRUCTS, HEADS, count, QW, KW)
        in_weights = jnp.concatenate([low_weights[11 + offset] for offset in range(in_blocks)], axis=1)
        out_weights = jnp.concatenate([low_weights[out_base + offset] for offset in range(FF // C)], axis=0)

        def one_sample(sample_in, struct_id):
            normed = layer_norm(sample_in)
            ada_rows = low(scale_one[struct_id] * normed + shift_one[struct_id])
            queries = low(low_back(matmul_high(ada_rows, low_weights[2]) + vector_in[2]))
            key_rows = low(matmul_high(ada_rows, low_weights[3]))
            value_rows = low(matmul_high(ada_rows, low_weights[4]))
            attn_gate = jax.nn.sigmoid(low_back(matmul_high(ada_rows, low_weights[5])))
            key_win = low_back(windows(jnp.pad(key_rows, ((HALO, HALO), (0, 0))), count)).reshape(count, KW, HEADS, head_dim)
            value_win = low_back(windows(jnp.pad(value_rows, ((HALO, HALO), (0, 0))), count)).reshape(count, KW, HEADS, head_dim)
            query_heads = queries.reshape(count, QW, HEADS, head_dim)
            scores = jnp.einsum('wqhd,wkhd->hwqk', query_heads, key_win, precision=high) * factor + bias[struct_id]
            scores = low_back(scores)
            scores = jnp.where(key_valid[None, :, None, :], scores, -1000000000.0)
            row_top = lax.optimization_barrier(jnp.max(scores, axis=-1, keepdims=True))
            row_exp = jnp.exp(scores - row_top)
            attn_probs = row_exp / lax.optimization_barrier(jnp.sum(row_exp, axis=-1, keepdims=True))
            attn_mix = jnp.einsum('hwqk,wkhd->wqhd', low(attn_probs), value_win, precision=high).reshape(ATOMS, C)
            attn_mix = low_back(attn_mix)
            mixed_low = low(attn_gate * attn_mix)
            hidden_one = sample_in + gate_one[struct_id] * low_back(matmul_high(mixed_low, low_weights[6]))
            ada_two = low(scale_two[struct_id] * layer_norm(hidden_one) + shift_two[struct_id])
            expand = matmul_high(ada_two, in_weights)
            gate_ff = low_back(expand[:, :FF])
            up_ff = low_back(expand[:, FF:])
            hidden_low = low(jax.nn.silu(gate_ff) * up_ff)
            return hidden_one + gate_two[struct_id] * low_back(matmul_high(hidden_low, out_weights))

        def scan_step(carry, items):
            return (carry, jax.checkpoint(one_sample)(items[0], items[1]))
        _, results = lax.scan(scan_step, jnp.zeros((), jnp.float32), (atom_in, struct_ids))
        return results
    atom_in = atoms.astype(jnp.float32)
    results, pull = jax.vjp(forward, atom_in, weights, vectors, pair_weight)
    grad_in, grad_w, grad_v, grad_p = pull(cotangent.astype(jnp.float32))
    left_new = stat_decay * stat_left + (1.0 - stat_decay) * jnp.einsum('bij,bkj->bik', grad_w, grad_w, precision=high)
    right_new = stat_decay * stat_right + (1.0 - stat_decay) * jnp.einsum('bji,bjk->bik', grad_w, grad_w, precision=high)
    update_step = jnp.einsum('bij,bjk->bik', jnp.einsum('bij,bjk->bik', root_left, grad_w, precision=high), root_right, precision=high)
    weights_new = weights - matrix_rate * update_step
    stat_v_new = stat_decay * stat_vectors + (1.0 - stat_decay) * grad_v * grad_v
    vectors_new = vectors - vector_rate * grad_v * lax.rsqrt(stat_v_new)
    stat_p_new = stat_decay * stat_pair + (1.0 - stat_decay) * grad_p * grad_p
    pair_new = pair_weight - vector_rate * grad_p * lax.rsqrt(stat_p_new)
    return (results.astype(jnp.bfloat16), grad_in.astype(jnp.bfloat16), grad_w, grad_v, grad_p, left_new, right_new, weights_new, weights_new.astype(jnp.bfloat16), vectors_new, pair_new, stat_v_new, stat_p_new, ema_decay * ema_weights + (1.0 - ema_decay) * weights_new, ema_decay * ema_vectors + (1.0 - ema_decay) * vectors_new, ema_decay * ema_pair + (1.0 - ema_decay) * pair_new)
```

```python
import functools
import math

import jax
import jax.numpy as jnp
from jax import lax
from jax.experimental import pallas as pl
from jax.experimental.pallas import tpu as pltpu
from jax.sharding import PartitionSpec as P

HEADS = 4
FF = 256
QW = 32
HALO = 48
KW = 128
C = 128
PAIR = 16
NBLK = 17
GROUP = 4

stat_decay = 0.5
ema_decay = 0.8
matrix_rate = 1.0
vector_rate = 0.2

F32 = jnp.float32
BF16 = jnp.bfloat16
LOG2E = math.log2(math.e)
FACTOR = 1.0 / math.sqrt(C // HEADS)
INVALID = -1000000000.0
VMEM_LIMIT = 60 * 1024 * 1024


def dot(left, right):
    return lax.dot_general(left, right, (((1,), (0,)), ((), ())), preferred_element_type=F32)


def dot_nt(left, right):
    return lax.dot_general(left, right, (((1,), (1,)), ((), ())), preferred_element_type=F32)


def dot_tn(left, right):
    return lax.dot_general(left, right, (((0,), (0,)), ((), ())), preferred_element_type=F32)


def layer_stats(values):
    center = values - jnp.mean(values, axis=-1, keepdims=True)
    inverse = lax.rsqrt(jnp.mean(center * center, axis=-1, keepdims=True) + 1e-05)
    return (center * inverse, inverse)


def layer_back(normed, inverse, grad_norm):
    return inverse * (
        grad_norm
        - jnp.mean(grad_norm, axis=-1, keepdims=True)
        - normed * jnp.mean(grad_norm * normed, axis=-1, keepdims=True)
    )


def rows_sum(values):
    return jnp.sum(values, axis=0, keepdims=True)


def normed_channels(scratch, start):
    channels = [scratch[pl.ds(start + c, 8, stride=PAIR), :] for c in range(PAIR)]
    mean = sum(channels[1:], channels[0]) * (1.0 / PAIR)
    center = [channel - mean for channel in channels]
    squares = [part * part for part in center]
    spread = sum(squares[1:], squares[0]) * (1.0 / PAIR)
    return center, lax.rsqrt(spread + 1e-05)


def bias_kernel(base_ref, pair_ref, pw_ref, bias_ref, flat, tile):
    group = pl.program_id(1)
    flat[...] = pair_ref[0].astype(F32).reshape(flat.shape)
    for w in range(GROUP):
        for part in range(QW // 8):
            center, inverse = normed_channels(flat, (w * QW + part * 8) * PAIR)
            for h in range(HEADS):
                terms = [center[c] * pw_ref[c, h] for c in range(PAIR)]
                total = sum(terms[1:], terms[0]) * inverse
                tile[w, h * QW + part * 8 : h * QW + part * 8 + 8, :] = total
    for w in range(GROUP):
        start = base_ref[0] + (group * GROUP + w) * QW - HALO
        position = start + lax.broadcasted_iota(jnp.int32, (KW, C), 0)
        valid = (position >= 0) & (position < base_ref[1])
        bias_ref[0, w] = jnp.where(valid, tile[w].T * LOG2E, INVALID * LOG2E)


def bias_table(base, pair, pair_weight):
    structs, atoms = pair.shape[:2]
    rows = GROUP * QW
    return pl.pallas_call(
        bias_kernel,
        grid_spec=pltpu.PrefetchScalarGridSpec(
            num_scalar_prefetch=1,
            grid=(structs, atoms // rows),
            in_specs=[
                pl.BlockSpec((1, rows, PAIR, KW), lambda s, i, _: (s, i, 0, 0)),
                pl.BlockSpec(memory_space=pltpu.SMEM),
            ],
            out_specs=pl.BlockSpec((1, GROUP, KW, C), lambda s, i, _: (s, i, 0, 0)),
            scratch_shapes=[
                pltpu.VMEM((rows * PAIR, KW), F32),
                pltpu.VMEM((GROUP, C, KW), F32),
            ],
        ),
        out_shape=jax.ShapeDtypeStruct((structs, atoms // QW, KW, C), F32),
        compiler_params=pltpu.CompilerParams(vmem_limit_bytes=VMEM_LIMIT),
        cost_estimate=pl.CostEstimate(flops=10**8, bytes_accessed=13 * 2**20, transcendentals=0),
        name="pair_bias",
    )(base, pair, pair_weight)


def pair_grad_kernel(pair_ref, dbias_ref, out_ref, flat, tile):
    first = (pl.program_id(0) == 0) & (pl.program_id(1) == 0)

    @pl.when(first)
    def _():
        out_ref[...] = jnp.zeros_like(out_ref)

    flat[...] = pair_ref[0].astype(F32).reshape(flat.shape)
    for w in range(GROUP):
        tile[w] = dbias_ref[0, w].T
    for w in range(GROUP):
        for part in range(QW // 8):
            center, inverse = normed_channels(flat, (w * QW + part * 8) * PAIR)
            for h in range(HEADS):
                grad = tile[w, h * QW + part * 8 : h * QW + part * 8 + 8, :] * inverse
                for c in range(PAIR):
                    out_ref[c * HEADS + h] += center[c] * grad


def pair_grad(pair, dbias):
    structs, atoms = pair.shape[:2]
    rows = GROUP * QW
    return pl.pallas_call(
        pair_grad_kernel,
        grid=(structs, atoms // rows),
        in_specs=[
            pl.BlockSpec((1, rows, PAIR, KW), lambda s, i: (s, i, 0, 0)),
            pl.BlockSpec((1, GROUP, KW, C), lambda s, i: (s, i, 0, 0)),
        ],
        out_specs=pl.BlockSpec((PAIR * HEADS, 8, KW), lambda s, i: (0, 0, 0)),
        scratch_shapes=[
            pltpu.VMEM((rows * PAIR, KW), F32),
            pltpu.VMEM((GROUP, C, KW), F32),
        ],
        out_shape=jax.ShapeDtypeStruct((PAIR * HEADS, 8, KW), F32),
        compiler_params=pltpu.CompilerParams(vmem_limit_bytes=VMEM_LIMIT),
        cost_estimate=pl.CostEstimate(flops=10**8, bytes_accessed=13 * 2**20, transcendentals=0),
        name="pair_grad",
    )(pair, dbias)


def main_kernel(
    ids_ref,
    x_ref,
    xlo_ref,
    xhi_ref,
    g_ref,
    bias_ref,
    cond_ref,
    clo_ref,
    chi_ref,
    w_ref,
    vec_ref,
    out_ref,
    grad_ref,
    gxb_ref,
    rlo_ref,
    rhi_ref,
    dbias_ref,
    gw_ref,
    dvec_ref,
    accb_ref,
    tabb_ref,
    wq,
    w6,
    win,
    wo,
    wc1,
    wc2,
    mask,
    t_s1,
    t_h1,
    t_hs,
    t_hh,
    t_g1,
    t_s2,
    t_h2,
    t_g2,
    a_s1,
    a_h1,
    a_g1,
    a_s2,
    a_h2,
    a_g2,
    k_scr,
    v_scr,
    q_scr,
    gate_scr,
    ada_scr,
    n1_scr,
    inv_scr,
    o_scr,
    p_scr,
    do_scr,
    dd_scr,
    d4_scr,
    dk_scr,
    dv_scr,
    dx_scr,
):
    step = pl.program_id(0)
    structs, atoms, _ = cond_ref.shape
    windows = atoms // QW
    tile = min(256, atoms)
    tiles = atoms // tile
    s = ids_ref[step]

    def cond_rows(source):
        normed, _ = layer_stats(source)
        one = (normed * vec_ref[0:1]).astype(BF16)
        two = (normed * vec_ref[4:5]).astype(BF16)
        return normed, one, two

    @pl.when(step == 0)
    def _():
        def low(b):
            return w_ref[b].astype(BF16)

        for at, b in enumerate((2, 5, 3, 4)):
            wq[:, at * C : at * C + C] = low(b)
        w6[...] = low(6)
        for at in range(4):
            win[:, at * C : at * C + C] = low(11 + at)
        for at in range(2):
            wo[at * C : at * C + C, :] = low(15 + at)
        for at, b in enumerate((0, 1, 7)):
            wc1[:, at * C : at * C + C] = low(b)
        for at, b in enumerate((8, 9, 10)):
            wc2[:, at * C : at * C + C] = low(b)
        rows_head = lax.broadcasted_iota(jnp.int32, (C, C), 0) // QW
        lane_head = lax.broadcasted_iota(jnp.int32, (C, C), 1) // (C // HEADS)
        mask[...] = jnp.where(rows_head == lane_head, 1.0, 0.0).astype(BF16)
        for acc in (a_s1, a_h1, a_g1, a_s2, a_h2, a_g2, gw_ref, dvec_ref):
            acc[...] = jnp.zeros_like(acc)
        dbias_ref[...] = jnp.zeros_like(dbias_ref)
        for st in range(structs):

            def table(i, carry):
                rows = pl.ds(pl.multiple_of(i * tile, tile), tile)
                _, one, two = cond_rows(cond_ref[st, rows])
                first = dot(one, wc1[...])
                t_s1[st, rows] = jax.nn.sigmoid(first[:, :C] + vec_ref[1:2])
                t_h1[st, rows] = first[:, C : 2 * C]
                t_g1[st, rows] = jax.nn.sigmoid(first[:, 2 * C :] + vec_ref[3:4])
                second = dot(two, wc2[...])
                t_s2[st, rows] = jax.nn.sigmoid(second[:, :C] + vec_ref[5:6])
                t_h2[st, rows] = second[:, C : 2 * C]
                t_g2[st, rows] = jax.nn.sigmoid(second[:, 2 * C :] + vec_ref[6:7])
                return carry

            lax.fori_loop(0, tiles, table, 0)
            _, one, _ = cond_rows(jnp.concatenate([clo_ref[st], chi_ref[st]], axis=0))
            first = dot(one, wc1[:, : 2 * C])
            t_hs[st] = jax.nn.sigmoid(first[:, :C] + vec_ref[1:2])
            t_hh[st] = first[:, C:]
            tabb_ref[0, st, :HALO] = t_s1[st, :HALO]
            tabb_ref[0, st, HALO:] = t_s1[st, atoms - HALO :]
            tabb_ref[1, st, :HALO] = t_h1[st, :HALO]
            tabb_ref[1, st, HALO:] = t_h1[st, atoms - HALO :]

    def project(i, carry):
        start = pl.multiple_of(i * tile, tile)
        rows = pl.ds(start, tile)
        normed, inverse = layer_stats(x_ref[0, rows].astype(F32))
        n1_scr[rows] = normed
        inv_scr[rows] = jnp.broadcast_to(inverse, (tile, C))
        ada = (t_s1[s, rows] * normed + t_h1[s, rows]).astype(BF16)
        ada_scr[rows] = ada
        out = dot(ada, wq[...])
        q_scr[rows] = (out[:, :C] + vec_ref[2:3]).astype(BF16)
        gate_scr[rows] = jax.nn.sigmoid(out[:, C : 2 * C])
        pad = pl.ds(pl.multiple_of(start + HALO, 16), tile)
        k_scr[pad] = out[:, 2 * C : 3 * C].astype(BF16)
        v_scr[pad] = out[:, 3 * C :].astype(BF16)
        return carry

    lax.fori_loop(0, tiles, project, 0)
    halo = jnp.concatenate([xlo_ref[0], xhi_ref[0]], axis=0).astype(F32)
    normed, _ = layer_stats(halo)
    out = dot((t_hs[s] * normed + t_hh[s]).astype(BF16), wq[:, 2 * C :])
    k_scr[:HALO] = out[:HALO, :C].astype(BF16)
    v_scr[:HALO] = out[:HALO, C:].astype(BF16)
    k_scr[HALO + atoms :] = out[HALO:, :C].astype(BF16)
    v_scr[HALO + atoms :] = out[HALO:, C:].astype(BF16)

    lane_head = lax.broadcasted_iota(jnp.int32, (QW, C), 1) // (C // HEADS)

    def spread(rows):
        return jnp.concatenate([rows] * HEADS, axis=0) * mask[...]

    def gathered(full):
        parts = [full[h * QW : h * QW + QW] for h in range(HEADS)]
        last = parts[HEADS - 1]
        for h in range(HEADS - 2, -1, -1):
            last = jnp.where(lane_head == h, parts[h], last)
        return last

    def attend(i, carry):
        spans = []
        scores = []
        for u in range(GROUP):
            w = i * GROUP + u
            start = pl.multiple_of(w * QW, QW)
            spans.append((w, start))
            queries = spread(q_scr[pl.ds(start, QW)])
            scores.append(dot_nt(k_scr[pl.ds(start, KW)], queries))
        probs = []
        for u in range(GROUP):
            value = scores[u] * (FACTOR * LOG2E) + bias_ref[s, spans[u][0]]
            exps = jnp.exp2(value - jnp.max(value, axis=0, keepdims=True))
            prob = (exps * (1.0 / rows_sum(exps))).astype(BF16)
            p_scr[spans[u][0]] = prob
            probs.append(prob)
        for u in range(GROUP):
            start = spans[u][1]
            o_scr[pl.ds(start, QW)] = gathered(dot_tn(probs[u], v_scr[pl.ds(start, KW)]))
        return carry

    lax.fori_loop(0, windows // GROUP, attend, 0)

    def middle(i, carry):
        rows = pl.ds(pl.multiple_of(i * tile, tile), tile)
        gate = gate_scr[rows]
        mixed = o_scr[rows]
        y = (gate * mixed).astype(BF16)
        attn = dot(y, w6[...])
        gate_one = t_g1[s, rows]
        x1 = x_ref[0, rows].astype(F32) + gate_one * attn
        normed, inverse = layer_stats(x1)
        scale_two = t_s2[s, rows]
        ada = (scale_two * normed + t_h2[s, rows]).astype(BF16)
        expand = dot(ada, win[...])
        a = expand[:, :FF]
        b = expand[:, FF:]
        sig = jax.nn.sigmoid(a)
        silu = a * sig
        hid = (silu * b).astype(BF16)
        ff = dot(hid, wo[...])
        gate_two = t_g2[s, rows]
        out_ref[0, rows] = (x1 + gate_two * ff).astype(BF16)
        g = g_ref[0, rows].astype(F32)
        a_g2[s, rows] += g * ff
        dff = (g * gate_two).astype(BF16)
        dwo = dot_tn(dff, hid)
        gw_ref[15] += dwo[:, :C]
        gw_ref[16] += dwo[:, C:]
        dhid = dot_nt(dff, wo[...])
        da = (dhid * b * (sig + silu * (1.0 - sig))).astype(BF16)
        db = (dhid * silu).astype(BF16)
        dab = jnp.concatenate([da, db], axis=1)
        dwin = dot_tn(ada, dab)
        for at in range(4):
            gw_ref[11 + at] += dwin[:, at * C : at * C + C]
        dada = dot_nt(dab, win[...])
        a_s2[s, rows] += dada * normed
        a_h2[s, rows] += dada
        dx1 = g + layer_back(normed, inverse, dada * scale_two)
        dx_scr[rows] = dx1
        a_g1[s, rows] += dx1 * attn
        dattn = (dx1 * gate_one).astype(BF16)
        gw_ref[6] += dot_tn(y, dattn)
        dy = dot_nt(dattn, w6[...])
        do = (dy * gate).astype(BF16)
        do_scr[rows] = do
        dd_scr[rows] = (do.astype(F32) * mixed * -1.0).astype(BF16)
        d4_scr[rows, C : 2 * C] = (dy * mixed * gate * (1.0 - gate)).astype(BF16)
        return carry

    lax.fori_loop(0, tiles, middle, 0)

    dk_scr[...] = jnp.zeros_like(dk_scr)
    dv_scr[...] = jnp.zeros_like(dv_scr)
    ones = jnp.ones((KW, C), BF16)

    def attend_back(i, carry):
        items = []
        for u in range(GROUP):
            w = i * GROUP + u
            start = pl.multiple_of(w * QW, QW)
            dox = spread(do_scr[pl.ds(start, QW)])
            ddx = spread(dd_scr[pl.ds(start, QW)])
            values = jnp.concatenate([v_scr[pl.ds(start, KW)], ones], axis=1)
            diff = dot_nt(values, jnp.concatenate([dox, ddx], axis=1))
            items.append((w, start, dox, diff))
        grads = []
        for w, start, dox, diff in items:
            ds = p_scr[w] * diff.astype(BF16)
            dbias_ref[s, w] += ds.astype(F32)
            grads.append(ds)
        for u in range(GROUP):
            w, start, dox, _ = items[u]
            keys = pl.ds(start, KW)
            dq = gathered(dot_tn(grads[u], k_scr[keys])) * FACTOR
            dvec_ref[2] += jnp.sum(dq.reshape(QW // 8, 8, C), axis=0)
            d4_scr[pl.ds(start, QW), :C] = dq.astype(BF16)
            dk_scr[keys] += dot(grads[u], spread(q_scr[pl.ds(start, QW)]))
            dv_scr[keys] += dot(p_scr[w], dox)
        return carry

    lax.fori_loop(0, windows // GROUP, attend_back, 0)

    def finish(i, carry):
        start = pl.multiple_of(i * tile, tile)
        rows = pl.ds(start, tile)
        pad = pl.ds(pl.multiple_of(start + HALO, 16), tile)
        d4_scr[rows, 2 * C : 3 * C] = (dk_scr[pad] * FACTOR).astype(BF16)
        d4_scr[rows, 3 * C :] = dv_scr[pad].astype(BF16)
        d4 = d4_scr[rows]
        dwq = dot_tn(ada_scr[rows], d4)
        for at, b in enumerate((2, 5, 3, 4)):
            gw_ref[b] += dwq[:, at * C : at * C + C]
        dada = dot_nt(d4, wq[...])
        normed = n1_scr[rows]
        a_s1[s, rows] += dada * normed
        a_h1[s, rows] += dada
        grad = dx_scr[rows] + layer_back(normed, inv_scr[rows], dada * t_s1[s, rows])
        dx_scr[rows] = grad
        grad_ref[0, rows] = grad.astype(BF16)
        return carry

    lax.fori_loop(0, tiles, finish, 0)
    gxb_ref[0, :HALO] = dx_scr[:HALO]
    gxb_ref[0, HALO:] = dx_scr[atoms - HALO :]
    rlo_ref[0, 0] = (dk_scr[:HALO] * FACTOR).astype(BF16)
    rlo_ref[0, 1] = dv_scr[:HALO].astype(BF16)
    rhi_ref[0, 0] = (dk_scr[HALO + atoms :] * FACTOR).astype(BF16)
    rhi_ref[0, 1] = dv_scr[HALO + atoms :].astype(BF16)

    @pl.when(step == pl.num_programs(0) - 1)
    def _():
        for b in (15, 16):
            gw_ref[b] = gw_ref[b].T
        for st in range(structs):
            accb_ref[0, st, :HALO] = a_s1[st, :HALO]
            accb_ref[0, st, HALO:] = a_s1[st, atoms - HALO :]
            accb_ref[1, st, :HALO] = a_h1[st, :HALO]
            accb_ref[1, st, HALO:] = a_h1[st, atoms - HALO :]
            for acc in (a_s1, a_h1):
                acc[st, :HALO] = jnp.zeros((HALO, C), F32)
                acc[st, atoms - HALO :] = jnp.zeros((HALO, C), F32)

            def conditioning(i, carry):
                rows = pl.ds(pl.multiple_of(i * tile, tile), tile)
                normed, one, two = cond_rows(cond_ref[st, rows])

                def pre(acc, gate):
                    return (acc[st, rows] * gate[st, rows] * (1.0 - gate[st, rows])).astype(BF16)

                first = [pre(a_s1, t_s1), a_h1[st, rows].astype(BF16), pre(a_g1, t_g1)]
                second = [pre(a_s2, t_s2), a_h2[st, rows].astype(BF16), pre(a_g2, t_g2)]
                for at, part in ((1, first[0]), (3, first[2]), (5, second[0]), (6, second[2])):
                    dvec_ref[at] += jnp.sum(part.astype(F32).reshape(tile // 8, 8, C), axis=0)
                for at, source, parts, weight, blocks in (
                    (0, one, first, wc1, (0, 1, 7)),
                    (4, two, second, wc2, (8, 9, 10)),
                ):
                    joined = jnp.concatenate(parts, axis=1)
                    grads = dot_tn(source, joined)
                    for j, b in enumerate(blocks):
                        gw_ref[b] += grads[:, j * C : j * C + C]
                    back = dot_nt(joined, weight[...]) * normed
                    dvec_ref[at] += jnp.sum(back.reshape(tile // 8, 8, C), axis=0)
                return carry

            lax.fori_loop(0, tiles, conditioning, 0)


def main_call(ids, atoms, xlo, xhi, cotangent, bias, cond, clo, chi, weights, vectors):
    samples, rows, _ = atoms.shape
    structs = cond.shape[0]
    windows = rows // QW
    padded = rows + 2 * HALO

    def per_sample(*shape):
        zeros = (0,) * len(shape)
        return pl.BlockSpec((1,) + shape, lambda i, _: (i,) + zeros)

    def whole(*shape):
        zeros = (0,) * len(shape)
        return pl.BlockSpec(shape, lambda i, _: zeros, pipeline_mode=pl.Buffered(1))

    def table(count=rows):
        return pltpu.VMEM((structs, count, C), F32)

    shape = jax.ShapeDtypeStruct
    return pl.pallas_call(
        main_kernel,
        grid_spec=pltpu.PrefetchScalarGridSpec(
            num_scalar_prefetch=1,
            grid=(samples,),
            in_specs=[
                per_sample(rows, C),
                per_sample(HALO, C),
                per_sample(HALO, C),
                per_sample(rows, C),
                whole(structs, windows, KW, C),
                whole(structs, rows, C),
                whole(structs, HALO, C),
                whole(structs, HALO, C),
                whole(NBLK, C, C),
                whole(7, C),
            ],
            out_specs=[
                per_sample(rows, C),
                per_sample(rows, C),
                per_sample(2 * HALO, C),
                per_sample(2, HALO, C),
                per_sample(2, HALO, C),
                whole(structs, windows, KW, C),
                whole(NBLK, C, C),
                whole(7, 8, C),
                whole(2, structs, 2 * HALO, C),
                whole(2, structs, 2 * HALO, C),
            ],
            scratch_shapes=[
                pltpu.VMEM((C, 4 * C), BF16),
                pltpu.VMEM((C, C), BF16),
                pltpu.VMEM((C, 2 * FF), BF16),
                pltpu.VMEM((FF, C), BF16),
                pltpu.VMEM((C, 3 * C), BF16),
                pltpu.VMEM((C, 3 * C), BF16),
                pltpu.VMEM((C, C), BF16),
                table(),
                table(),
                table(2 * HALO),
                table(2 * HALO),
                table(),
                table(),
                table(),
                table(),
                table(),
                table(),
                table(),
                table(),
                table(),
                table(),
                pltpu.VMEM((padded, C), BF16),
                pltpu.VMEM((padded, C), BF16),
                pltpu.VMEM((rows, C), BF16),
                pltpu.VMEM((rows, C), F32),
                pltpu.VMEM((rows, C), BF16),
                pltpu.VMEM((rows, C), F32),
                pltpu.VMEM((rows, C), F32),
                pltpu.VMEM((rows, C), F32),
                pltpu.VMEM((windows, KW, C), BF16),
                pltpu.VMEM((rows, C), BF16),
                pltpu.VMEM((rows, C), BF16),
                pltpu.VMEM((rows, 4 * C), BF16),
                pltpu.VMEM((padded, C), F32),
                pltpu.VMEM((padded, C), F32),
                pltpu.VMEM((rows, C), F32),
            ],
        ),
        out_shape=[
            shape((samples, rows, C), BF16),
            shape((samples, rows, C), BF16),
            shape((samples, 2 * HALO, C), F32),
            shape((samples, 2, HALO, C), BF16),
            shape((samples, 2, HALO, C), BF16),
            shape((structs, windows, KW, C), F32),
            shape((NBLK, C, C), F32),
            shape((7, 8, C), F32),
            shape((2, structs, 2 * HALO, C), F32),
            shape((2, structs, 2 * HALO, C), F32),
        ],
        compiler_params=pltpu.CompilerParams(vmem_limit_bytes=VMEM_LIMIT),
        name="block",
    )(ids, atoms, xlo, xhi, cotangent, bias, cond, clo, chi, weights, vectors)


def rim_kernel(
    ids_ref,
    below_ref,
    above_ref,
    xlo_ref,
    xhi_ref,
    gxb_ref,
    tab_ref,
    acc_ref,
    cond_ref,
    w_ref,
    vec_ref,
    gw_ref,
    dvec_ref,
    grad_ref,
    gwo_ref,
    dveco_ref,
    sums,
    dw,
):
    samples = xlo_ref.shape[0]
    structs = cond_ref.shape[0]
    sums[...] = acc_ref[...]
    dw[...] = jnp.zeros_like(dw)
    weight = jnp.concatenate([w_ref[3], w_ref[4]], axis=1).astype(BF16)

    def one(i, carry):
        s = ids_ref[i]
        x = jnp.concatenate([xlo_ref[i], xhi_ref[i]], axis=0).astype(F32)
        normed, inverse = layer_stats(x)
        scale = tab_ref[0, s]
        ada = (scale * normed + tab_ref[1, s]).astype(BF16)
        dkv = jnp.concatenate(
            [
                jnp.concatenate([below_ref[i, 0], above_ref[i, 0]], axis=0),
                jnp.concatenate([below_ref[i, 1], above_ref[i, 1]], axis=0),
            ],
            axis=1,
        )
        dw[...] += dot_tn(ada, dkv)
        dada = dot_nt(dkv, weight)
        sums[0, s] += dada * normed
        sums[1, s] += dada
        grad_ref[i] = (gxb_ref[i] + layer_back(normed, inverse, dada * scale)).astype(BF16)
        return carry

    lax.fori_loop(0, samples, one, 0)
    gwo_ref[...] = gw_ref[...]
    gwo_ref[3] += dw[:, :C]
    gwo_ref[4] += dw[:, C:]
    dveco_ref[...] = dvec_ref[...]
    weight = jnp.concatenate([w_ref[0], w_ref[1]], axis=1).astype(BF16)
    for st in range(structs):
        normed, _ = layer_stats(cond_ref[st])
        source = (normed * vec_ref[0:1]).astype(BF16)
        scale = tab_ref[0, st]
        pre_scale = (sums[0, st] * scale * (1.0 - scale)).astype(BF16)
        pre_shift = sums[1, st].astype(BF16)
        joined = jnp.concatenate([pre_scale, pre_shift], axis=1)
        grads = dot_tn(source, joined)
        gwo_ref[0] += grads[:, :C]
        gwo_ref[1] += grads[:, C:]
        back = dot_nt(joined, weight) * normed
        dveco_ref[0] += jnp.sum(back.reshape(2 * HALO // 8, 8, C), axis=0)
        dveco_ref[1] += jnp.sum(pre_scale.astype(F32).reshape(2 * HALO // 8, 8, C), axis=0)


def rim_call(ids, below, above, xlo, xhi, gxb, tab, acc, cond, weights, vectors, gw, dvec):
    samples = xlo.shape[0]
    structs = cond.shape[0]
    full = pl.BlockSpec(memory_space=pltpu.VMEM)
    shape = jax.ShapeDtypeStruct
    return pl.pallas_call(
        rim_kernel,
        in_specs=[pl.BlockSpec(memory_space=pltpu.SMEM)] + [full] * 12,
        out_specs=[full] * 3,
        out_shape=[
            shape((samples, 2 * HALO, C), BF16),
            shape((NBLK, C, C), F32),
            shape((7, 8, C), F32),
        ],
        scratch_shapes=[
            pltpu.VMEM((2, structs, 2 * HALO, C), F32),
            pltpu.VMEM((C, 2 * C), F32),
        ],
        compiler_params=pltpu.CompilerParams(vmem_limit_bytes=VMEM_LIMIT),
        name="rims",
    )(ids, below, above, xlo, xhi, gxb, tab, acc, cond, weights, vectors, gw, dvec)


def passed(shard, by):
    devices = lax.axis_size("win")
    pairs = [(i, i + by) for i in range(devices) if 0 <= i + by < devices]
    return lax.ppermute(shard, "win", pairs)


def body(
    atoms,
    cond,
    pair,
    struct_ids,
    cotangent,
    weights,
    vectors,
    pair_weight,
    stat_left,
    stat_right,
    root_left,
    root_right,
    stat_vectors,
    stat_pair,
    ema_weights,
    ema_vectors,
    ema_pair,
):
    high = lax.Precision.HIGHEST
    rows = atoms.shape[1]
    struct_dev = cond.shape[0]
    win_index = lax.axis_index("win")
    win_count = lax.axis_size("win")
    ids = struct_ids - lax.axis_index("samp") * struct_dev
    x_first, x_last = atoms[:, :HALO], atoms[:, rows - HALO :]
    c_first, c_last = cond[:, :HALO], cond[:, rows - HALO :]
    xlo, xhi = passed(x_last, 1), passed(x_first, -1)
    clo, chi = passed(c_last, 1), passed(c_first, -1)
    base = jnp.stack([win_index * rows, jnp.int32(rows * win_count)]).astype(jnp.int32)
    bias = bias_table(base, pair, pair_weight)
    (result, grad_atoms, gxb, rim_low, rim_high, dbias, gw, dvec, accb, tabb) = main_call(
        ids, atoms, xlo, xhi, cotangent, bias, cond, clo, chi, weights, vectors
    )
    above = passed(rim_low, -1)
    below = passed(rim_high, 1)
    dpair = pair_grad(pair, dbias)
    cond_rim = jnp.concatenate([c_first, c_last], axis=1)
    grad_rim, gw, dvec = rim_call(
        ids, below, above, x_first, x_last, gxb, tabb, accb, cond_rim, weights, vectors, gw, dvec
    )
    grad_atoms = grad_atoms.at[:, :HALO].set(grad_rim[:, :HALO])
    grad_atoms = grad_atoms.at[:, rows - HALO :].set(grad_rim[:, HALO:])
    total_w, total_v, total_p = lax.psum(
        (gw, jnp.sum(dvec, axis=1), jnp.sum(dpair, axis=(1, 2)).reshape(PAIR, HEADS)),
        ("samp", "win"),
    )
    own_count = stat_left.shape[1]
    row_start = win_index * own_count
    own_rows = lax.dynamic_slice_in_dim(total_w, row_start, own_count, 1)
    own_cols = lax.dynamic_slice_in_dim(total_w, row_start, own_count, 2)
    left_new = stat_decay * stat_left + (1.0 - stat_decay) * jnp.einsum(
        "bic,bjc->bij", own_rows, total_w, precision=high
    )
    right_new = stat_decay * stat_right + (1.0 - stat_decay) * jnp.einsum(
        "bci,bcj->bij", own_cols, total_w, precision=high
    )
    left_part = jnp.einsum("bij,bjk->bik", root_left, total_w, precision=high)
    update_step = jnp.einsum("bik,bkl->bil", left_part, root_right, precision=high)
    weight_rows = lax.dynamic_slice_in_dim(weights, row_start, own_count, 1)
    weights_new = weight_rows - matrix_rate * update_step
    stat_v_new = stat_decay * stat_vectors + (1.0 - stat_decay) * total_v * total_v
    vectors_new = vectors - vector_rate * total_v * lax.rsqrt(stat_v_new)
    stat_p_new = stat_decay * stat_pair + (1.0 - stat_decay) * total_p * total_p
    pair_new = pair_weight - vector_rate * total_p * lax.rsqrt(stat_p_new)
    return (
        result,
        grad_atoms,
        own_rows,
        total_v,
        total_p,
        left_new,
        right_new,
        weights_new,
        weights_new.astype(BF16),
        vectors_new,
        pair_new,
        stat_v_new,
        stat_p_new,
        ema_decay * ema_weights + (1.0 - ema_decay) * weights_new,
        ema_decay * ema_vectors + (1.0 - ema_decay) * vectors_new,
        ema_decay * ema_pair + (1.0 - ema_decay) * pair_new,
    )


def solution(mesh):
    placed = (
        P("samp", "win", None),
        P("samp", "win", None),
        P("samp", "win", None, None),
        P("samp"),
        P("samp", "win", None),
        P(),
        P(),
        P(),
        P(None, "win", None),
        P(None, "win", None),
        P(None, "win", None),
        P(),
        P(),
        P(),
        P(None, "win", None),
        P(),
        P(),
    )
    return jax.shard_map(
        body,
        mesh=mesh,
        in_specs=placed,
        out_specs=(
            P("samp", "win", None),
            P("samp", "win", None),
            P(None, "win", None),
            P(),
            P(),
            P(None, "win", None),
            P(None, "win", None),
            P(None, "win", None),
            P(None, "win", None),
            P(),
            P(),
            P(),
            P(),
            P(None, "win", None),
            P(),
            P(),
        ),
        check_vma=False,
    )
```

```python
import functools
import math

import jax
import jax.numpy as jnp
from jax import lax
from jax.experimental import pallas as pl
from jax.experimental.pallas import tpu as pltpu
from jax.sharding import PartitionSpec as P

HEADS = 4
FF = 256
QW = 32
HALO = 48
KW = 128
C = 128
PAIR = 16
NBLK = 17
UNROLL = 8
PACK = 2
TILE = 512

stat_decay = 0.5
ema_decay = 0.8
matrix_rate = 1.0
vector_rate = 0.2

F32 = jnp.float32
BF16 = jnp.bfloat16
LOG2E = math.log2(math.e)
FACTOR = 1.0 / math.sqrt(C // HEADS)
INVALID = -1000000000.0
VMEM_LIMIT = 60 * 1024 * 1024
VEC_AT = NBLK * C
PW_AT = VEC_AT + 8
PACKED = 2240


def dot(left, right):
    return lax.dot_general(left, right, (((1,), (0,)), ((), ())), preferred_element_type=F32)


def dot_nt(left, right):
    return lax.dot_general(left, right, (((1,), (1,)), ((), ())), preferred_element_type=F32)


def dot_tn(left, right):
    return lax.dot_general(left, right, (((0,), (0,)), ((), ())), preferred_element_type=F32)


def layer_stats(values):
    center = values - jnp.mean(values, axis=-1, keepdims=True)
    inverse = lax.rsqrt(jnp.mean(center * center, axis=-1, keepdims=True) + 1e-05)
    return (center * inverse, inverse)


def layer_back(normed, inverse, grad_norm):
    return inverse * (
        grad_norm
        - jnp.mean(grad_norm, axis=-1, keepdims=True)
        - normed * jnp.mean(grad_norm * normed, axis=-1, keepdims=True)
    )


def pipeline(stages):
    waiting = list(stages)
    active = []
    while waiting or active:
        if waiting:
            active.append(waiting.pop(0))
        active = [item for item in active if next(item, active) is None]
        yield


def together(streams):
    count = len(streams[0])
    for at in range(count + len(streams) - 1):
        pipes = []
        for behind, phases in enumerate(streams):
            if 0 <= at - behind < count:
                depth, stages = phases[at - behind]
                pipes.append([pipeline(stages), depth + len(stages), 0])
        longest = max(length for _, length, _ in pipes)
        for tick in range(1, longest + 1):
            for item in pipes:
                while item[2] * longest < tick * item[1]:
                    item[2] += 1
                    next(item[0], None)
        for pipe, _, _ in pipes:
            for _ in pipe:
                pass


def rows_sum(values):
    return jnp.sum(values, axis=0, keepdims=True)


def bias_kernel(pair_ref, pw_ref, bias_ref, root_ref, expand):
    group = pl.program_id(1)
    per_step = bias_ref.shape[1]
    atoms = pl.num_programs(1) * per_step * QW

    @pl.when((pl.program_id(0) == 0) & (group == 0))
    def _():
        rows = lax.broadcasted_iota(jnp.int32, (QW * PAIR, C), 0) // PAIR
        lanes = lax.broadcasted_iota(jnp.int32, (QW * PAIR, C), 1) % QW
        same = rows == lanes
        weight = pw_ref[...] - jnp.mean(pw_ref[...], axis=0, keepdims=True)
        full = jnp.where(same, jnp.concatenate([weight] * QW, axis=0), 0.0)
        high = full.astype(BF16)
        expand[:, :C] = high
        expand[:, C : 2 * C] = (full - high.astype(F32)).astype(BF16)
        expand[:, 2 * C :] = jnp.where(same, 1.0 / PAIR, 0.0).astype(BF16)

    def one(w):
        low = pair_ref[0, w * QW : w * QW + QW].reshape(QW * PAIR, KW)
        wide = low.astype(F32)
        square = wide * wide
        high = square.astype(BF16)
        rest = (square - high.astype(F32)).astype(BF16)
        yield
        out = dot_tn(low, expand[...])
        second = dot_tn(high, expand[:, 2 * C :]) + dot_tn(rest, expand[:, 2 * C :])
        yield
        mean = out[:, 2 * C :]
        root = lax.rsqrt(jnp.maximum(second - mean * mean, 0.0) + 1e-05)
        value = (out[:, :C] + out[:, C : 2 * C]) * (root * LOG2E)
        start = lax.axis_index("win") * atoms + (group * per_step + w) * QW - HALO
        position = start + lax.broadcasted_iota(jnp.int32, (KW, C), 0)
        valid = (position >= 0) & (position < lax.axis_size("win") * atoms)
        bias_ref[0, w] = jnp.where(valid, value, INVALID * LOG2E)
        root_ref[0, w] = root.astype(BF16)

    for _ in pipeline([one(w) for w in range(per_step)]):
        pass


def bias_table(pair, wide_weight):
    structs, atoms = pair.shape[:2]
    count = min(8, atoms // QW)
    rows = count * QW
    return pl.pallas_call(
        bias_kernel,
        grid=(structs, atoms // rows),
        in_specs=[
            pl.BlockSpec((1, rows, PAIR, KW), lambda s, i: (s, i, 0, 0)),
            pl.BlockSpec((PAIR, C), lambda s, i: (0, 0)),
        ],
        out_specs=[
            pl.BlockSpec((1, count, KW, C), lambda s, i: (s, i, 0, 0)),
            pl.BlockSpec((1, count, KW, C), lambda s, i: (s, i, 0, 0)),
        ],
        scratch_shapes=[pltpu.VMEM((QW * PAIR, 3 * C), BF16)],
        out_shape=[
            jax.ShapeDtypeStruct((structs, atoms // QW, KW, C), F32),
            jax.ShapeDtypeStruct((structs, atoms // QW, KW, C), BF16),
        ],
        compiler_params=pltpu.CompilerParams(vmem_limit_bytes=VMEM_LIMIT),
        cost_estimate=pl.CostEstimate(flops=10**9, bytes_accessed=15 * 2**20, transcendentals=0),
        name="pair_bias",
    )(pair, wide_weight)


def pair_grad_kernel(pair_ref, dbias_ref, root_ref, out_ref, total):
    step = pl.program_id(0) * pl.num_programs(1) + pl.program_id(1)

    @pl.when(step == 0)
    def _():
        total[...] = jnp.zeros_like(total)

    parts = []
    for w in range(dbias_ref.shape[1]):
        low = pair_ref[0, w * QW : w * QW + QW].reshape(QW * PAIR, KW)
        grad = (dbias_ref[0, w] * root_ref[0, w].astype(F32)).astype(BF16)
        parts.append((low, grad))
    for at in range(0, len(parts), 2):
        pair_of = parts[at : at + 2]
        left = jnp.concatenate([low for low, _ in pair_of], axis=1)
        right = jnp.concatenate([grad for _, grad in pair_of], axis=0)
        total[...] += dot(left, right)

    @pl.when(step == pl.num_programs(0) * pl.num_programs(1) - 1)
    def _():
        lanes = lax.broadcasted_iota(jnp.int32, (PAIR, C), 1) % QW
        acc = jnp.zeros((PAIR, C), F32)
        for q in range(QW):
            acc = acc + jnp.where(lanes == q, total[q * PAIR : q * PAIR + PAIR], 0.0)
        out_ref[...] = acc - jnp.mean(acc, axis=0, keepdims=True)


def pair_grad(pair, dbias, root):
    structs, atoms = pair.shape[:2]
    count = min(8, atoms // QW)
    rows = count * QW
    table = pl.BlockSpec((1, count, KW, C), lambda s, i: (s, i, 0, 0))
    return pl.pallas_call(
        pair_grad_kernel,
        grid=(structs, atoms // rows),
        in_specs=[
            pl.BlockSpec((1, rows, PAIR, KW), lambda s, i: (s, i, 0, 0)),
            table,
            table,
        ],
        out_specs=pl.BlockSpec((PAIR, C), lambda s, i: (0, 0)),
        scratch_shapes=[pltpu.VMEM((QW * PAIR, C), F32)],
        out_shape=jax.ShapeDtypeStruct((PAIR, C), F32),
        compiler_params=pltpu.CompilerParams(vmem_limit_bytes=VMEM_LIMIT),
        cost_estimate=pl.CostEstimate(flops=10**9, bytes_accessed=15 * 2**20, transcendentals=0),
        name="pair_grad",
    )(pair, dbias, root)


def main_kernel(
    ids_ref,
    x_ref,
    xlo_ref,
    xhi_ref,
    g_ref,
    bias_ref,
    cond_ref,
    clo_ref,
    chi_ref,
    w_ref,
    vec_ref,
    out_ref,
    grad_ref,
    gxb_ref,
    rlo_ref,
    rhi_ref,
    dbias_ref,
    gw_ref,
    dvec_ref,
    accb_ref,
    tabb_ref,
    wq,
    w6,
    win,
    wo,
    wqt,
    w6t,
    wint,
    wot,
    wc1,
    wc2,
    mask,
    t_s1,
    t_h1,
    t_hs,
    t_hh,
    t_g1,
    t_s2,
    t_h2,
    t_g2,
    a_s1,
    a_h1,
    a_g1,
    a_s2,
    a_h2,
    a_g2,
    k_scr,
    v_scr,
    q_scr,
    gate_scr,
    ada_scr,
    n1_scr,
    inv_scr,
    o_scr,
    p_scr,
    do_scr,
    dd_scr,
    d4_scr,
    dk_scr,
    dv_scr,
    dx_scr,
):
    step = pl.program_id(0)
    structs, atoms, _ = cond_ref.shape
    windows = atoms // QW
    tile = min(TILE, atoms)
    tiles = atoms // tile
    s = [lax.rem(ids_ref[step * PACK + b], structs) for b in range(PACK)]

    def cond_rows(source):
        normed, _ = layer_stats(source)
        one = (normed * vec_ref[0:1]).astype(BF16)
        two = (normed * vec_ref[4:5]).astype(BF16)
        return normed, one, two

    def joined(ref, st):
        return ref[st].astype(F32) + ref[structs + st].astype(F32)

    @pl.when(step == 0)
    def _():
        def low(b):
            return w_ref[b].astype(BF16)

        for at, b in enumerate((2, 5, 3, 4)):
            wq[:, at * C : at * C + C] = low(b)
        w6[...] = low(6)
        for at in range(4):
            win[:, at * C : at * C + C] = low(11 + at)
        for at in range(2):
            wo[at * C : at * C + C, :] = low(15 + at)
        for source, turned in ((wq, wqt), (w6, w6t), (win, wint), (wo, wot)):
            turned[...] = source[...].T
        for at, b in enumerate((0, 1, 7)):
            wc1[:, at * C : at * C + C] = low(b)
        for at, b in enumerate((8, 9, 10)):
            wc2[:, at * C : at * C + C] = low(b)
        rows_head = lax.broadcasted_iota(jnp.int32, (C, C), 0) // QW
        lane_head = lax.broadcasted_iota(jnp.int32, (C, C), 1) // (C // HEADS)
        mask[...] = jnp.where(rows_head == lane_head, 1.0, 0.0).astype(BF16)
        for acc in (a_s1, a_h1, a_g1, a_s2, a_h2, a_g2, gw_ref, dvec_ref):
            acc[...] = jnp.zeros_like(acc)
        dbias_ref[...] = jnp.zeros_like(dbias_ref)
        for st in range(structs):

            def table(i, carry):
                rows = pl.ds(pl.multiple_of(i * tile, tile), tile)
                _, one, two = cond_rows(cond_ref[st, rows])
                first = dot(one, wc1[...])
                t_s1[st, rows] = jax.nn.sigmoid(first[:, :C] + vec_ref[1:2])
                t_h1[st, rows] = first[:, C : 2 * C]
                t_g1[st, rows] = jax.nn.sigmoid(first[:, 2 * C :] + vec_ref[3:4])
                second = dot(two, wc2[...])
                t_s2[st, rows] = jax.nn.sigmoid(second[:, :C] + vec_ref[5:6])
                t_h2[st, rows] = second[:, C : 2 * C]
                t_g2[st, rows] = jax.nn.sigmoid(second[:, 2 * C :] + vec_ref[6:7])
                return carry

            lax.fori_loop(0, tiles, table, 0)
            _, one, _ = cond_rows(jnp.concatenate([joined(clo_ref, st), joined(chi_ref, st)], axis=0))
            first = dot(one, wc1[:, : 2 * C])
            t_hs[st] = jax.nn.sigmoid(first[:, :C] + vec_ref[1:2])
            t_hh[st] = first[:, C:]
            tabb_ref[0, st, :HALO] = t_s1[st, :HALO]
            tabb_ref[0, st, HALO:] = t_s1[st, atoms - HALO :]
            tabb_ref[1, st, :HALO] = t_h1[st, :HALO]
            tabb_ref[1, st, HALO:] = t_h1[st, atoms - HALO :]

    def project(b, i):
        start = i * tile
        rows = pl.ds(start, tile)
        pad = pl.ds(start + HALO, tile)
        normed, inverse = layer_stats(x_ref[b, rows].astype(F32))
        n1_scr[b, rows] = normed
        inv_scr[b, rows] = jnp.broadcast_to(inverse, (tile, C))
        ada = (t_s1[s[b], rows] * normed + t_h1[s[b], rows]).astype(BF16)
        ada_scr[b, rows] = ada
        yield
        out = dot(ada, wq[...])
        yield
        q_scr[b, rows] = (out[:, :C] + vec_ref[2:3]).astype(BF16)
        gate_scr[b, rows] = jax.nn.sigmoid(out[:, C : 2 * C])
        k_scr[b, pad] = out[:, 2 * C : 3 * C].astype(BF16)
        v_scr[b, pad] = out[:, 3 * C :].astype(BF16)

    def project_halo(b):
        halo = jnp.concatenate([xlo_ref[b], xhi_ref[b]], axis=0).astype(F32)
        normed, _ = layer_stats(halo)
        ada = (t_hs[s[b]] * normed + t_hh[s[b]]).astype(BF16)
        yield
        out = dot(ada, wq[:, 2 * C :])
        yield
        k_scr[b, :HALO] = out[:HALO, :C].astype(BF16)
        v_scr[b, :HALO] = out[:HALO, C:].astype(BF16)
        k_scr[b, HALO + atoms :] = out[HALO:, :C].astype(BF16)
        v_scr[b, HALO + atoms :] = out[HALO:, C:].astype(BF16)

    lane_head = lax.broadcasted_iota(jnp.int32, (QW, C), 1) // (C // HEADS)

    def spread(rows):
        return jnp.concatenate([rows] * HEADS, axis=0) * mask[...]

    def gathered(full):
        parts = [full[h * QW : h * QW + QW] for h in range(HEADS)]
        last = parts[HEADS - 1]
        for h in range(HEADS - 2, -1, -1):
            last = jnp.where(lane_head == h, parts[h], last)
        return last

    def attend(b, group):
        scores = []
        for w in group:
            queries = spread(q_scr[b, w * QW : w * QW + QW])
            scores.append(dot(k_scr[b, w * QW : w * QW + KW], queries.T))
        yield
        probs = []
        for u, w in enumerate(group):
            value = scores[u] * (FACTOR * LOG2E) + bias_ref[s[b], w]
            exps = jnp.exp2(value - jnp.max(value, axis=0, keepdims=True))
            prob = (exps * (1.0 / rows_sum(exps))).astype(BF16)
            p_scr[b, w] = prob
            probs.append(prob)
        yield
        fulls = [dot_tn(probs[u], v_scr[b, w * QW : w * QW + KW]) for u, w in enumerate(group)]
        yield
        for u, w in enumerate(group):
            o_scr[b, w * QW : w * QW + QW] = gathered(fulls[u])

    def middle(b, i):
        rows = pl.ds(i * tile, tile)
        gate = gate_scr[b, rows]
        mixed = o_scr[b, rows]
        y = (gate * mixed).astype(BF16)
        yield
        attn = dot(y, w6[...])
        yield
        gate_one = t_g1[s[b], rows]
        x1 = x_ref[b, rows].astype(F32) + gate_one * attn
        normed, inverse = layer_stats(x1)
        scale_two = t_s2[s[b], rows]
        ada = (scale_two * normed + t_h2[s[b], rows]).astype(BF16)
        yield
        expand = dot(ada, win[...])
        yield
        a = expand[:, :FF]
        up = expand[:, FF:]
        sig = jax.nn.sigmoid(a)
        silu = a * sig
        hid = (silu * up).astype(BF16)
        yield
        ff = dot(hid, wo[...])
        gate_two = t_g2[s[b], rows]
        g = g_ref[b, rows].astype(F32)
        dff = (g * gate_two).astype(BF16)
        dhid = dot(dff, wot[...])
        yield
        out_ref[b, rows] = (x1 + gate_two * ff).astype(BF16)
        a_g2[s[b], rows] += g * ff
        da = (dhid * up * (sig + silu * (1.0 - sig))).astype(BF16)
        db = (dhid * silu).astype(BF16)
        dab = jnp.concatenate([da, db], axis=1)
        yield
        dada = dot(dab, wint[...])
        yield
        a_s2[s[b], rows] += dada * normed
        a_h2[s[b], rows] += dada
        dx1 = g + layer_back(normed, inverse, dada * scale_two)
        dx_scr[b, rows] = dx1
        a_g1[s[b], rows] += dx1 * attn
        dattn = (dx1 * gate_one).astype(BF16)
        yield
        dy = dot(dattn, w6t[...])
        dwo = dot_tn(dff, hid)
        dwin = dot_tn(ada, dab)
        dw6 = dot_tn(y, dattn)
        yield
        do = (dy * gate).astype(BF16)
        do_scr[b, rows] = do
        dd_scr[b, rows] = (do.astype(F32) * mixed * -1.0).astype(BF16)
        d4_scr[b, rows, C : 2 * C] = (dy * mixed * gate * (1.0 - gate)).astype(BF16)
        gw_ref[15] += dwo[:, :C]
        gw_ref[16] += dwo[:, C:]
        for at in range(4):
            gw_ref[11 + at] += dwin[:, at * C : at * C + C]
        gw_ref[6] += dw6

    dk_scr[...] = jnp.zeros_like(dk_scr)
    dv_scr[...] = jnp.zeros_like(dv_scr)
    ones = jnp.ones((KW, C), BF16)

    def attend_back(b, group):
        diffs = []
        spreads = []
        for w in group:
            dox = spread(do_scr[b, w * QW : w * QW + QW])
            ddx = spread(dd_scr[b, w * QW : w * QW + QW])
            values = jnp.concatenate([v_scr[b, w * QW : w * QW + KW], ones], axis=1)
            diffs.append(dot(values, jnp.concatenate([dox.T, ddx.T], axis=0)))
            spreads.append(dox)
        yield
        grads = []
        for u, w in enumerate(group):
            ds = p_scr[b, w] * diffs[u].astype(BF16)
            dbias_ref[s[b], w] += ds.astype(F32)
            grads.append(ds)
        yield
        fulls = []
        dks = []
        dvs = []
        for u, w in enumerate(group):
            fulls.append(dot_tn(grads[u], k_scr[b, w * QW : w * QW + KW]))
            dks.append(dot(grads[u], spread(q_scr[b, w * QW : w * QW + QW])))
            dvs.append(dot(p_scr[b, w], spreads[u]))
        yield
        for u, w in enumerate(group):
            dq = gathered(fulls[u]) * FACTOR
            dvec_ref[2] += jnp.sum(dq.reshape(QW // 8, 8, C), axis=0)
            d4_scr[b, w * QW : w * QW + QW, :C] = dq.astype(BF16)
            dk_scr[b, w * QW : w * QW + KW] += dks[u]
            dv_scr[b, w * QW : w * QW + KW] += dvs[u]

    def finish(b, i):
        start = i * tile
        rows = pl.ds(start, tile)
        pad = pl.ds(start + HALO, tile)
        d4_scr[b, rows, 2 * C : 3 * C] = (dk_scr[b, pad] * FACTOR).astype(BF16)
        d4_scr[b, rows, 3 * C :] = dv_scr[b, pad].astype(BF16)
        yield
        d4 = d4_scr[b, rows]
        dwq = dot_tn(ada_scr[b, rows], d4)
        dada = dot(d4, wqt[...])
        yield
        for at, block in enumerate((2, 5, 3, 4)):
            gw_ref[block] += dwq[:, at * C : at * C + C]
        normed = n1_scr[b, rows]
        a_s1[s[b], rows] += dada * normed
        a_h1[s[b], rows] += dada
        grad = dx_scr[b, rows] + layer_back(normed, inv_scr[b, rows], dada * t_s1[s[b], rows])
        dx_scr[b, rows] = grad
        grad_ref[b, rows] = grad.astype(BF16)

    groups = [tuple(range(at, at + UNROLL)) for at in range(0, windows, UNROLL)]

    def phases(b):
        return [
            (3, [project_halo(b)] + [project(b, i) for i in range(tiles)]),
            (4, [attend(b, group) for group in groups]),
            (11, [middle(b, i) for i in range(tiles)]),
            (4, [attend_back(b, group) for group in groups]),
            (3, [finish(b, i) for i in range(tiles)]),
        ]

    together([phases(b) for b in range(PACK)])
    for b in range(PACK):
        gxb_ref[b, :HALO] = dx_scr[b, :HALO]
        gxb_ref[b, HALO:] = dx_scr[b, atoms - HALO :]
        for ref, span in ((rlo_ref, slice(0, HALO)), (rhi_ref, slice(HALO + atoms, None))):
            ref[b, :, :C] = (dk_scr[b, span] * FACTOR).astype(BF16)
            ref[b, :, C:] = dv_scr[b, span].astype(BF16)

    @pl.when(step == pl.num_programs(0) - 1)
    def _():
        for b in (15, 16):
            gw_ref[b] = gw_ref[b].T
        for st in range(structs):
            accb_ref[0, st, :HALO] = a_s1[st, :HALO]
            accb_ref[0, st, HALO:] = a_s1[st, atoms - HALO :]
            accb_ref[1, st, :HALO] = a_h1[st, :HALO]
            accb_ref[1, st, HALO:] = a_h1[st, atoms - HALO :]
            for acc in (a_s1, a_h1):
                acc[st, :HALO] = jnp.zeros((HALO, C), F32)
                acc[st, atoms - HALO :] = jnp.zeros((HALO, C), F32)

            def conditioning(i, carry):
                rows = pl.ds(pl.multiple_of(i * tile, tile), tile)
                normed, one, two = cond_rows(cond_ref[st, rows])

                def pre(acc, gate):
                    return (acc[st, rows] * gate[st, rows] * (1.0 - gate[st, rows])).astype(BF16)

                first = [pre(a_s1, t_s1), a_h1[st, rows].astype(BF16), pre(a_g1, t_g1)]
                second = [pre(a_s2, t_s2), a_h2[st, rows].astype(BF16), pre(a_g2, t_g2)]
                for at, part in ((1, first[0]), (3, first[2]), (5, second[0]), (6, second[2])):
                    dvec_ref[at] += jnp.sum(part.astype(F32).reshape(tile // 8, 8, C), axis=0)
                for at, source, parts, weight, blocks in (
                    (0, one, first, wc1, (0, 1, 7)),
                    (4, two, second, wc2, (8, 9, 10)),
                ):
                    joined = jnp.concatenate(parts, axis=1)
                    grads = dot_tn(source, joined)
                    for j, b in enumerate(blocks):
                        gw_ref[b] += grads[:, j * C : j * C + C]
                    back = dot_nt(joined, weight[...]) * normed
                    dvec_ref[at] += jnp.sum(back.reshape(tile // 8, 8, C), axis=0)
                return carry

            lax.fori_loop(0, tiles, conditioning, 0)


def main_call(ids, atoms, low_msg, high_msg, cotangent, bias, cond, weights, vectors):
    samples, rows, _ = atoms.shape
    structs = cond.shape[0]
    windows = rows // QW
    padded = rows + 2 * HALO

    def per_sample(*shape):
        zeros = (0,) * len(shape)
        return pl.BlockSpec((PACK,) + shape, lambda i, _: (i,) + zeros)

    def whole(*shape):
        zeros = (0,) * len(shape)
        return pl.BlockSpec(shape, lambda i, _: zeros, pipeline_mode=pl.Buffered(1))

    def table(count=rows):
        return pltpu.VMEM((structs, count, C), F32)

    cond_part = pl.BlockSpec((2 * structs, HALO, C), lambda i, _: (samples // (2 * structs), 0, 0))
    shape = jax.ShapeDtypeStruct
    return pl.pallas_call(
        main_kernel,
        grid_spec=pltpu.PrefetchScalarGridSpec(
            num_scalar_prefetch=1,
            grid=(samples // PACK,),
            in_specs=[
                per_sample(rows, C),
                per_sample(HALO, C),
                per_sample(HALO, C),
                per_sample(rows, C),
                whole(structs, windows, KW, C),
                whole(structs, rows, C),
                cond_part,
                cond_part,
                whole(NBLK, C, C),
                whole(7, C),
            ],
            out_specs=[
                per_sample(rows, C),
                per_sample(rows, C),
                per_sample(2 * HALO, C),
                per_sample(HALO, 2 * C),
                per_sample(HALO, 2 * C),
                whole(structs, windows, KW, C),
                whole(NBLK, C, C),
                whole(7, 8, C),
                whole(2, structs, 2 * HALO, C),
                whole(2, structs, 2 * HALO, C),
            ],
            scratch_shapes=[
                pltpu.VMEM((C, 4 * C), BF16),
                pltpu.VMEM((C, C), BF16),
                pltpu.VMEM((C, 2 * FF), BF16),
                pltpu.VMEM((FF, C), BF16),
                pltpu.VMEM((4 * C, C), BF16),
                pltpu.VMEM((C, C), BF16),
                pltpu.VMEM((2 * FF, C), BF16),
                pltpu.VMEM((C, FF), BF16),
                pltpu.VMEM((C, 3 * C), BF16),
                pltpu.VMEM((C, 3 * C), BF16),
                pltpu.VMEM((C, C), BF16),
                table(),
                table(),
                table(2 * HALO),
                table(2 * HALO),
                table(),
                table(),
                table(),
                table(),
                table(),
                table(),
                table(),
                table(),
                table(),
                table(),
                pltpu.VMEM((PACK, padded, C), BF16),
                pltpu.VMEM((PACK, padded, C), BF16),
                pltpu.VMEM((PACK, rows, C), BF16),
                pltpu.VMEM((PACK, rows, C), F32),
                pltpu.VMEM((PACK, rows, C), BF16),
                pltpu.VMEM((PACK, rows, C), F32),
                pltpu.VMEM((PACK, rows, C), F32),
                pltpu.VMEM((PACK, rows, C), F32),
                pltpu.VMEM((PACK, windows, KW, C), BF16),
                pltpu.VMEM((PACK, rows, C), BF16),
                pltpu.VMEM((PACK, rows, C), BF16),
                pltpu.VMEM((PACK, rows, 4 * C), BF16),
                pltpu.VMEM((PACK, padded, C), F32),
                pltpu.VMEM((PACK, padded, C), F32),
                pltpu.VMEM((PACK, rows, C), F32),
            ],
        ),
        out_shape=[
            shape((samples, rows, C), BF16),
            shape((samples, rows, C), BF16),
            shape((samples, 2 * HALO, C), F32),
            shape((samples, HALO, 2 * C), BF16),
            shape((samples, HALO, 2 * C), BF16),
            shape((structs, windows, KW, C), F32),
            shape((NBLK, C, C), F32),
            shape((7, 8, C), F32),
            shape((2, structs, 2 * HALO, C), F32),
            shape((2, structs, 2 * HALO, C), F32),
        ],
        compiler_params=pltpu.CompilerParams(vmem_limit_bytes=VMEM_LIMIT),
        name="block",
    )(ids, atoms, low_msg, high_msg, cotangent, bias, cond, low_msg, high_msg, weights, vectors)


def rim_kernel(
    ids_ref,
    below_ref,
    above_ref,
    first_ref,
    last_ref,
    gxb_ref,
    tab_ref,
    acc_ref,
    w_ref,
    vec_ref,
    gw_ref,
    dvec_ref,
    dpair_ref,
    grad_ref,
    packed_ref,
    sums,
    dw,
):
    samples = below_ref.shape[0]
    structs = tab_ref.shape[1]
    sums[...] = acc_ref[...]
    dw[...] = jnp.zeros_like(dw)
    weight = jnp.concatenate([w_ref[3], w_ref[4]], axis=1).astype(BF16).T
    vecs = VEC_AT
    packed_ref[:vecs] = gw_ref[...].reshape(NBLK * C, C)
    packed_ref[vecs : vecs + 8] = jnp.concatenate(
        [jnp.sum(dvec_ref[at], axis=0, keepdims=True) for at in range(7)] + [jnp.zeros((1, C), F32)],
        axis=0,
    )
    packed_ref[PW_AT : PW_AT + PAIR] = dpair_ref[...]
    packed_ref[PW_AT + PAIR :] = jnp.zeros((PACKED - PW_AT - PAIR, C), F32)

    def one(i):
        s = lax.rem(ids_ref[i], structs)
        x = jnp.concatenate([first_ref[i], last_ref[i]], axis=0).astype(F32)
        normed, inverse = layer_stats(x)
        scale = tab_ref[0, s]
        ada = (scale * normed + tab_ref[1, s]).astype(BF16)
        dkv = jnp.concatenate([below_ref[i], above_ref[i]], axis=0)
        dada = dot(dkv, weight)
        yield
        part = dot_tn(ada, dkv)
        grad_norm = dada * scale
        grad = gxb_ref[i] + layer_back(normed, inverse, grad_norm)
        yield
        dw[...] += part
        sums[0, s] += dada * normed
        sums[1, s] += dada
        grad_ref[i] = grad.astype(BF16)

    for _ in pipeline([one(i) for i in range(samples)]):
        pass
    packed_ref[3 * C : 4 * C] += dw[:, :C]
    packed_ref[4 * C : 5 * C] += dw[:, C:]
    weight = jnp.concatenate([w_ref[0], w_ref[1]], axis=1).astype(BF16)
    for st in range(structs):
        at = samples + st
        cond = jnp.concatenate([first_ref[at], last_ref[at]], axis=0).astype(F32)
        at = samples + structs + st
        cond = cond + jnp.concatenate([first_ref[at], last_ref[at]], axis=0).astype(F32)
        normed, _ = layer_stats(cond)
        source = (normed * vec_ref[0:1]).astype(BF16)
        scale = tab_ref[0, st]
        pre_scale = (sums[0, st] * scale * (1.0 - scale)).astype(BF16)
        pre_shift = sums[1, st].astype(BF16)
        joined = jnp.concatenate([pre_scale, pre_shift], axis=1)
        grads = dot_tn(source, joined)
        packed_ref[:C] += grads[:, :C]
        packed_ref[C : 2 * C] += grads[:, C:]
        back = dot_nt(joined, weight) * normed
        packed_ref[vecs : vecs + 1] += rows_sum(back)
        packed_ref[vecs + 1 : vecs + 2] += rows_sum(pre_scale.astype(F32))


def rim_call(ids, below, above, first, last, gxb, tab, acc, weights, vectors, gw, dvec, dpair):
    samples = below.shape[0]
    structs = tab.shape[1]
    full = pl.BlockSpec(memory_space=pltpu.VMEM)
    shape = jax.ShapeDtypeStruct
    return pl.pallas_call(
        rim_kernel,
        in_specs=[pl.BlockSpec(memory_space=pltpu.SMEM)] + [full] * 12,
        out_specs=[full] * 2,
        out_shape=[
            shape((samples, 2 * HALO, C), BF16),
            shape((PACKED, C), F32),
        ],
        scratch_shapes=[
            pltpu.VMEM((2, structs, 2 * HALO, C), F32),
            pltpu.VMEM((C, 2 * C), F32),
        ],
        compiler_params=pltpu.CompilerParams(vmem_limit_bytes=VMEM_LIMIT),
        name="rims",
    )(ids, below, above, first, last, gxb, tab, acc, weights, vectors, gw, dvec, dpair)


def split_low(values):
    high = values.astype(BF16)
    return high, (values - high.astype(F32)).astype(BF16)


def update_kernel(
    total_ref,
    sl_ref,
    sr_ref,
    rl_ref,
    rr_ref,
    w_ref,
    ew_ref,
    vec_ref,
    sv_ref,
    ev_ref,
    pw_ref,
    sp_ref,
    ep_ref,
    rows_ref,
    tv_ref,
    tp_ref,
    left_ref,
    right_ref,
    neww_ref,
    low_ref,
    newv_ref,
    newp_ref,
    nsv_ref,
    nsp_ref,
    neww_ema_ref,
    newv_ema_ref,
    newp_ema_ref,
    turned,
):
    count = sl_ref.shape[1]
    own = pl.ds(lax.axis_index("win") * count, count)

    def product(parts, right):
        high, low = split_low(right)
        lefts = [split_low(part) for part in parts]
        tall = jnp.concatenate([a for a, _ in lefts] + [b for _, b in lefts], axis=0)
        size = tall.shape[0] // 2
        first = dot(tall, high)
        return first[:size] + first[size:] + dot(tall[:size], low)

    def one(b):
        block = total_ref[b * C : b * C + C]
        turned[b] = block.T
        pad = jnp.zeros((16 - count, C), F32) if count < 16 else None

        def rows(values):
            return values if pad is None else jnp.concatenate([values, pad], axis=0)

        own_rows = total_ref[pl.ds(b * C + lax.axis_index("win") * count, count)]
        rows_ref[b] = own_rows
        yield
        own_cols = turned[b, own]
        both = product([rows(own_cols), rows(rl_ref[b])], block)
        left = product([rows(own_rows)], turned[b])
        size = max(count, 16)
        yield
        step = product([both[size:]], rr_ref[b])
        right_ref[b] = stat_decay * sr_ref[b] + (1.0 - stat_decay) * both[:count]
        left_ref[b] = stat_decay * sl_ref[b] + (1.0 - stat_decay) * left[:count]
        yield
        new = w_ref[b, own] - matrix_rate * step[:count]
        neww_ref[b] = new
        low_ref[b] = new.astype(BF16)
        neww_ema_ref[b] = ema_decay * ew_ref[b] + (1.0 - ema_decay) * new

    for _ in pipeline([one(b) for b in range(NBLK)]):
        pass
    sums = total_ref[PW_AT : PW_AT + PAIR]
    pair_total = jnp.concatenate(
        [jnp.sum(sums[:, h * QW : h * QW + QW], axis=1, keepdims=True) for h in range(HEADS)], axis=1
    )
    for total, param, stat, ema, out, new_ref, stat_ref, ema_ref in (
        (total_ref[VEC_AT : VEC_AT + 7], vec_ref, sv_ref, ev_ref, tv_ref, newv_ref, nsv_ref, newv_ema_ref),
        (pair_total, pw_ref, sp_ref, ep_ref, tp_ref, newp_ref, nsp_ref, newp_ema_ref),
    ):
        out[...] = total
        new_stat = stat_decay * stat[...] + (1.0 - stat_decay) * total * total
        stat_ref[...] = new_stat
        new = param[...] - vector_rate * total * lax.rsqrt(new_stat)
        new_ref[...] = new
        ema_ref[...] = ema_decay * ema[...] + (1.0 - ema_decay) * new


def update_call(*args):
    rows = args[1].shape
    vec = args[7].shape
    pw = args[10].shape
    full = pl.BlockSpec(memory_space=pltpu.VMEM)

    def shape(dims, kind=F32):
        return jax.ShapeDtypeStruct(dims, kind)

    return pl.pallas_call(
        update_kernel,
        in_specs=[full] * len(args),
        out_specs=[full] * 14,
        out_shape=[
            shape(rows),
            shape(vec),
            shape(pw),
            shape(rows),
            shape(rows),
            shape(rows),
            shape(rows, BF16),
            shape(vec),
            shape(pw),
            shape(vec),
            shape(pw),
            shape(rows),
            shape(vec),
            shape(pw),
        ],
        scratch_shapes=[pltpu.VMEM((NBLK, C, C), F32)],
        compiler_params=pltpu.CompilerParams(vmem_limit_bytes=VMEM_LIMIT),
        name="update",
    )(*args)


def passed(shard, by):
    devices = lax.axis_size("win")
    pairs = [(i, i + by) for i in range(devices) if 0 <= i + by < devices]
    return lax.ppermute(shard, "win", pairs)


def rounded(values):
    return lax.reduce_precision(values, exponent_bits=8, mantissa_bits=7)


def partner(values, axis, bit):
    devices = lax.axis_size(axis)
    return lax.ppermute(values, axis, [(i, i ^ bit) for i in range(devices)])


def bits(axis):
    devices = lax.axis_size(axis)
    return [(axis, 1 << at) for at in range((devices - 1).bit_length())]


def summed(values):
    halvings = bits("samp")
    for at, (axis, bit) in enumerate(halvings):
        side = (lax.axis_index(axis) // bit) % 2
        half = values.shape[0] // 2
        send = lax.dynamic_slice_in_dim(values, (1 - side) * half, half)
        keep = lax.dynamic_slice_in_dim(values, side * half, half)
        wire = F32 if at == 0 else BF16
        values = keep + partner(send.astype(wire), axis, bit).astype(F32)
    for axis, bit in bits("win"):
        values = rounded(values)
        values = values + partner(values.astype(BF16), axis, bit).astype(F32)
    values = values.astype(BF16)
    for axis, bit in reversed(halvings):
        side = (lax.axis_index(axis) // bit) % 2
        other = partner(values, axis, bit)
        values = jnp.where(
            side == 0,
            jnp.concatenate([values, other]),
            jnp.concatenate([other, values]),
        )
    return values.astype(F32)


def body(
    atoms,
    cond,
    pair,
    struct_ids,
    cotangent,
    weights,
    vectors,
    pair_weight,
    stat_left,
    stat_right,
    root_left,
    root_right,
    stat_vectors,
    stat_pair,
    ema_weights,
    ema_vectors,
    ema_pair,
):
    rows = atoms.shape[1]
    messages = []
    for span in (slice(0, HALO), slice(rows - HALO, rows)):
        high = rounded(cond[:, span])
        rest = cond[:, span] - high
        parts = [atoms[:, span], high.astype(BF16), rest.astype(BF16)]
        messages.append(jnp.concatenate(parts, axis=0))
    first, last = messages
    low_msg, high_msg = passed(last, 1), passed(first, -1)
    bias, root = bias_table(pair, jnp.repeat(pair_weight, QW, axis=1))
    (result, grad_atoms, gxb, rim_low, rim_high, dbias, gw, dvec, accb, tabb) = main_call(
        struct_ids, atoms, low_msg, high_msg, cotangent, bias, cond, weights, vectors
    )
    above = passed(rim_low, -1)
    below = passed(rim_high, 1)
    dpair = pair_grad(pair, dbias, root)
    grad_rim, packed = rim_call(
        struct_ids, below, above, first, last, gxb, tabb, accb, weights, vectors, gw, dvec, dpair
    )
    grad_atoms = grad_atoms.at[:, :HALO].set(grad_rim[:, :HALO])
    grad_atoms = grad_atoms.at[:, rows - HALO :].set(grad_rim[:, HALO:])
    updated = update_call(
        summed(packed),
        stat_left,
        stat_right,
        root_left,
        root_right,
        weights,
        ema_weights,
        vectors,
        stat_vectors,
        ema_vectors,
        pair_weight,
        stat_pair,
        ema_pair,
    )
    return (result, grad_atoms, *updated)


def solution(mesh):
    placed = (
        P("samp", "win", None),
        P("samp", "win", None),
        P("samp", "win", None, None),
        P("samp"),
        P("samp", "win", None),
        P(),
        P(),
        P(),
        P(None, "win", None),
        P(None, "win", None),
        P(None, "win", None),
        P(),
        P(),
        P(),
        P(None, "win", None),
        P(),
        P(),
    )
    return jax.shard_map(
        body,
        mesh=mesh,
        in_specs=placed,
        out_specs=(
            P("samp", "win", None),
            P("samp", "win", None),
            P(None, "win", None),
            P(),
            P(),
            P(None, "win", None),
            P(None, "win", None),
            P(None, "win", None),
            P(None, "win", None),
            P(),
            P(),
            P(),
            P(),
            P(None, "win", None),
            P(),
            P(),
        ),
        check_vma=False,
    )
```

```python
import functools
import math

import jax
import jax.numpy as jnp
from jax import lax
from jax.experimental import pallas as pl
from jax.experimental.pallas import tpu as pltpu
from jax.sharding import PartitionSpec as P

HEADS = 4
FF = 256
QW = 32
HALO = 48
KW = 128
C = 128
PAIR = 16
NBLK = 17
UNROLL = 16
PACK = 2
SLOTS = 3
TILE = 512

stat_decay = 0.5
ema_decay = 0.8
matrix_rate = 1.0
vector_rate = 0.2

F32 = jnp.float32
BF16 = jnp.bfloat16
LOG2E = math.log2(math.e)
FACTOR = 1.0 / math.sqrt(C // HEADS)
INVALID = -1000000000.0
VMEM_LIMIT = 60 * 1024 * 1024


def dot(left, right):
    return lax.dot_general(left, right, (((1,), (0,)), ((), ())), preferred_element_type=F32)


def dot_nt(left, right):
    return lax.dot_general(left, right, (((1,), (1,)), ((), ())), preferred_element_type=F32)


def dot_tn(left, right):
    return lax.dot_general(left, right, (((0,), (0,)), ((), ())), preferred_element_type=F32)


def layer_stats(values):
    center = values - jnp.mean(values, axis=-1, keepdims=True)
    inverse = lax.rsqrt(jnp.mean(center * center, axis=-1, keepdims=True) + 1e-05)
    return (center * inverse, inverse)


def layer_back(normed, inverse, grad_norm):
    return inverse * (
        grad_norm
        - jnp.mean(grad_norm, axis=-1, keepdims=True)
        - normed * jnp.mean(grad_norm * normed, axis=-1, keepdims=True)
    )


def pipeline(stages):
    waiting = list(stages)
    active = []
    while waiting or active:
        if waiting:
            active.append(waiting.pop(0))
        active = [item for item in active if next(item, active) is None]
        yield


def together(streams):
    count = len(streams[0])
    for at in range(count + len(streams) - 1):
        pipes = []
        for behind, phases in enumerate(streams):
            if 0 <= at - behind < count:
                depth, stages = phases[at - behind]
                pipes.append([pipeline(stages), depth + len(stages), 0])
        longest = max(length for _, length, _ in pipes)
        for tick in range(1, longest + 1):
            for item in pipes:
                while item[2] * longest < tick * item[1]:
                    item[2] += 1
                    next(item[0], None)
        for pipe, _, _ in pipes:
            for _ in pipe:
                pass


def rows_sum(values):
    return jnp.sum(values, axis=0, keepdims=True)


def bias_kernel(pair_ref, pw_ref, bias_ref, root_ref, expand, flat):
    group = pl.program_id(1)
    per_step = bias_ref.shape[1]
    atoms = pl.num_programs(1) * per_step * QW
    span = QW * PAIR

    @pl.when((pl.program_id(0) == 0) & (group == 0))
    def _():
        rows = lax.broadcasted_iota(jnp.int32, (span, C), 0) // PAIR
        lanes = lax.broadcasted_iota(jnp.int32, (span, C), 1) % QW
        wide = lax.dot_general(
            pw_ref[...],
            head_lanes(),
            (((0,), (0,)), ((), ())),
            precision=lax.Precision.HIGHEST,
            preferred_element_type=F32,
        )
        weight = wide - jnp.mean(wide, axis=0, keepdims=True)
        full = jnp.where(rows == lanes, jnp.concatenate([weight] * QW, axis=0), 0.0)
        high = full.astype(BF16)
        expand[:, :C] = high
        expand[:, C:] = (full - high.astype(F32)).astype(BF16)

    def one(w):
        low = pair_ref[0, w * QW : w * QW + QW].reshape(span, KW)
        flat[w * span : w * span + span] = low.astype(F32)
        yield
        out = dot_tn(low, expand[...])
        roots = []
        for part in range(QW // 8):
            start = w * span + part * 8 * PAIR
            channels = [flat[pl.ds(start + c, 8, stride=PAIR), :] for c in range(PAIR)]
            mean = sum(channels[1:], channels[0]) * (1.0 / PAIR)
            center = [channel - mean for channel in channels]
            squares = [value * value for value in center]
            spread = sum(squares[1:], squares[0]) * (1.0 / PAIR)
            roots.append(lax.rsqrt(spread + 1e-05))
        yield
        root = jnp.concatenate(roots * HEADS, axis=0).T
        value = (out[:, :C] + out[:, C:]) * (root * LOG2E)
        start = lax.axis_index("win") * atoms + (group * per_step + w) * QW - HALO
        position = start + lax.broadcasted_iota(jnp.int32, (KW, C), 0)
        valid = (position >= 0) & (position < lax.axis_size("win") * atoms)
        bias_ref[0, w] = jnp.where(valid, value, INVALID * LOG2E)
        root_ref[0, w] = root.astype(BF16)

    for _ in pipeline([one(w) for w in range(per_step)]):
        pass


def head_lanes():
    rows = lax.broadcasted_iota(jnp.int32, (HEADS, C), 0)
    lanes = lax.broadcasted_iota(jnp.int32, (HEADS, C), 1) // QW
    return jnp.where(rows == lanes, 1.0, 0.0)


def bias_table(pair, turned_weight):
    structs, atoms = pair.shape[:2]
    count = min(8, atoms // QW)
    rows = count * QW
    table = pl.BlockSpec((1, count, KW, C), lambda s, i: (s, i, 0, 0))
    return pl.pallas_call(
        bias_kernel,
        grid=(structs, atoms // rows),
        in_specs=[
            pl.BlockSpec((1, rows, PAIR, KW), lambda s, i: (s, i, 0, 0)),
            pl.BlockSpec((HEADS, PAIR), lambda s, i: (0, 0)),
        ],
        out_specs=[table, table],
        scratch_shapes=[
            pltpu.VMEM((QW * PAIR, 2 * C), BF16),
            pltpu.VMEM((rows * PAIR, KW), F32),
        ],
        out_shape=[
            jax.ShapeDtypeStruct((structs, atoms // QW, KW, C), F32),
            jax.ShapeDtypeStruct((structs, atoms // QW, KW, C), BF16),
        ],
        compiler_params=pltpu.CompilerParams(vmem_limit_bytes=VMEM_LIMIT),
        cost_estimate=pl.CostEstimate(flops=10**9, bytes_accessed=15 * 2**20, transcendentals=0),
        name="pair_bias",
    )(pair, turned_weight)


def main_kernel(
    ids_ref,
    x_ref,
    xlo_ref,
    xhi_ref,
    g_ref,
    bias_ref,
    root_ref,
    pair_ref,
    cond_ref,
    clo_ref,
    chi_ref,
    w_ref,
    vec_ref,
    out_ref,
    grad_ref,
    rlo_ref,
    rhi_ref,
    packed_ref,
    small_ref,
    dbias_ref,
    dvec_ref,
    pair_scr,
    pair_sem,
    pair_total,
    wq,
    w6,
    win,
    wo,
    wqt,
    w6t,
    wint,
    wot,
    wc1,
    wc2,
    mask,
    t_s1,
    t_h1,
    t_hs,
    t_hh,
    t_g1,
    t_s2,
    t_h2,
    t_g2,
    a_s1,
    a_h1,
    a_g1,
    a_s2,
    a_h2,
    a_g2,
    a_hs,
    a_hh,
    nh_scr,
    ih_scr,
    ah_scr,
    k_scr,
    v_scr,
    q_scr,
    gate_scr,
    ada_scr,
    n1_scr,
    inv_scr,
    o_scr,
    p_scr,
    do_scr,
    dd_scr,
    d4_scr,
    dk_scr,
    dv_scr,
    dx_scr,
):
    step = pl.program_id(0)
    structs, atoms, _ = cond_ref.shape
    windows = atoms // QW
    unroll = min(UNROLL, windows)
    tile = min(TILE, atoms)
    tiles = atoms // tile
    s = [lax.rem(ids_ref[step * PACK + b], structs) for b in range(PACK)]

    def cond_rows(source):
        normed, _ = layer_stats(source)
        one = (normed * vec_ref[0:1]).astype(BF16)
        two = (normed * vec_ref[4:5]).astype(BF16)
        return normed, one, two

    def block(at):
        return packed_ref.at[at * C : at * C + C]

    def joined(ref, st):
        return ref[st].astype(F32) + ref[structs + st].astype(F32)

    chunk = min(8, windows)
    chunks = structs * windows // chunk

    def pair_copy(at):
        st, first = divmod(at * chunk, windows)
        return pltpu.make_async_copy(
            pair_ref.at[st, pl.ds(first * QW, chunk * QW)],
            pair_scr.at[at % SLOTS],
            pair_sem.at[at % SLOTS],
        )

    @pl.when(step == 0)
    def _():
        for at in range(min(SLOTS, chunks)):
            pair_copy(at).start()

        def low(b):
            return w_ref[b].astype(BF16)

        for at, b in enumerate((2, 5, 3, 4)):
            wq[:, at * C : at * C + C] = low(b)
        w6[...] = low(6)
        for at in range(4):
            win[:, at * C : at * C + C] = low(11 + at)
        for at in range(2):
            wo[at * C : at * C + C, :] = low(15 + at)
        for source, turned in ((wq, wqt), (w6, w6t), (win, wint), (wo, wot)):
            turned[...] = source[...].T
        for at, b in enumerate((0, 1, 7)):
            wc1[:, at * C : at * C + C] = low(b)
        for at, b in enumerate((8, 9, 10)):
            wc2[:, at * C : at * C + C] = low(b)
        rows_head = lax.broadcasted_iota(jnp.int32, (C, C), 0) // QW
        lane_head = lax.broadcasted_iota(jnp.int32, (C, C), 1) // (C // HEADS)
        mask[...] = jnp.where(rows_head == lane_head, 1.0, 0.0).astype(BF16)
        for acc in (a_s1, a_h1, a_g1, a_s2, a_h2, a_g2, a_hs, a_hh, packed_ref, dvec_ref):
            acc[...] = jnp.zeros_like(acc)
        dbias_ref[...] = jnp.zeros_like(dbias_ref)
        pair_total[...] = jnp.zeros_like(pair_total)
        for st in range(structs):

            def table(i, carry):
                rows = pl.ds(pl.multiple_of(i * tile, tile), tile)
                _, one, two = cond_rows(cond_ref[st, rows])
                first = dot(one, wc1[...])
                t_s1[st, rows] = jax.nn.sigmoid(first[:, :C] + vec_ref[1:2])
                t_h1[st, rows] = first[:, C : 2 * C]
                t_g1[st, rows] = jax.nn.sigmoid(first[:, 2 * C :] + vec_ref[3:4])
                second = dot(two, wc2[...])
                t_s2[st, rows] = jax.nn.sigmoid(second[:, :C] + vec_ref[5:6])
                t_h2[st, rows] = second[:, C : 2 * C]
                t_g2[st, rows] = jax.nn.sigmoid(second[:, 2 * C :] + vec_ref[6:7])
                return carry

            lax.fori_loop(0, tiles, table, 0)
            _, one, _ = cond_rows(jnp.concatenate([joined(clo_ref, st), joined(chi_ref, st)], axis=0))
            first = dot(one, wc1[:, : 2 * C])
            t_hs[st] = jax.nn.sigmoid(first[:, :C] + vec_ref[1:2])
            t_hh[st] = first[:, C:]

    def project(b, i):
        start = i * tile
        rows = pl.ds(start, tile)
        pad = pl.ds(start + HALO, tile)
        normed, inverse = layer_stats(x_ref[b, rows].astype(F32))
        n1_scr[b, rows] = normed
        inv_scr[b, rows] = jnp.broadcast_to(inverse, (tile, C))
        ada = (t_s1[s[b], rows] * normed + t_h1[s[b], rows]).astype(BF16)
        ada_scr[b, rows] = ada
        yield
        out = dot(ada, wq[...])
        yield
        q_scr[b, rows] = (out[:, :C] + vec_ref[2:3]).astype(BF16)
        gate_scr[b, rows] = jax.nn.sigmoid(out[:, C : 2 * C])
        k_scr[b, pad] = out[:, 2 * C : 3 * C].astype(BF16)
        v_scr[b, pad] = out[:, 3 * C :].astype(BF16)

    def project_halo(b):
        halo = jnp.concatenate([xlo_ref[b], xhi_ref[b]], axis=0).astype(F32)
        normed, inverse = layer_stats(halo)
        ada = (t_hs[s[b]] * normed + t_hh[s[b]]).astype(BF16)
        nh_scr[b] = normed
        ih_scr[b] = jnp.broadcast_to(inverse, (2 * HALO, C))
        ah_scr[b] = ada
        yield
        out = dot(ada, wq[:, 2 * C :])
        yield
        k_scr[b, :HALO] = out[:HALO, :C].astype(BF16)
        v_scr[b, :HALO] = out[:HALO, C:].astype(BF16)
        k_scr[b, HALO + atoms :] = out[HALO:, :C].astype(BF16)
        v_scr[b, HALO + atoms :] = out[HALO:, C:].astype(BF16)

    lane_head = lax.broadcasted_iota(jnp.int32, (QW, C), 1) // (C // HEADS)

    def spread(rows):
        return jnp.concatenate([rows] * HEADS, axis=0) * mask[...]

    def gathered(full):
        parts = [full[h * QW : h * QW + QW] for h in range(HEADS)]
        last = parts[HEADS - 1]
        for h in range(HEADS - 2, -1, -1):
            last = jnp.where(lane_head == h, parts[h], last)
        return last

    def attend(b, group):
        scores = []
        for w in group:
            queries = spread(q_scr[b, w * QW : w * QW + QW])
            scores.append(dot(k_scr[b, w * QW : w * QW + KW], queries.T))
        yield
        probs = []
        for u, w in enumerate(group):
            value = scores[u] * (FACTOR * LOG2E) + bias_ref[s[b], w]
            exps = jnp.exp2(value - jnp.max(value, axis=0, keepdims=True))
            prob = (exps * (1.0 / rows_sum(exps))).astype(BF16)
            p_scr[b, w] = prob
            probs.append(prob)
        yield
        fulls = [dot_tn(probs[u], v_scr[b, w * QW : w * QW + KW]) for u, w in enumerate(group)]
        yield
        for u, w in enumerate(group):
            o_scr[b, w * QW : w * QW + QW] = gathered(fulls[u])

    def middle(b, i):
        rows = pl.ds(i * tile, tile)
        gate = gate_scr[b, rows]
        mixed = o_scr[b, rows]
        y = (gate * mixed).astype(BF16)
        yield
        attn = dot(y, w6[...])
        yield
        gate_one = t_g1[s[b], rows]
        x1 = x_ref[b, rows].astype(F32) + gate_one * attn
        normed, inverse = layer_stats(x1)
        scale_two = t_s2[s[b], rows]
        ada = (scale_two * normed + t_h2[s[b], rows]).astype(BF16)
        yield
        expand = dot(ada, win[...])
        yield
        a = expand[:, :FF]
        up = expand[:, FF:]
        sig = jax.nn.sigmoid(a)
        silu = a * sig
        hid = (silu * up).astype(BF16)
        yield
        ff = dot(hid, wo[...])
        gate_two = t_g2[s[b], rows]
        g = g_ref[b, rows].astype(F32)
        dff = (g * gate_two).astype(BF16)
        dhid = dot(dff, wot[...])
        yield
        out_ref[b, rows] = (x1 + gate_two * ff).astype(BF16)
        a_g2[s[b], rows] += g * ff
        da = (dhid * up * (sig + silu * (1.0 - sig))).astype(BF16)
        db = (dhid * silu).astype(BF16)
        dab = jnp.concatenate([da, db], axis=1)
        yield
        dada = dot(dab, wint[...])
        yield
        a_s2[s[b], rows] += dada * normed
        a_h2[s[b], rows] += dada
        dx1 = g + layer_back(normed, inverse, dada * scale_two)
        dx_scr[b, rows] = dx1
        a_g1[s[b], rows] += dx1 * attn
        dattn = (dx1 * gate_one).astype(BF16)
        yield
        dy = dot(dattn, w6t[...])
        dwo = dot_tn(dff, hid)
        dwin = dot_tn(ada, dab)
        dw6 = dot_tn(y, dattn)
        yield
        do = (dy * gate).astype(BF16)
        do_scr[b, rows] = do
        dd_scr[b, rows] = (do.astype(F32) * mixed * -1.0).astype(BF16)
        d4_scr[b, rows, C : 2 * C] = (dy * mixed * gate * (1.0 - gate)).astype(BF16)
        block(15)[...] += dwo[:, :C]
        block(16)[...] += dwo[:, C:]
        for at in range(4):
            block(11 + at)[...] += dwin[:, at * C : at * C + C]
        block(6)[...] += dw6

    dk_scr[...] = jnp.zeros_like(dk_scr)
    dv_scr[...] = jnp.zeros_like(dv_scr)
    ones = jnp.ones((KW, C), BF16)

    def attend_back(b, group):
        diffs = []
        spreads = []
        for w in group:
            dox = spread(do_scr[b, w * QW : w * QW + QW])
            ddx = spread(dd_scr[b, w * QW : w * QW + QW])
            values = jnp.concatenate([v_scr[b, w * QW : w * QW + KW], ones], axis=1)
            diffs.append(dot(values, jnp.concatenate([dox.T, ddx.T], axis=0)))
            spreads.append(dox)
        yield
        grads = []
        for u, w in enumerate(group):
            ds = p_scr[b, w].astype(F32) * diffs[u]
            dbias_ref[s[b], w] += ds
            grads.append(ds.astype(BF16))
        yield
        fulls = []
        dks = []
        dvs = []
        for u, w in enumerate(group):
            fulls.append(dot_tn(grads[u], k_scr[b, w * QW : w * QW + KW]))
            dks.append(dot(grads[u], spread(q_scr[b, w * QW : w * QW + QW])))
            dvs.append(dot(p_scr[b, w], spreads[u]))
        yield
        for u, w in enumerate(group):
            dq = gathered(fulls[u]) * FACTOR
            dvec_ref[2] += jnp.sum(dq.reshape(QW // 8, 8, C), axis=0)
            d4_scr[b, w * QW : w * QW + QW, :C] = dq.astype(BF16)
            dk_scr[b, w * QW : w * QW + KW] += dks[u]
            dv_scr[b, w * QW : w * QW + KW] += dvs[u]

    def finish(b, i):
        start = i * tile
        rows = pl.ds(start, tile)
        pad = pl.ds(start + HALO, tile)
        d4_scr[b, rows, 2 * C : 3 * C] = (dk_scr[b, pad] * FACTOR).astype(BF16)
        d4_scr[b, rows, 3 * C :] = dv_scr[b, pad].astype(BF16)
        yield
        d4 = d4_scr[b, rows]
        dwq = dot_tn(ada_scr[b, rows], d4)
        dada = dot(d4, wqt[...])
        yield
        for at, which in enumerate((2, 5, 3, 4)):
            block(which)[...] += dwq[:, at * C : at * C + C]
        normed = n1_scr[b, rows]
        a_s1[s[b], rows] += dada * normed
        a_h1[s[b], rows] += dada
        grad = dx_scr[b, rows] + layer_back(normed, inv_scr[b, rows], dada * t_s1[s[b], rows])
        dx_scr[b, rows] = grad
        grad_ref[b, rows] = grad.astype(BF16)

    def finish_halo(b):
        spans = (slice(0, HALO), slice(HALO + atoms, None))
        dk = jnp.concatenate([dk_scr[b, span] for span in spans], axis=0) * FACTOR
        dv = jnp.concatenate([dv_scr[b, span] for span in spans], axis=0)
        dkv = jnp.concatenate([dk.astype(BF16), dv.astype(BF16)], axis=1)
        yield
        dw = dot_tn(ah_scr[b], dkv)
        dada = dot(dkv, wqt[2 * C :])
        yield
        block(3)[...] += dw[:, :C]
        block(4)[...] += dw[:, C:]
        normed = nh_scr[b]
        a_hs[s[b]] += dada * normed
        a_hh[s[b]] += dada
        rim = layer_back(normed, ih_scr[b], dada * t_hs[s[b]]).astype(BF16)
        rlo_ref[b] = rim[:HALO]
        rhi_ref[b] = rim[HALO:]

    groups = [tuple(range(at, at + unroll)) for at in range(0, windows, unroll)]

    def phases(b):
        return [
            (3, [project_halo(b)] + [project(b, i) for i in range(tiles)]),
            (4, [attend(b, group) for group in groups]),
            (11, [middle(b, i) for i in range(tiles)]),
            (4, [attend_back(b, group) for group in groups]),
            (3, [finish_halo(b)] + [finish(b, i) for i in range(tiles)]),
        ]

    together([phases(b) for b in range(PACK)])

    @pl.when(step == pl.num_programs(0) - 1)
    def _():
        for at in (15, 16):
            block(at)[...] = block(at)[...].T

        def apply(source, normed, parts, weight, blocks, gain):
            joined_parts = jnp.concatenate(parts, axis=1)
            grads = dot_tn(source, joined_parts)
            back = dot_nt(joined_parts, weight) * normed
            for at, which in enumerate(blocks):
                block(which)[...] += grads[:, at * C : at * C + C]
            dvec_ref[gain] += jnp.sum(back.reshape(-1, 8, C), axis=0)

        def bias_sum(at, part):
            dvec_ref[at] += jnp.sum(part.astype(F32).reshape(-1, 8, C), axis=0)

        def pre(total, gate):
            return (total * gate * (1.0 - gate)).astype(BF16)

        def conditioning(st, i):
            rows = pl.ds(i * tile, tile)
            normed, one, two = cond_rows(cond_ref[st, rows])
            first = [
                pre(a_s1[st, rows], t_s1[st, rows]),
                a_h1[st, rows].astype(BF16),
                pre(a_g1[st, rows], t_g1[st, rows]),
            ]
            second = [
                pre(a_s2[st, rows], t_s2[st, rows]),
                a_h2[st, rows].astype(BF16),
                pre(a_g2[st, rows], t_g2[st, rows]),
            ]
            yield
            for at, part in ((1, first[0]), (3, first[2]), (5, second[0]), (6, second[2])):
                bias_sum(at, part)
            apply(one, normed, first, wc1[...], (0, 1, 7), 0)
            apply(two, normed, second, wc2[...], (8, 9, 10), 4)

        def conditioning_halo(st):
            source = jnp.concatenate([joined(clo_ref, st), joined(chi_ref, st)], axis=0)
            normed, one, _ = cond_rows(source)
            parts = [pre(a_hs[st], t_hs[st]), a_hh[st].astype(BF16)]
            yield
            bias_sum(1, parts[0])
            apply(one, normed, parts, wc1[:, : 2 * C], (0, 1), 0)

        items = [conditioning_halo(st) for st in range(structs)]
        items += [conditioning(st, i) for st in range(structs) for i in range(tiles)]
        for _ in pipeline(items):
            pass

        for at in range(chunks):
            pair_copy(at).wait()
            st, first = divmod(at * chunk, windows)
            lefts = []
            rights = []
            for w in range(chunk):
                lefts.append(
                    pair_scr[at % SLOTS, w * QW : w * QW + QW].reshape(QW * PAIR, KW)
                )
                grad = dbias_ref[st, first + w] * root_ref[st, first + w].astype(F32)
                rights.append(grad.astype(BF16))
            left = jnp.concatenate(lefts, axis=1)
            pair_total[...] += dot(left, jnp.concatenate(rights, axis=0))
            if at + SLOTS < chunks:
                pair_copy(at + SLOTS).start()
        lanes = lax.broadcasted_iota(jnp.int32, (PAIR, C), 1) % QW
        acc = jnp.zeros((PAIR, C), F32)
        for q in range(QW):
            acc = acc + jnp.where(lanes == q, pair_total[q * PAIR : q * PAIR + PAIR], 0.0)
        small_ref[8:] = acc - jnp.mean(acc, axis=0, keepdims=True)
        small_ref[:8] = jnp.concatenate(
            [rows_sum(dvec_ref[at]) for at in range(7)] + [jnp.zeros((1, C), F32)], axis=0
        )


def main_call(
    ids, atoms, low_msg, high_msg, cotangent, bias, root, pair, cond, weights, vectors
):
    samples, rows, _ = atoms.shape
    structs = cond.shape[0]
    windows = rows // QW
    padded = rows + 2 * HALO

    def per_sample(*shape):
        zeros = (0,) * len(shape)
        return pl.BlockSpec((PACK,) + shape, lambda i, _: (i,) + zeros)

    def whole(*shape):
        zeros = (0,) * len(shape)
        return pl.BlockSpec(shape, lambda i, _: zeros, pipeline_mode=pl.Buffered(1))

    def table(count=rows):
        return pltpu.VMEM((structs, count, C), F32)

    cond_part = pl.BlockSpec((2 * structs, HALO, C), lambda i, _: (samples // (2 * structs), 0, 0))
    shape = jax.ShapeDtypeStruct
    return pl.pallas_call(
        main_kernel,
        grid_spec=pltpu.PrefetchScalarGridSpec(
            num_scalar_prefetch=1,
            grid=(samples // PACK,),
            in_specs=[
                per_sample(rows, C),
                per_sample(HALO, C),
                per_sample(HALO, C),
                per_sample(rows, C),
                whole(structs, windows, KW, C),
                whole(structs, windows, KW, C),
                pl.BlockSpec(memory_space=pl.ANY),
                whole(structs, rows, C),
                cond_part,
                cond_part,
                whole(NBLK, C, C),
                whole(7, C),
            ],
            out_specs=[
                per_sample(rows, C),
                per_sample(rows, C),
                per_sample(HALO, C),
                per_sample(HALO, C),
                whole(NBLK * C, C),
                whole(8 + PAIR, C),
            ],
            scratch_shapes=[
                pltpu.VMEM((structs, windows, KW, C), F32),
                pltpu.VMEM((7, 8, C), F32),
                pltpu.VMEM((SLOTS, min(rows, 8 * QW), PAIR, KW), BF16),
                pltpu.SemaphoreType.DMA((SLOTS,)),
                pltpu.VMEM((QW * PAIR, C), F32),
                pltpu.VMEM((C, 4 * C), BF16),
                pltpu.VMEM((C, C), BF16),
                pltpu.VMEM((C, 2 * FF), BF16),
                pltpu.VMEM((FF, C), BF16),
                pltpu.VMEM((4 * C, C), BF16),
                pltpu.VMEM((C, C), BF16),
                pltpu.VMEM((2 * FF, C), BF16),
                pltpu.VMEM((C, FF), BF16),
                pltpu.VMEM((C, 3 * C), BF16),
                pltpu.VMEM((C, 3 * C), BF16),
                pltpu.VMEM((C, C), BF16),
                table(),
                table(),
                table(2 * HALO),
                table(2 * HALO),
                table(),
                table(),
                table(),
                table(),
                table(),
                table(),
                table(),
                table(),
                table(),
                table(),
                table(2 * HALO),
                table(2 * HALO),
                pltpu.VMEM((PACK, 2 * HALO, C), F32),
                pltpu.VMEM((PACK, 2 * HALO, C), F32),
                pltpu.VMEM((PACK, 2 * HALO, C), BF16),
                pltpu.VMEM((PACK, padded, C), BF16),
                pltpu.VMEM((PACK, padded, C), BF16),
                pltpu.VMEM((PACK, rows, C), BF16),
                pltpu.VMEM((PACK, rows, C), F32),
                pltpu.VMEM((PACK, rows, C), BF16),
                pltpu.VMEM((PACK, rows, C), F32),
                pltpu.VMEM((PACK, rows, C), F32),
                pltpu.VMEM((PACK, rows, C), F32),
                pltpu.VMEM((PACK, windows, KW, C), BF16),
                pltpu.VMEM((PACK, rows, C), BF16),
                pltpu.VMEM((PACK, rows, C), BF16),
                pltpu.VMEM((PACK, rows, 4 * C), BF16),
                pltpu.VMEM((PACK, padded, C), F32),
                pltpu.VMEM((PACK, padded, C), F32),
                pltpu.VMEM((PACK, rows, C), F32),
            ],
        ),
        out_shape=[
            shape((samples, rows, C), BF16),
            shape((samples, rows, C), BF16),
            shape((samples, HALO, C), BF16),
            shape((samples, HALO, C), BF16),
            shape((NBLK * C, C), F32),
            shape((8 + PAIR, C), F32),
        ],
        compiler_params=pltpu.CompilerParams(vmem_limit_bytes=VMEM_LIMIT),
        name="block",
    )(
        ids,
        atoms,
        low_msg,
        high_msg,
        cotangent,
        bias,
        root,
        pair,
        cond,
        low_msg,
        high_msg,
        weights,
        vectors,
    )


def split_low(values):
    high = values.astype(BF16)
    return high, (values - high.astype(F32)).astype(BF16)


def update_kernel(
    total_ref,
    small_ref,
    sl_ref,
    sr_ref,
    rl_ref,
    rr_ref,
    w_ref,
    ew_ref,
    vec_ref,
    sv_ref,
    ev_ref,
    pw_ref,
    sp_ref,
    ep_ref,
    rows_ref,
    tv_ref,
    tp_ref,
    left_ref,
    right_ref,
    neww_ref,
    low_ref,
    newv_ref,
    newp_ref,
    nsv_ref,
    nsp_ref,
    neww_ema_ref,
    newv_ema_ref,
    newp_ema_ref,
    turned,
):
    count = sl_ref.shape[1]
    own = pl.ds(lax.axis_index("win") * count, count)

    def product(parts, right):
        high, low = split_low(right)
        lefts = [split_low(part) for part in parts]
        tall = jnp.concatenate([a for a, _ in lefts] + [b for _, b in lefts], axis=0)
        size = tall.shape[0] // 2
        first = dot(tall, high)
        return first[:size] + first[size:] + dot(tall[:size], low)

    def one(b):
        block = total_ref[b * C : b * C + C]
        turned[b] = block.T
        pad = jnp.zeros((16 - count, C), F32) if count < 16 else None

        def rows(values):
            return values if pad is None else jnp.concatenate([values, pad], axis=0)

        own_rows = total_ref[pl.ds(b * C + lax.axis_index("win") * count, count)]
        rows_ref[b] = own_rows
        yield
        own_cols = turned[b, own]
        both = product([rows(own_cols), rows(rl_ref[b])], block)
        left = product([rows(own_rows)], turned[b])
        size = max(count, 16)
        yield
        step = product([both[size:]], rr_ref[b])
        right_ref[b] = stat_decay * sr_ref[b] + (1.0 - stat_decay) * both[:count]
        left_ref[b] = stat_decay * sl_ref[b] + (1.0 - stat_decay) * left[:count]
        yield
        new = w_ref[b, own] - matrix_rate * step[:count]
        neww_ref[b] = new
        low_ref[b] = new.astype(BF16)
        neww_ema_ref[b] = ema_decay * ew_ref[b] + (1.0 - ema_decay) * new

    for _ in pipeline([one(b) for b in range(NBLK)]):
        pass
    sums = small_ref[8:]
    pair_total = lax.dot_general(
        head_lanes(),
        sums,
        (((1,), (1,)), ((), ())),
        precision=lax.Precision.HIGHEST,
        preferred_element_type=F32,
    )
    for total, param, stat, ema, out, new_ref, stat_ref, ema_ref in (
        (small_ref[:7], vec_ref, sv_ref, ev_ref, tv_ref, newv_ref, nsv_ref, newv_ema_ref),
        (pair_total, pw_ref, sp_ref, ep_ref, tp_ref, newp_ref, nsp_ref, newp_ema_ref),
    ):
        out[...] = total
        new_stat = stat_decay * stat[...] + (1.0 - stat_decay) * total * total
        stat_ref[...] = new_stat
        new = param[...] - vector_rate * total * lax.rsqrt(new_stat)
        new_ref[...] = new
        ema_ref[...] = ema_decay * ema[...] + (1.0 - ema_decay) * new


def update_call(*args):
    rows = args[2].shape
    vec = args[8].shape
    pw = args[11].shape
    full = pl.BlockSpec(memory_space=pltpu.VMEM)

    def shape(dims, kind=F32):
        return jax.ShapeDtypeStruct(dims, kind)

    def out_block(dims):
        zeros = (0,) * len(dims)
        return pl.BlockSpec(dims, lambda i: zeros)

    outs = [rows, vec, pw, rows, rows, rows, rows, vec, pw, vec, pw, rows, vec, pw]
    return pl.pallas_call(
        update_kernel,
        grid=(1,),
        in_specs=[full] * len(args),
        out_specs=[out_block(dims) for dims in outs],
        out_shape=[
            shape(dims, BF16 if at == 6 else F32) for at, dims in enumerate(outs)
        ],
        scratch_shapes=[pltpu.VMEM((NBLK, C, C), F32)],
        compiler_params=pltpu.CompilerParams(vmem_limit_bytes=VMEM_LIMIT),
        name="update",
    )(*args)


def passed(shard, by):
    devices = lax.axis_size("win")
    pairs = [(i, i + by) for i in range(devices) if 0 <= i + by < devices]
    return lax.ppermute(shard, "win", pairs)


def rounded(values):
    return lax.reduce_precision(values, exponent_bits=8, mantissa_bits=7)


def partner(values, axis, bit):
    devices = lax.axis_size(axis)
    return lax.ppermute(values, axis, [(i, i ^ bit) for i in range(devices)])


def bits(axis):
    devices = lax.axis_size(axis)
    return [(axis, 1 << at) for at in range((devices - 1).bit_length())]


def summed(values, small, after):
    halvings = bits("samp")
    count = small.shape[0]

    def exchange(part, axis, bit):
        high = rounded(small)
        rest = rounded(small - high)
        message = [part.astype(BF16), high.astype(BF16), rest.astype(BF16)]
        got = partner(jnp.concatenate(message, axis=0), axis, bit).astype(F32)
        size = part.shape[0]
        total = (high + rest) + (got[size : size + count] + got[size + count :])
        return got[:size], total

    for at, (axis, bit) in enumerate(halvings):
        side = (lax.axis_index(axis) // bit) % 2
        half = values.shape[0] // 2
        send = lax.dynamic_slice_in_dim(values, (1 - side) * half, half)
        keep = lax.dynamic_slice_in_dim(values, side * half, half)
        if at == 0:
            got = partner(jnp.concatenate([send, small], axis=0), axis, bit)
            small = small + got[half:]
            values = keep + got[:half]
        else:
            got, small = exchange(send, axis, bit)
            values = keep + got
    for at, (axis, bit) in enumerate(bits("win")):
        values = rounded(values)
        got, small = exchange(values, axis, bit)
        values = values + got
        if at == 1:
            values, after = lax.optimization_barrier((values, after))
    values = values.astype(BF16)
    for at, (axis, bit) in enumerate(reversed(halvings)):
        side = (lax.axis_index(axis) // bit) % 2
        other = partner(values, axis, bit)
        values = jnp.where(
            side == 0,
            jnp.concatenate([values, other]),
            jnp.concatenate([other, values]),
        )
    return values.astype(F32), small, after


def body(
    atoms,
    cond,
    pair,
    struct_ids,
    cotangent,
    weights,
    vectors,
    pair_weight,
    stat_left,
    stat_right,
    root_left,
    root_right,
    stat_vectors,
    stat_pair,
    ema_weights,
    ema_vectors,
    ema_pair,
):
    rows = atoms.shape[1]
    messages = []
    for span in (slice(0, HALO), slice(rows - HALO, rows)):
        high = rounded(cond[:, span])
        rest = cond[:, span] - high
        parts = [atoms[:, span], high.astype(BF16), rest.astype(BF16)]
        messages.append(jnp.concatenate(parts, axis=0))
    first, last = messages
    low_msg, high_msg = passed(last, 1), passed(first, -1)
    bias, root = bias_table(pair, pair_weight.T)
    result, grad_atoms, rim_low, rim_high, packed, small = main_call(
        struct_ids, atoms, low_msg, high_msg, cotangent, bias, root, pair, cond, weights, vectors
    )
    above = passed(rim_low, -1)
    below = passed(rim_high, 1)
    packed, small, (below, above) = summed(packed, small, (below, above))
    for span, part in ((slice(0, HALO), below), (slice(rows - HALO, rows), above)):
        edge = grad_atoms[:, span].astype(F32) + part.astype(F32)
        grad_atoms = grad_atoms.at[:, span].set(edge.astype(BF16))
    outs = list(
        update_call(
            packed,
            small,
            stat_left,
            stat_right,
            root_left,
            root_right,
            weights,
            ema_weights,
            vectors,
            stat_vectors,
            ema_vectors,
            pair_weight.T,
            stat_pair.T,
            ema_pair.T,
        )
    )
    for at in (2, 8, 10, 13):
        outs[at] = outs[at].T
    return (result, grad_atoms, *outs)


def solution(mesh):
    placed = (
        P("samp", "win", None),
        P("samp", "win", None),
        P("samp", "win", None, None),
        P("samp"),
        P("samp", "win", None),
        P(),
        P(),
        P(),
        P(None, "win", None),
        P(None, "win", None),
        P(None, "win", None),
        P(),
        P(),
        P(),
        P(None, "win", None),
        P(),
        P(),
    )
    return jax.shard_map(
        body,
        mesh=mesh,
        in_specs=placed,
        out_specs=(
            P("samp", "win", None),
            P("samp", "win", None),
            P(None, "win", None),
            P(),
            P(),
            P(None, "win", None),
            P(None, "win", None),
            P(None, "win", None),
            P(None, "win", None),
            P(),
            P(),
            P(),
            P(),
            P(None, "win", None),
            P(),
            P(),
        ),
        check_vma=False,
    )
```

```python
import functools
import math

import jax
import jax.numpy as jnp
from jax import lax
from jax.experimental import pallas as pl
from jax.experimental.pallas import tpu as pltpu
from jax.sharding import PartitionSpec as P

HEADS = 4
FF = 256
QW = 32
HALO = 48
KW = 128
C = 128
PAIR = 16
NBLK = 17
UNROLL = 16
PACK = 2
SLOTS = 3
TILE = 512

stat_decay = 0.5
ema_decay = 0.8
matrix_rate = 1.0
vector_rate = 0.2

F32 = jnp.float32
BF16 = jnp.bfloat16
LOG2E = math.log2(math.e)
FACTOR = 1.0 / math.sqrt(C // HEADS)
INVALID = -1000000000.0
VMEM_LIMIT = 60 * 1024 * 1024


def dot(left, right):
    return lax.dot_general(left, right, (((1,), (0,)), ((), ())), preferred_element_type=F32)


def dot_nt(left, right):
    return lax.dot_general(left, right, (((1,), (1,)), ((), ())), preferred_element_type=F32)


def dot_tn(left, right):
    return lax.dot_general(left, right, (((0,), (0,)), ((), ())), preferred_element_type=F32)


def layer_stats(values):
    center = values - jnp.mean(values, axis=-1, keepdims=True)
    inverse = lax.rsqrt(jnp.mean(center * center, axis=-1, keepdims=True) + 1e-05)
    return (center * inverse, inverse)


def layer_back(normed, inverse, grad_norm):
    return inverse * (
        grad_norm
        - jnp.mean(grad_norm, axis=-1, keepdims=True)
        - normed * jnp.mean(grad_norm * normed, axis=-1, keepdims=True)
    )


def pipeline(stages):
    waiting = list(stages)
    active = []
    while waiting or active:
        if waiting:
            active.append(waiting.pop(0))
        active = [item for item in active if next(item, active) is None]
        yield


def beside(items):
    active = list(items)
    while active:
        active = [item for item in active if next(item, active) is None]
        yield


def together(streams):
    count = len(streams[0])
    for at in range(count + len(streams) - 1):
        pipes = []
        for behind, phases in enumerate(streams):
            if 0 <= at - behind < count:
                depth, stages = phases[at - behind]
                pipes.append([pipeline(stages), depth + len(stages), 0])
        longest = max(length for _, length, _ in pipes)
        for tick in range(1, longest + 1):
            for item in pipes:
                while item[2] * longest < tick * item[1]:
                    item[2] += 1
                    next(item[0], None)
        for pipe, _, _ in pipes:
            for _ in pipe:
                pass


def rows_sum(values):
    return jnp.sum(values, axis=0, keepdims=True)


def bias_kernel(pair_ref, pw_ref, bias_ref, root_ref, expand, flat):
    group = pl.program_id(1)
    per_step = bias_ref.shape[1]
    atoms = pl.num_programs(1) * per_step * QW
    span = QW * PAIR

    @pl.when((pl.program_id(0) == 0) & (group == 0))
    def _():
        rows = lax.broadcasted_iota(jnp.int32, (span, C), 0) // PAIR
        lanes = lax.broadcasted_iota(jnp.int32, (span, C), 1) % QW
        wide = lax.dot_general(
            pw_ref[...],
            head_lanes(),
            (((0,), (0,)), ((), ())),
            precision=lax.Precision.HIGHEST,
            preferred_element_type=F32,
        )
        weight = wide - jnp.mean(wide, axis=0, keepdims=True)
        full = jnp.where(rows == lanes, jnp.concatenate([weight] * QW, axis=0), 0.0)
        high = full.astype(BF16)
        expand[:, :C] = high
        expand[:, C:] = (full - high.astype(F32)).astype(BF16)

    def one(w):
        low = pair_ref[0, w * QW : w * QW + QW].reshape(span, KW)
        flat[w * span : w * span + span] = low.astype(F32)
        yield
        out = dot_tn(low, expand[...])
        roots = []
        for part in range(QW // 8):
            start = w * span + part * 8 * PAIR
            channels = [flat[pl.ds(start + c, 8, stride=PAIR), :] for c in range(PAIR)]
            mean = sum(channels[1:], channels[0]) * (1.0 / PAIR)
            center = [channel - mean for channel in channels]
            squares = [value * value for value in center]
            spread = sum(squares[1:], squares[0]) * (1.0 / PAIR)
            roots.append(lax.rsqrt(spread + 1e-05))
        yield
        root = jnp.concatenate(roots * HEADS, axis=0).T
        value = (out[:, :C] + out[:, C:]) * (root * LOG2E)
        start = lax.axis_index("win") * atoms + (group * per_step + w) * QW - HALO
        position = start + lax.broadcasted_iota(jnp.int32, (KW, C), 0)
        valid = (position >= 0) & (position < lax.axis_size("win") * atoms)
        bias_ref[0, w] = jnp.where(valid, value, INVALID * LOG2E)
        root_ref[0, w] = root.astype(BF16)

    for _ in pipeline([one(w) for w in range(per_step)]):
        pass


def head_lanes():
    rows = lax.broadcasted_iota(jnp.int32, (HEADS, C), 0)
    lanes = lax.broadcasted_iota(jnp.int32, (HEADS, C), 1) // QW
    return jnp.where(rows == lanes, 1.0, 0.0)


def bias_table(pair, turned_weight):
    structs, atoms = pair.shape[:2]
    count = min(8, atoms // QW)
    rows = count * QW
    table = pl.BlockSpec((1, count, KW, C), lambda s, i: (s, i, 0, 0))
    return pl.pallas_call(
        bias_kernel,
        grid=(structs, atoms // rows),
        in_specs=[
            pl.BlockSpec((1, rows, PAIR, KW), lambda s, i: (s, i, 0, 0)),
            pl.BlockSpec((HEADS, PAIR), lambda s, i: (0, 0)),
        ],
        out_specs=[table, table],
        scratch_shapes=[
            pltpu.VMEM((QW * PAIR, 2 * C), BF16),
            pltpu.VMEM((rows * PAIR, KW), F32),
        ],
        out_shape=[
            jax.ShapeDtypeStruct((structs, atoms // QW, KW, C), F32),
            jax.ShapeDtypeStruct((structs, atoms // QW, KW, C), BF16),
        ],
        compiler_params=pltpu.CompilerParams(vmem_limit_bytes=VMEM_LIMIT),
        cost_estimate=pl.CostEstimate(flops=10**9, bytes_accessed=15 * 2**20, transcendentals=0),
        name="pair_bias",
    )(pair, turned_weight)


def main_kernel(
    ids_ref,
    x_ref,
    xlo_ref,
    xhi_ref,
    g_ref,
    bias_hbm,
    root_hbm,
    pair_ref,
    cond_ref,
    clo_ref,
    chi_ref,
    w_ref,
    vec_ref,
    out_ref,
    grad_ref,
    ride_ref,
    away_ref,
    send_ref,
    keep_ref,
    packed_ref,
    bias_ref,
    root_ref,
    table_sem,
    dbias_ref,
    dvec_ref,
    pair_scr,
    pair_sem,
    pair_total,
    wq,
    w6,
    win,
    wo,
    wqt,
    w6t,
    wint,
    wot,
    wc1,
    wc2,
    mask,
    t_s1,
    t_h1,
    t_hs,
    t_hh,
    t_g1,
    t_s2,
    t_h2,
    t_g2,
    a_s1,
    a_h1,
    a_g1,
    a_s2,
    a_h2,
    a_g2,
    a_hs,
    a_hh,
    nh_scr,
    ih_scr,
    ah_scr,
    k_scr,
    v_scr,
    q_scr,
    gate_scr,
    ada_scr,
    n1_scr,
    inv_scr,
    o_scr,
    p_scr,
    do_scr,
    dd_scr,
    d4_scr,
    dk_scr,
    dv_scr,
    dx_scr,
):
    step = pl.program_id(0)
    structs, atoms, _ = cond_ref.shape
    windows = atoms // QW
    unroll = min(UNROLL, windows)
    tile = min(TILE, atoms)
    tiles = atoms // tile
    s = [lax.rem(ids_ref[step * PACK + b], structs) for b in range(PACK)]

    def cond_rows(source):
        normed, _ = layer_stats(source)
        one = (normed * vec_ref[0:1]).astype(BF16)
        two = (normed * vec_ref[4:5]).astype(BF16)
        return normed, one, two

    def block(at):
        return packed_ref.at[at * C : at * C + C]

    def joined(ref, st):
        return ref[st].astype(F32) + ref[structs + st].astype(F32)

    bias_copy = pltpu.make_async_copy(bias_hbm, bias_ref, table_sem.at[0])
    root_copy = pltpu.make_async_copy(root_hbm, root_ref, table_sem.at[1])
    chunk = min(8, windows)
    chunks = structs * windows // chunk

    def pair_copy(at):
        st, first = divmod(at * chunk, windows)
        return pltpu.make_async_copy(
            pair_ref.at[st, pl.ds(first * QW, chunk * QW)],
            pair_scr.at[at % SLOTS],
            pair_sem.at[at % SLOTS],
        )

    @pl.when(step == 0)
    def _():
        bias_copy.start()
        root_copy.start()
        for at in range(min(SLOTS, chunks)):
            pair_copy(at).start()

        def low(b):
            return w_ref[b].astype(BF16)

        for at, b in enumerate((2, 5, 3, 4)):
            wq[:, at * C : at * C + C] = low(b)
        w6[...] = low(6)
        for at in range(4):
            win[:, at * C : at * C + C] = low(11 + at)
        for at in range(2):
            wo[at * C : at * C + C, :] = low(15 + at)
        for source, turned in ((wq, wqt), (w6, w6t), (win, wint), (wo, wot)):
            turned[...] = source[...].T
        for at, b in enumerate((0, 1, 7)):
            wc1[:, at * C : at * C + C] = low(b)
        for at, b in enumerate((8, 9, 10)):
            wc2[:, at * C : at * C + C] = low(b)
        rows_head = lax.broadcasted_iota(jnp.int32, (C, C), 0) // QW
        lane_head = lax.broadcasted_iota(jnp.int32, (C, C), 1) // (C // HEADS)
        mask[...] = jnp.where(rows_head == lane_head, 1.0, 0.0).astype(BF16)
        for acc in (a_s1, a_h1, a_g1, a_s2, a_h2, a_g2, a_hs, a_hh, packed_ref, dvec_ref):
            acc[...] = jnp.zeros_like(acc)
        dbias_ref[...] = jnp.zeros_like(dbias_ref)
        pair_total[...] = jnp.zeros_like(pair_total)
        for st in range(structs):

            def table(i, carry):
                rows = pl.ds(pl.multiple_of(i * tile, tile), tile)
                _, one, two = cond_rows(cond_ref[st, rows])
                first = dot(one, wc1[...])
                t_s1[st, rows] = jax.nn.sigmoid(first[:, :C] + vec_ref[1:2])
                t_h1[st, rows] = first[:, C : 2 * C]
                t_g1[st, rows] = jax.nn.sigmoid(first[:, 2 * C :] + vec_ref[3:4])
                second = dot(two, wc2[...])
                t_s2[st, rows] = jax.nn.sigmoid(second[:, :C] + vec_ref[5:6])
                t_h2[st, rows] = second[:, C : 2 * C]
                t_g2[st, rows] = jax.nn.sigmoid(second[:, 2 * C :] + vec_ref[6:7])
                return carry

            lax.fori_loop(0, tiles, table, 0)
            _, one, _ = cond_rows(jnp.concatenate([joined(clo_ref, st), joined(chi_ref, st)], axis=0))
            first = dot(one, wc1[:, : 2 * C])
            t_hs[st] = jax.nn.sigmoid(first[:, :C] + vec_ref[1:2])
            t_hh[st] = first[:, C:]

    @pl.when(step == 0)
    def _():
        bias_copy.wait()

    def project(b, i):
        start = i * tile
        rows = pl.ds(start, tile)
        pad = pl.ds(start + HALO, tile)
        normed, inverse = layer_stats(x_ref[b, rows].astype(F32))
        n1_scr[b, rows] = normed
        inv_scr[b, rows] = jnp.broadcast_to(inverse, (tile, C))
        ada = (t_s1[s[b], rows] * normed + t_h1[s[b], rows]).astype(BF16)
        ada_scr[b, rows] = ada
        yield
        out = dot(ada, wq[...])
        yield
        q_scr[b, rows] = (out[:, :C] + vec_ref[2:3]).astype(BF16)
        gate_scr[b, rows] = jax.nn.sigmoid(out[:, C : 2 * C])
        k_scr[b, pad] = out[:, 2 * C : 3 * C].astype(BF16)
        v_scr[b, pad] = out[:, 3 * C :].astype(BF16)

    def project_halo(b):
        halo = jnp.concatenate([xlo_ref[b], xhi_ref[b]], axis=0).astype(F32)
        normed, inverse = layer_stats(halo)
        ada = (t_hs[s[b]] * normed + t_hh[s[b]]).astype(BF16)
        nh_scr[b] = normed
        ih_scr[b] = jnp.broadcast_to(inverse, (2 * HALO, C))
        ah_scr[b] = ada
        yield
        out = dot(ada, wq[:, 2 * C :])
        yield
        k_scr[b, :HALO] = out[:HALO, :C].astype(BF16)
        v_scr[b, :HALO] = out[:HALO, C:].astype(BF16)
        k_scr[b, HALO + atoms :] = out[HALO:, :C].astype(BF16)
        v_scr[b, HALO + atoms :] = out[HALO:, C:].astype(BF16)

    lane_head = lax.broadcasted_iota(jnp.int32, (QW, C), 1) // (C // HEADS)

    def spread(rows):
        return jnp.concatenate([rows] * HEADS, axis=0) * mask[...]

    def gathered(full):
        parts = [full[h * QW : h * QW + QW] for h in range(HEADS)]
        last = parts[HEADS - 1]
        for h in range(HEADS - 2, -1, -1):
            last = jnp.where(lane_head == h, parts[h], last)
        return last

    def attend(b, group):
        scores = []
        for w in group:
            queries = spread(q_scr[b, w * QW : w * QW + QW])
            scores.append(dot(k_scr[b, w * QW : w * QW + KW], queries.T))
        yield
        probs = []
        for u, w in enumerate(group):
            value = scores[u] * (FACTOR * LOG2E) + bias_ref[s[b], w]
            exps = jnp.exp2(value - jnp.max(value, axis=0, keepdims=True))
            prob = (exps * (1.0 / rows_sum(exps))).astype(BF16)
            p_scr[b, w] = prob
            probs.append(prob)
        yield
        fulls = [dot_tn(probs[u], v_scr[b, w * QW : w * QW + KW]) for u, w in enumerate(group)]
        yield
        for u, w in enumerate(group):
            o_scr[b, w * QW : w * QW + QW] = gathered(fulls[u])

    def middle(b, i):
        rows = pl.ds(i * tile, tile)
        gate = gate_scr[b, rows]
        mixed = o_scr[b, rows]
        y = (gate * mixed).astype(BF16)
        yield
        attn = dot(y, w6[...])
        yield
        gate_one = t_g1[s[b], rows]
        x1 = x_ref[b, rows].astype(F32) + gate_one * attn
        normed, inverse = layer_stats(x1)
        scale_two = t_s2[s[b], rows]
        ada = (scale_two * normed + t_h2[s[b], rows]).astype(BF16)
        yield
        expand = dot(ada, win[...])
        yield
        a = expand[:, :FF]
        up = expand[:, FF:]
        sig = jax.nn.sigmoid(a)
        silu = a * sig
        hid = (silu * up).astype(BF16)
        yield
        ff = dot(hid, wo[...])
        gate_two = t_g2[s[b], rows]
        g = g_ref[b, rows].astype(F32)
        dff = (g * gate_two).astype(BF16)
        dhid = dot(dff, wot[...])
        yield
        out_ref[b, rows] = (x1 + gate_two * ff).astype(BF16)
        a_g2[s[b], rows] += g * ff
        da = (dhid * up * (sig + silu * (1.0 - sig))).astype(BF16)
        db = (dhid * silu).astype(BF16)
        dab = jnp.concatenate([da, db], axis=1)
        yield
        dada = dot(dab, wint[...])
        yield
        a_s2[s[b], rows] += dada * normed
        a_h2[s[b], rows] += dada
        dx1 = g + layer_back(normed, inverse, dada * scale_two)
        dx_scr[b, rows] = dx1
        a_g1[s[b], rows] += dx1 * attn
        dattn = (dx1 * gate_one).astype(BF16)
        yield
        dy = dot(dattn, w6t[...])
        dwo = dot_tn(dff, hid)
        dwin = dot_tn(ada, dab)
        dw6 = dot_tn(y, dattn)
        yield
        do = (dy * gate).astype(BF16)
        do_scr[b, rows] = do
        dd_scr[b, rows] = (do.astype(F32) * mixed * -1.0).astype(BF16)
        d4_scr[b, rows, C : 2 * C] = (dy * mixed * gate * (1.0 - gate)).astype(BF16)
        block(15)[...] += dwo[:, :C]
        block(16)[...] += dwo[:, C:]
        for at in range(4):
            block(11 + at)[...] += dwin[:, at * C : at * C + C]
        block(6)[...] += dw6

    dk_scr[...] = jnp.zeros_like(dk_scr)
    dv_scr[...] = jnp.zeros_like(dv_scr)
    ones = jnp.ones((KW, C), BF16)

    def attend_back(b, group):
        diffs = []
        spreads = []
        for w in group:
            dox = spread(do_scr[b, w * QW : w * QW + QW])
            ddx = spread(dd_scr[b, w * QW : w * QW + QW])
            values = jnp.concatenate([v_scr[b, w * QW : w * QW + KW], ones], axis=1)
            diffs.append(dot(values, jnp.concatenate([dox.T, ddx.T], axis=0)))
            spreads.append(dox)
        yield
        grads = []
        for u, w in enumerate(group):
            ds = p_scr[b, w].astype(F32) * diffs[u]
            dbias_ref[s[b], w] += ds
            grads.append(ds.astype(BF16))
        yield
        fulls = []
        dks = []
        dvs = []
        for u, w in enumerate(group):
            fulls.append(dot_tn(grads[u], k_scr[b, w * QW : w * QW + KW]))
            dks.append(dot(grads[u], spread(q_scr[b, w * QW : w * QW + QW])))
            dvs.append(dot(p_scr[b, w], spreads[u]))
        yield
        for u, w in enumerate(group):
            dq = gathered(fulls[u]) * FACTOR
            dvec_ref[2] += jnp.sum(dq.reshape(QW // 8, 8, C), axis=0)
            d4_scr[b, w * QW : w * QW + QW, :C] = dq.astype(BF16)
            dk_scr[b, w * QW : w * QW + KW] += dks[u]
            dv_scr[b, w * QW : w * QW + KW] += dvs[u]

    def finish(b, i):
        start = i * tile
        rows = pl.ds(start, tile)
        pad = pl.ds(start + HALO, tile)
        d4_scr[b, rows, 2 * C : 3 * C] = (dk_scr[b, pad] * FACTOR).astype(BF16)
        d4_scr[b, rows, 3 * C :] = dv_scr[b, pad].astype(BF16)
        yield
        d4 = d4_scr[b, rows]
        dwq = dot_tn(ada_scr[b, rows], d4)
        dada = dot(d4, wqt[...])
        yield
        for at, which in enumerate((2, 5, 3, 4)):
            block(which)[...] += dwq[:, at * C : at * C + C]
        normed = n1_scr[b, rows]
        a_s1[s[b], rows] += dada * normed
        a_h1[s[b], rows] += dada
        grad = dx_scr[b, rows] + layer_back(normed, inv_scr[b, rows], dada * t_s1[s[b], rows])
        dx_scr[b, rows] = grad
        grad_ref[b, rows] = grad.astype(BF16)

    def finish_halo(b):
        spans = (slice(0, HALO), slice(HALO + atoms, None))
        dk = jnp.concatenate([dk_scr[b, span] for span in spans], axis=0) * FACTOR
        dv = jnp.concatenate([dv_scr[b, span] for span in spans], axis=0)
        dkv = jnp.concatenate([dk.astype(BF16), dv.astype(BF16)], axis=1)
        yield
        dw = dot_tn(ah_scr[b], dkv)
        dada = dot(dkv, wqt[2 * C :])
        yield
        block(3)[...] += dw[:, :C]
        block(4)[...] += dw[:, C:]
        normed = nh_scr[b]
        a_hs[s[b]] += dada * normed
        a_hh[s[b]] += dada
        rim = layer_back(normed, ih_scr[b], dada * t_hs[s[b]]).astype(BF16)
        even = lax.axis_index("win") % 2 == 0
        ride_ref[b] = jnp.where(even, rim[HALO:], rim[:HALO])
        away_ref[b] = jnp.where(even, rim[:HALO], rim[HALO:])

    groups = [tuple(range(at, at + unroll)) for at in range(0, windows, unroll)]

    def phases(b):
        return [
            (3, [project_halo(b)] + [project(b, i) for i in range(tiles)]),
            (4, [attend(b, group) for group in groups]),
            (11, [middle(b, i) for i in range(tiles)]),
            (4, [attend_back(b, group) for group in groups]),
            (3, [finish_halo(b)] + [finish(b, i) for i in range(tiles)]),
        ]

    together([phases(b) for b in range(PACK)])

    @pl.when(step == pl.num_programs(0) - 1)
    def _():
        for at in (15, 16):
            block(at)[...] = block(at)[...].T

        def apply(source, normed, parts, weight, blocks, gain):
            joined_parts = jnp.concatenate(parts, axis=1)
            grads = dot_tn(source, joined_parts)
            back = dot_nt(joined_parts, weight) * normed
            for at, which in enumerate(blocks):
                block(which)[...] += grads[:, at * C : at * C + C]
            dvec_ref[gain] += jnp.sum(back.reshape(-1, 8, C), axis=0)

        def bias_sum(at, part):
            dvec_ref[at] += jnp.sum(part.astype(F32).reshape(-1, 8, C), axis=0)

        def pre(total, gate):
            return (total * gate * (1.0 - gate)).astype(BF16)

        def conditioning(st, i):
            rows = pl.ds(i * tile, tile)
            normed, one, two = cond_rows(cond_ref[st, rows])
            first = [
                pre(a_s1[st, rows], t_s1[st, rows]),
                a_h1[st, rows].astype(BF16),
                pre(a_g1[st, rows], t_g1[st, rows]),
            ]
            second = [
                pre(a_s2[st, rows], t_s2[st, rows]),
                a_h2[st, rows].astype(BF16),
                pre(a_g2[st, rows], t_g2[st, rows]),
            ]
            yield
            for at, part in ((1, first[0]), (3, first[2]), (5, second[0]), (6, second[2])):
                bias_sum(at, part)
            apply(one, normed, first, wc1[...], (0, 1, 7), 0)
            apply(two, normed, second, wc2[...], (8, 9, 10), 4)

        def conditioning_halo(st):
            source = jnp.concatenate([joined(clo_ref, st), joined(chi_ref, st)], axis=0)
            normed, one, _ = cond_rows(source)
            parts = [pre(a_hs[st], t_hs[st]), a_hh[st].astype(BF16)]
            yield
            bias_sum(1, parts[0])
            apply(one, normed, parts, wc1[:, : 2 * C], (0, 1), 0)

        items = [conditioning_halo(st) for st in range(structs)]
        items += [conditioning(st, i) for st in range(structs) for i in range(tiles)]
        for _ in pipeline(items):
            pass

        root_copy.wait()
        for at in range(chunks):
            pair_copy(at).wait()
            st, first = divmod(at * chunk, windows)
            lefts = []
            rights = []
            for w in range(chunk):
                lefts.append(
                    pair_scr[at % SLOTS, w * QW : w * QW + QW].reshape(QW * PAIR, KW)
                )
                grad = dbias_ref[st, first + w] * root_ref[st, first + w].astype(F32)
                rights.append(grad.astype(BF16))
            left = jnp.concatenate(lefts, axis=1)
            pair_total[...] += dot(left, jnp.concatenate(rights, axis=0))
            if at + SLOTS < chunks:
                pair_copy(at + SLOTS).start()
        lanes = lax.broadcasted_iota(jnp.int32, (PAIR, C), 1) % QW
        acc = jnp.zeros((PAIR, C), F32)
        for q in range(QW):
            acc = acc + jnp.where(lanes == q, pair_total[q * PAIR : q * PAIR + PAIR], 0.0)
        half = NBLK * C // 2
        side = lax.axis_index("samp") % 2
        send_ref[:half] = packed_ref[pl.ds(pl.multiple_of((1 - side) * half, 64), half)]
        keep_ref[...] = packed_ref[pl.ds(pl.multiple_of(side * half, 64), half)]
        send_ref[half:] = jnp.concatenate(
            [rows_sum(dvec_ref[at]) for at in range(7)]
            + [jnp.zeros((1, C), F32), acc - jnp.mean(acc, axis=0, keepdims=True)],
            axis=0,
        )


def main_call(
    ids, atoms, low_msg, high_msg, cotangent, bias, root, pair, cond, weights, vectors
):
    samples, rows, _ = atoms.shape
    structs = cond.shape[0]
    windows = rows // QW
    padded = rows + 2 * HALO

    def per_sample(*shape):
        zeros = (0,) * len(shape)
        return pl.BlockSpec((PACK,) + shape, lambda i, _: (i,) + zeros)

    def whole(*shape):
        zeros = (0,) * len(shape)
        return pl.BlockSpec(shape, lambda i, _: zeros, pipeline_mode=pl.Buffered(1))

    def table(count=rows):
        return pltpu.VMEM((structs, count, C), F32)

    cond_part = pl.BlockSpec((2 * structs, HALO, C), lambda i, _: (samples // (2 * structs), 0, 0))
    shape = jax.ShapeDtypeStruct
    return pl.pallas_call(
        main_kernel,
        grid_spec=pltpu.PrefetchScalarGridSpec(
            num_scalar_prefetch=1,
            grid=(samples // PACK,),
            in_specs=[
                per_sample(rows, C),
                per_sample(HALO, C),
                per_sample(HALO, C),
                per_sample(rows, C),
                pl.BlockSpec(memory_space=pl.ANY),
                pl.BlockSpec(memory_space=pl.ANY),
                pl.BlockSpec(memory_space=pl.ANY),
                whole(structs, rows, C),
                cond_part,
                cond_part,
                whole(NBLK, C, C),
                whole(7, C),
            ],
            out_specs=[
                per_sample(rows, C),
                per_sample(rows, C),
                per_sample(HALO, C),
                per_sample(HALO, C),
                whole(NBLK * C // 2 + 8 + PAIR, C),
                whole(NBLK * C // 2, C),
            ],
            scratch_shapes=[
                pltpu.VMEM((NBLK * C, C), F32),
                pltpu.VMEM((structs, windows, KW, C), F32),
                pltpu.VMEM((structs, windows, KW, C), BF16),
                pltpu.SemaphoreType.DMA((2,)),
                pltpu.VMEM((structs, windows, KW, C), F32),
                pltpu.VMEM((7, 8, C), F32),
                pltpu.VMEM((SLOTS, min(rows, 8 * QW), PAIR, KW), BF16),
                pltpu.SemaphoreType.DMA((SLOTS,)),
                pltpu.VMEM((QW * PAIR, C), F32),
                pltpu.VMEM((C, 4 * C), BF16),
                pltpu.VMEM((C, C), BF16),
                pltpu.VMEM((C, 2 * FF), BF16),
                pltpu.VMEM((FF, C), BF16),
                pltpu.VMEM((4 * C, C), BF16),
                pltpu.VMEM((C, C), BF16),
                pltpu.VMEM((2 * FF, C), BF16),
                pltpu.VMEM((C, FF), BF16),
                pltpu.VMEM((C, 3 * C), BF16),
                pltpu.VMEM((C, 3 * C), BF16),
                pltpu.VMEM((C, C), BF16),
                table(),
                table(),
                table(2 * HALO),
                table(2 * HALO),
                table(),
                table(),
                table(),
                table(),
                table(),
                table(),
                table(),
                table(),
                table(),
                table(),
                table(2 * HALO),
                table(2 * HALO),
                pltpu.VMEM((PACK, 2 * HALO, C), F32),
                pltpu.VMEM((PACK, 2 * HALO, C), F32),
                pltpu.VMEM((PACK, 2 * HALO, C), BF16),
                pltpu.VMEM((PACK, padded, C), BF16),
                pltpu.VMEM((PACK, padded, C), BF16),
                pltpu.VMEM((PACK, rows, C), BF16),
                pltpu.VMEM((PACK, rows, C), F32),
                pltpu.VMEM((PACK, rows, C), BF16),
                pltpu.VMEM((PACK, rows, C), F32),
                pltpu.VMEM((PACK, rows, C), F32),
                pltpu.VMEM((PACK, rows, C), F32),
                pltpu.VMEM((PACK, windows, KW, C), BF16),
                pltpu.VMEM((PACK, rows, C), BF16),
                pltpu.VMEM((PACK, rows, C), BF16),
                pltpu.VMEM((PACK, rows, 4 * C), BF16),
                pltpu.VMEM((PACK, padded, C), F32),
                pltpu.VMEM((PACK, padded, C), F32),
                pltpu.VMEM((PACK, rows, C), F32),
            ],
        ),
        out_shape=[
            shape((samples, rows, C), BF16),
            shape((samples, rows, C), BF16),
            shape((samples, HALO, C), BF16),
            shape((samples, HALO, C), BF16),
            shape((NBLK * C // 2 + 8 + PAIR, C), F32),
            shape((NBLK * C // 2, C), F32),
        ],
        compiler_params=pltpu.CompilerParams(vmem_limit_bytes=VMEM_LIMIT),
        name="block",
    )(
        ids,
        atoms,
        low_msg,
        high_msg,
        cotangent,
        bias,
        root,
        pair,
        cond,
        low_msg,
        high_msg,
        weights,
        vectors,
    )


def split_low(values):
    high = values.astype(BF16)
    return high, (values - high.astype(F32)).astype(BF16)


def update_kernel(
    own_ref,
    other_ref,
    small_ref,
    sl_ref,
    sr_ref,
    rl_ref,
    rr_ref,
    w_ref,
    ew_ref,
    vec_ref,
    sv_ref,
    ev_ref,
    pw_ref,
    sp_ref,
    ep_ref,
    rows_ref,
    tv_ref,
    tp_ref,
    left_ref,
    right_ref,
    neww_ref,
    low_ref,
    newv_ref,
    newp_ref,
    nsv_ref,
    nsp_ref,
    neww_ema_ref,
    newv_ema_ref,
    newp_ema_ref,
    turned,
    total_ref,
):
    half = own_ref.shape[0]
    side = lax.axis_index("samp") % 2
    total_ref[pl.ds(pl.multiple_of(side * half, 64), half)] = own_ref[...].astype(F32)
    total_ref[pl.ds(pl.multiple_of((1 - side) * half, 64), half)] = other_ref[...].astype(F32)
    count = sl_ref.shape[1]
    own = pl.ds(lax.axis_index("win") * count, count)

    def product(parts, right):
        high, low = split_low(right)
        lefts = [split_low(part) for part in parts]
        tall = jnp.concatenate([a for a, _ in lefts] + [b for _, b in lefts], axis=0)
        size = tall.shape[0] // 2
        first = dot(tall, high)
        return first[:size] + first[size:] + dot(tall[:size], low)

    def one(b):
        block = total_ref[b * C : b * C + C]
        turned[b] = block.T
        pad = jnp.zeros((16 - count, C), F32) if count < 16 else None

        def rows(values):
            return values if pad is None else jnp.concatenate([values, pad], axis=0)

        own_rows = total_ref[pl.ds(b * C + lax.axis_index("win") * count, count)]
        rows_ref[b] = own_rows
        yield
        own_cols = turned[b, own]
        both = product([rows(own_cols), rows(rl_ref[b])], block)
        left = product([rows(own_rows)], turned[b])
        size = max(count, 16)
        yield
        step = product([both[size:]], rr_ref[b])
        right_ref[b] = stat_decay * sr_ref[b] + (1.0 - stat_decay) * both[:count]
        left_ref[b] = stat_decay * sl_ref[b] + (1.0 - stat_decay) * left[:count]
        yield
        new = w_ref[b, own] - matrix_rate * step[:count]
        neww_ref[b] = new
        low_ref[b] = new.astype(BF16)
        neww_ema_ref[b] = ema_decay * ew_ref[b] + (1.0 - ema_decay) * new

    for _ in pipeline([beside([one(b) for b in range(at, min(at + 6, NBLK))]) for at in range(0, NBLK, 6)]):
        pass
    sums = small_ref[8:]
    pair_total = lax.dot_general(
        head_lanes(),
        sums,
        (((1,), (1,)), ((), ())),
        precision=lax.Precision.HIGHEST,
        preferred_element_type=F32,
    )
    for total, param, stat, ema, out, new_ref, stat_ref, ema_ref in (
        (small_ref[:7], vec_ref, sv_ref, ev_ref, tv_ref, newv_ref, nsv_ref, newv_ema_ref),
        (pair_total, pw_ref, sp_ref, ep_ref, tp_ref, newp_ref, nsp_ref, newp_ema_ref),
    ):
        out[...] = total
        new_stat = stat_decay * stat[...] + (1.0 - stat_decay) * total * total
        stat_ref[...] = new_stat
        new = param[...] - vector_rate * total * lax.rsqrt(new_stat)
        new_ref[...] = new
        ema_ref[...] = ema_decay * ema[...] + (1.0 - ema_decay) * new


def update_call(*args):
    rows = args[3].shape
    vec = args[9].shape
    pw = args[12].shape
    full = pl.BlockSpec(memory_space=pltpu.VMEM)

    def shape(dims, kind=F32):
        return jax.ShapeDtypeStruct(dims, kind)

    def out_block(dims):
        zeros = (0,) * len(dims)
        return pl.BlockSpec(dims, lambda i: zeros)

    outs = [rows, vec, pw, rows, rows, rows, rows, vec, pw, vec, pw, rows, vec, pw]
    return pl.pallas_call(
        update_kernel,
        grid=(1,),
        in_specs=[full] * len(args),
        out_specs=[out_block(dims) for dims in outs],
        out_shape=[
            shape(dims, BF16 if at == 6 else F32) for at, dims in enumerate(outs)
        ],
        scratch_shapes=[pltpu.VMEM((NBLK, C, C), F32), pltpu.VMEM((NBLK * C, C), F32)],
        compiler_params=pltpu.CompilerParams(vmem_limit_bytes=VMEM_LIMIT),
        name="update",
    )(*args)


def passed(shard, by):
    devices = lax.axis_size("win")
    pairs = [(i, i + by) for i in range(devices) if 0 <= i + by < devices]
    return lax.ppermute(shard, "win", pairs)


def rounded(values):
    return lax.reduce_precision(values, exponent_bits=8, mantissa_bits=7)


def partner(values, axis, bit):
    devices = lax.axis_size(axis)
    return lax.ppermute(values, axis, [(i, i ^ bit) for i in range(devices)])


def bits(axis):
    devices = lax.axis_size(axis)
    return [(axis, 1 << at) for at in range((devices - 1).bit_length())]


def neighbours(values):
    devices = lax.axis_size("win")
    pairs = [(i, i + 1) for i in range(1, devices - 1, 2)]
    return lax.ppermute(values, "win", pairs + [(j, i) for i, j in pairs])


def exchange(part, small, axis, bit, extra=()):
    count, size = small.shape[0], part.shape[0]
    high = rounded(small)
    rest = rounded(small - high)
    message = [part.astype(BF16), high.astype(BF16), rest.astype(BF16), *extra]
    got = partner(jnp.concatenate(message, axis=0), axis, bit)
    theirs = got[size : size + 2 * count].astype(F32)
    total = (high + rest) + (theirs[:count] + theirs[count:])
    return got[:size].astype(F32), total, got[size + 2 * count :]


def summed(send, keep, ride, away):
    half = keep.shape[0]
    arrived = neighbours(away)
    first, *halvings = bits("samp")
    got = partner(send, *first)
    values = keep + got[:half]
    small = send[half:] + got[half:]
    for axis, bit in halvings:
        side = (lax.axis_index(axis) // bit) % 2
        half = values.shape[0] // 2
        kept = lax.dynamic_slice_in_dim(values, side * half, half)
        got, small, _ = exchange(
            lax.dynamic_slice_in_dim(values, (1 - side) * half, half), small, axis, bit
        )
        values = kept + got
    values, arrived = lax.optimization_barrier((values, arrived))
    for at, (axis, bit) in enumerate(bits("win")):
        values = rounded(values)
        extra = [ride.reshape(-1, C)] if at == 0 else []
        got, small, rest = exchange(values, small, axis, bit, extra)
        values = values + got
        if at == 0:
            rode = rest.reshape(ride.shape)
    values = values.astype(BF16)
    for axis, bit in reversed(halvings):
        side = (lax.axis_index(axis) // bit) % 2
        other = partner(values, axis, bit)
        values = jnp.where(
            side == 0,
            jnp.concatenate([values, other]),
            jnp.concatenate([other, values]),
        )
    return values, first, small, rode, arrived


def body(
    atoms,
    cond,
    pair,
    struct_ids,
    cotangent,
    weights,
    vectors,
    pair_weight,
    stat_left,
    stat_right,
    root_left,
    root_right,
    stat_vectors,
    stat_pair,
    ema_weights,
    ema_vectors,
    ema_pair,
):
    rows = atoms.shape[1]
    messages = []
    for span in (slice(0, HALO), slice(rows - HALO, rows)):
        high = rounded(cond[:, span])
        rest = cond[:, span] - high
        parts = [atoms[:, span], high.astype(BF16), rest.astype(BF16)]
        messages.append(jnp.concatenate(parts, axis=0))
    first, last = messages
    low_msg, high_msg = passed(last, 1), passed(first, -1)
    bias, root = bias_table(pair, pair_weight.T)
    result, grad_atoms, ride, away, send, keep = main_call(
        struct_ids, atoms, low_msg, high_msg, cotangent, bias, root, pair, cond, weights, vectors
    )
    own, last_step, small, rode, arrived = summed(send, keep, ride, away)
    even = lax.axis_index("win") % 2 == 0
    below = jnp.where(even, arrived, rode)
    above = jnp.where(even, rode, arrived)
    for span, part in ((slice(0, HALO), below), (slice(rows - HALO, rows), above)):
        edge = grad_atoms[:, span].astype(F32) + part.astype(F32)
        grad_atoms = grad_atoms.at[:, span].set(edge.astype(BF16))
    other = partner(own, *last_step)
    outs = list(
        update_call(
            own,
            other,
            small,
            stat_left,
            stat_right,
            root_left,
            root_right,
            weights,
            ema_weights,
            vectors,
            stat_vectors,
            ema_vectors,
            pair_weight.T,
            stat_pair.T,
            ema_pair.T,
        )
    )
    for at in (2, 8, 10, 13):
        outs[at] = outs[at].T
    return (result, grad_atoms, *outs)


def solution(mesh):
    placed = (
        P("samp", "win", None),
        P("samp", "win", None),
        P("samp", "win", None, None),
        P("samp"),
        P("samp", "win", None),
        P(),
        P(),
        P(),
        P(None, "win", None),
        P(None, "win", None),
        P(None, "win", None),
        P(),
        P(),
        P(),
        P(None, "win", None),
        P(),
        P(),
    )
    return jax.shard_map(
        body,
        mesh=mesh,
        in_specs=placed,
        out_specs=(
            P("samp", "win", None),
            P("samp", "win", None),
            P(None, "win", None),
            P(),
            P(),
            P(None, "win", None),
            P(None, "win", None),
            P(None, "win", None),
            P(None, "win", None),
            P(),
            P(),
            P(),
            P(),
            P(None, "win", None),
            P(),
            P(),
        ),
        check_vma=False,
    )
```

```python
import functools
import math

import jax
import jax.numpy as jnp
from jax import lax
from jax.experimental import pallas as pl
from jax.experimental.pallas import tpu as pltpu
from jax.sharding import PartitionSpec as P

HEADS = 4
FF = 256
QW = 32
HALO = 48
KW = 128
C = 128
PAIR = 16
NBLK = 17
UNROLL = 16
PACK = 2
SLOTS = 3
TILE = 512

stat_decay = 0.5
ema_decay = 0.8
matrix_rate = 1.0
vector_rate = 0.2

F32 = jnp.float32
BF16 = jnp.bfloat16
LOG2E = math.log2(math.e)
FACTOR = 1.0 / math.sqrt(C // HEADS)
INVALID = -1000000000.0
VMEM_LIMIT = 60 * 1024 * 1024


def dot(left, right):
    return lax.dot_general(left, right, (((1,), (0,)), ((), ())), preferred_element_type=F32)


def dot_nt(left, right):
    return lax.dot_general(left, right, (((1,), (1,)), ((), ())), preferred_element_type=F32)


def dot_tn(left, right):
    return lax.dot_general(left, right, (((0,), (0,)), ((), ())), preferred_element_type=F32)


def layer_stats(values):
    center = values - jnp.mean(values, axis=-1, keepdims=True)
    inverse = lax.rsqrt(jnp.mean(center * center, axis=-1, keepdims=True) + 1e-05)
    return (center * inverse, inverse)


def layer_back(normed, inverse, grad_norm):
    return inverse * (
        grad_norm
        - jnp.mean(grad_norm, axis=-1, keepdims=True)
        - normed * jnp.mean(grad_norm * normed, axis=-1, keepdims=True)
    )


def pipeline(stages):
    waiting = list(stages)
    active = []
    while waiting or active:
        if waiting:
            active.append(waiting.pop(0))
        active = [item for item in active if next(item, active) is None]
        yield


def beside(items):
    active = list(items)
    while active:
        active = [item for item in active if next(item, active) is None]
        yield


def together(streams):
    count = len(streams[0])
    for at in range(count + len(streams) - 1):
        pipes = []
        for behind, phases in enumerate(streams):
            if 0 <= at - behind < count:
                depth, stages = phases[at - behind]
                pipes.append([pipeline(stages), depth + len(stages), 0])
        longest = max(length for _, length, _ in pipes)
        for tick in range(1, longest + 1):
            for item in pipes:
                while item[2] * longest < tick * item[1]:
                    item[2] += 1
                    next(item[0], None)
        for pipe, _, _ in pipes:
            for _ in pipe:
                pass


def rows_sum(values):
    return jnp.sum(values, axis=0, keepdims=True)


def bias_kernel(pair_ref, pw_ref, bias_ref, root_ref, expand, flat):
    group = pl.program_id(1)
    per_step = bias_ref.shape[1]
    atoms = pl.num_programs(1) * per_step * QW
    span = QW * PAIR

    @pl.when((pl.program_id(0) == 0) & (group == 0))
    def _():
        rows = lax.broadcasted_iota(jnp.int32, (span, C), 0) // PAIR
        lanes = lax.broadcasted_iota(jnp.int32, (span, C), 1) % QW
        wide = lax.dot_general(
            pw_ref[...],
            head_lanes(),
            (((0,), (0,)), ((), ())),
            precision=lax.Precision.HIGHEST,
            preferred_element_type=F32,
        )
        weight = wide - jnp.mean(wide, axis=0, keepdims=True)
        full = jnp.where(rows == lanes, jnp.concatenate([weight] * QW, axis=0), 0.0)
        high = full.astype(BF16)
        expand[:, :C] = high
        expand[:, C:] = (full - high.astype(F32)).astype(BF16)

    def one(w):
        low = pair_ref[0, w * QW : w * QW + QW].reshape(span, KW)
        flat[w * span : w * span + span] = low.astype(F32)
        yield
        out = dot_tn(low, expand[...])
        roots = []
        for part in range(QW // 8):
            start = w * span + part * 8 * PAIR
            channels = [flat[pl.ds(start + c, 8, stride=PAIR), :] for c in range(PAIR)]
            mean = sum(channels[1:], channels[0]) * (1.0 / PAIR)
            center = [channel - mean for channel in channels]
            squares = [value * value for value in center]
            spread = sum(squares[1:], squares[0]) * (1.0 / PAIR)
            roots.append(lax.rsqrt(spread + 1e-05))
        yield
        root = jnp.concatenate(roots * HEADS, axis=0).T
        value = (out[:, :C] + out[:, C:]) * (root * LOG2E)
        start = lax.axis_index("win") * atoms + (group * per_step + w) * QW - HALO
        position = start + lax.broadcasted_iota(jnp.int32, (KW, C), 0)
        valid = (position >= 0) & (position < lax.axis_size("win") * atoms)
        bias_ref[0, w] = jnp.where(valid, value, INVALID * LOG2E)
        root_ref[0, w] = root.astype(BF16)

    for _ in pipeline([one(w) for w in range(per_step)]):
        pass


def head_lanes():
    rows = lax.broadcasted_iota(jnp.int32, (HEADS, C), 0)
    lanes = lax.broadcasted_iota(jnp.int32, (HEADS, C), 1) // QW
    return jnp.where(rows == lanes, 1.0, 0.0)


def bias_table(pair, turned_weight):
    structs, atoms = pair.shape[:2]
    count = min(8, atoms // QW)
    rows = count * QW
    table = pl.BlockSpec((1, count, KW, C), lambda s, i: (s, i, 0, 0))
    return pl.pallas_call(
        bias_kernel,
        grid=(structs, atoms // rows),
        in_specs=[
            pl.BlockSpec((1, rows, PAIR, KW), lambda s, i: (s, i, 0, 0)),
            pl.BlockSpec((HEADS, PAIR), lambda s, i: (0, 0)),
        ],
        out_specs=[table, table],
        scratch_shapes=[
            pltpu.VMEM((QW * PAIR, 2 * C), BF16),
            pltpu.VMEM((rows * PAIR, KW), F32),
        ],
        out_shape=[
            jax.ShapeDtypeStruct((structs, atoms // QW, KW, C), F32),
            jax.ShapeDtypeStruct((structs, atoms // QW, KW, C), BF16),
        ],
        compiler_params=pltpu.CompilerParams(vmem_limit_bytes=VMEM_LIMIT),
        cost_estimate=pl.CostEstimate(flops=10**9, bytes_accessed=15 * 2**20, transcendentals=0),
        name="pair_bias",
    )(pair, turned_weight)


def main_kernel(
    ids_ref,
    x_ref,
    xlo_ref,
    xhi_ref,
    g_ref,
    bias_hbm,
    root_hbm,
    pair_ref,
    cond_ref,
    clo_ref,
    chi_ref,
    w_ref,
    vec_ref,
    out_ref,
    grad_ref,
    rlo_ref,
    rhi_ref,
    send_ref,
    keep_ref,
    packed_ref,
    bias_ref,
    root_ref,
    table_sem,
    dbias_ref,
    dvec_ref,
    pair_scr,
    pair_sem,
    pair_total,
    wq,
    w6,
    win,
    wo,
    wqt,
    w6t,
    wint,
    wot,
    wc1,
    wc2,
    mask,
    t_s1,
    t_h1,
    t_hs,
    t_hh,
    t_g1,
    t_s2,
    t_h2,
    t_g2,
    a_s1,
    a_h1,
    a_g1,
    a_s2,
    a_h2,
    a_g2,
    a_hs,
    a_hh,
    nh_scr,
    ih_scr,
    ah_scr,
    k_scr,
    v_scr,
    q_scr,
    gate_scr,
    ada_scr,
    n1_scr,
    inv_scr,
    o_scr,
    p_scr,
    do_scr,
    dd_scr,
    d4_scr,
    dk_scr,
    dv_scr,
    dx_scr,
):
    step = pl.program_id(0)
    structs, atoms, _ = cond_ref.shape
    windows = atoms // QW
    unroll = min(UNROLL, windows)
    tile = min(TILE, atoms)
    tiles = atoms // tile
    s = [lax.rem(ids_ref[step * PACK + b], structs) for b in range(PACK)]

    def cond_rows(source):
        normed, _ = layer_stats(source)
        one = (normed * vec_ref[0:1]).astype(BF16)
        two = (normed * vec_ref[4:5]).astype(BF16)
        return normed, one, two

    def block(at):
        return packed_ref.at[at * C : at * C + C]

    def joined(ref, st):
        return ref[st].astype(F32) + ref[structs + st].astype(F32)

    bias_copy = pltpu.make_async_copy(bias_hbm, bias_ref, table_sem.at[0])
    root_copy = pltpu.make_async_copy(root_hbm, root_ref, table_sem.at[1])
    chunk = min(8, windows)
    chunks = structs * windows // chunk

    def pair_copy(at):
        st, first = divmod(at * chunk, windows)
        return pltpu.make_async_copy(
            pair_ref.at[st, pl.ds(first * QW, chunk * QW)],
            pair_scr.at[at % SLOTS],
            pair_sem.at[at % SLOTS],
        )

    @pl.when(step == 0)
    def _():
        bias_copy.start()
        root_copy.start()
        for at in range(min(SLOTS, chunks)):
            pair_copy(at).start()

        def low(b):
            return w_ref[b].astype(BF16)

        for at, b in enumerate((2, 5, 3, 4)):
            wq[:, at * C : at * C + C] = low(b)
        w6[...] = low(6)
        for at in range(4):
            win[:, at * C : at * C + C] = low(11 + at)
        for at in range(2):
            wo[at * C : at * C + C, :] = low(15 + at)
        for source, turned in ((wq, wqt), (w6, w6t), (win, wint), (wo, wot)):
            turned[...] = source[...].T
        for at, b in enumerate((0, 1, 7)):
            wc1[:, at * C : at * C + C] = low(b)
        for at, b in enumerate((8, 9, 10)):
            wc2[:, at * C : at * C + C] = low(b)
        rows_head = lax.broadcasted_iota(jnp.int32, (C, C), 0) // QW
        lane_head = lax.broadcasted_iota(jnp.int32, (C, C), 1) // (C // HEADS)
        mask[...] = jnp.where(rows_head == lane_head, 1.0, 0.0).astype(BF16)
        for acc in (a_s1, a_h1, a_g1, a_s2, a_h2, a_g2, a_hs, a_hh, packed_ref, dvec_ref):
            acc[...] = jnp.zeros_like(acc)
        dbias_ref[...] = jnp.zeros_like(dbias_ref)
        pair_total[...] = jnp.zeros_like(pair_total)

        def table(st, i):
            rows = pl.ds(i * tile, tile)
            _, one, two = cond_rows(cond_ref[st, rows])
            yield
            first = dot(one, wc1[...])
            second = dot(two, wc2[...])
            yield
            t_s1[st, rows] = jax.nn.sigmoid(first[:, :C] + vec_ref[1:2])
            t_h1[st, rows] = first[:, C : 2 * C]
            t_g1[st, rows] = jax.nn.sigmoid(first[:, 2 * C :] + vec_ref[3:4])
            t_s2[st, rows] = jax.nn.sigmoid(second[:, :C] + vec_ref[5:6])
            t_h2[st, rows] = second[:, C : 2 * C]
            t_g2[st, rows] = jax.nn.sigmoid(second[:, 2 * C :] + vec_ref[6:7])

        def table_halo(st):
            source = jnp.concatenate([joined(clo_ref, st), joined(chi_ref, st)], axis=0)
            _, one, _ = cond_rows(source)
            yield
            first = dot(one, wc1[:, : 2 * C])
            yield
            t_hs[st] = jax.nn.sigmoid(first[:, :C] + vec_ref[1:2])
            t_hh[st] = first[:, C:]

        items = [table_halo(st) for st in range(structs)]
        items += [table(st, i) for st in range(structs) for i in range(tiles)]
        for _ in pipeline(items):
            pass

    @pl.when(step == 0)
    def _():
        bias_copy.wait()

    def project(b, i):
        start = i * tile
        rows = pl.ds(start, tile)
        pad = pl.ds(start + HALO, tile)
        normed, inverse = layer_stats(x_ref[b, rows].astype(F32))
        n1_scr[b, rows] = normed
        inv_scr[b, rows] = jnp.broadcast_to(inverse, (tile, C))
        ada = (t_s1[s[b], rows] * normed + t_h1[s[b], rows]).astype(BF16)
        ada_scr[b, rows] = ada
        yield
        out = dot(ada, wq[...])
        yield
        q_scr[b, rows] = (out[:, :C] + vec_ref[2:3]).astype(BF16)
        gate_scr[b, rows] = jax.nn.sigmoid(out[:, C : 2 * C])
        k_scr[b, pad] = out[:, 2 * C : 3 * C].astype(BF16)
        v_scr[b, pad] = out[:, 3 * C :].astype(BF16)

    def project_halo(b):
        halo = jnp.concatenate([xlo_ref[b], xhi_ref[b]], axis=0).astype(F32)
        normed, inverse = layer_stats(halo)
        ada = (t_hs[s[b]] * normed + t_hh[s[b]]).astype(BF16)
        nh_scr[b] = normed
        ih_scr[b] = jnp.broadcast_to(inverse, (2 * HALO, C))
        ah_scr[b] = ada
        yield
        out = dot(ada, wq[:, 2 * C :])
        yield
        k_scr[b, :HALO] = out[:HALO, :C].astype(BF16)
        v_scr[b, :HALO] = out[:HALO, C:].astype(BF16)
        k_scr[b, HALO + atoms :] = out[HALO:, :C].astype(BF16)
        v_scr[b, HALO + atoms :] = out[HALO:, C:].astype(BF16)

    lane_head = lax.broadcasted_iota(jnp.int32, (QW, C), 1) // (C // HEADS)

    def spread(rows):
        return jnp.concatenate([rows] * HEADS, axis=0) * mask[...]

    def gathered(full):
        parts = [full[h * QW : h * QW + QW] for h in range(HEADS)]
        last = parts[HEADS - 1]
        for h in range(HEADS - 2, -1, -1):
            last = jnp.where(lane_head == h, parts[h], last)
        return last

    def attend(b, group):
        scores = []
        for w in group:
            queries = spread(q_scr[b, w * QW : w * QW + QW])
            scores.append(dot(k_scr[b, w * QW : w * QW + KW], queries.T))
        yield
        probs = []
        for u, w in enumerate(group):
            value = scores[u] * (FACTOR * LOG2E) + bias_ref[s[b], w]
            exps = jnp.exp2(value - jnp.max(value, axis=0, keepdims=True))
            prob = (exps * (1.0 / rows_sum(exps))).astype(BF16)
            p_scr[b, w] = prob
            probs.append(prob)
        yield
        fulls = [dot_tn(probs[u], v_scr[b, w * QW : w * QW + KW]) for u, w in enumerate(group)]
        yield
        for u, w in enumerate(group):
            o_scr[b, w * QW : w * QW + QW] = gathered(fulls[u])

    def middle(b, i):
        rows = pl.ds(i * tile, tile)
        gate = gate_scr[b, rows]
        mixed = o_scr[b, rows]
        y = (gate * mixed).astype(BF16)
        yield
        attn = dot(y, w6[...])
        yield
        gate_one = t_g1[s[b], rows]
        x1 = x_ref[b, rows].astype(F32) + gate_one * attn
        normed, inverse = layer_stats(x1)
        scale_two = t_s2[s[b], rows]
        ada = (scale_two * normed + t_h2[s[b], rows]).astype(BF16)
        yield
        expand = dot(ada, win[...])
        yield
        a = expand[:, :FF]
        up = expand[:, FF:]
        sig = jax.nn.sigmoid(a)
        silu = a * sig
        hid = (silu * up).astype(BF16)
        yield
        ff = dot(hid, wo[...])
        gate_two = t_g2[s[b], rows]
        g = g_ref[b, rows].astype(F32)
        dff = (g * gate_two).astype(BF16)
        dhid = dot(dff, wot[...])
        yield
        out_ref[b, rows] = (x1 + gate_two * ff).astype(BF16)
        a_g2[s[b], rows] += g * ff
        da = (dhid * up * (sig + silu * (1.0 - sig))).astype(BF16)
        db = (dhid * silu).astype(BF16)
        dab = jnp.concatenate([da, db], axis=1)
        yield
        dada = dot(dab, wint[...])
        yield
        a_s2[s[b], rows] += dada * normed
        a_h2[s[b], rows] += dada
        dx1 = g + layer_back(normed, inverse, dada * scale_two)
        dx_scr[b, rows] = dx1
        a_g1[s[b], rows] += dx1 * attn
        dattn = (dx1 * gate_one).astype(BF16)
        yield
        dy = dot(dattn, w6t[...])
        dwo = dot_tn(dff, hid)
        dwin = dot_tn(ada, dab)
        dw6 = dot_tn(y, dattn)
        yield
        do = (dy * gate).astype(BF16)
        do_scr[b, rows] = do
        dd_scr[b, rows] = (do.astype(F32) * mixed * -1.0).astype(BF16)
        d4_scr[b, rows, C : 2 * C] = (dy * mixed * gate * (1.0 - gate)).astype(BF16)
        block(15)[...] += dwo[:, :C]
        block(16)[...] += dwo[:, C:]
        for at in range(4):
            block(11 + at)[...] += dwin[:, at * C : at * C + C]
        block(6)[...] += dw6

    ones = jnp.ones((KW, C), BF16)

    def attend_back(b, group):
        diffs = []
        spreads = []
        for w in group:
            dox = spread(do_scr[b, w * QW : w * QW + QW])
            ddx = spread(dd_scr[b, w * QW : w * QW + QW])
            values = jnp.concatenate([v_scr[b, w * QW : w * QW + KW], ones], axis=1)
            diffs.append(dot(values, jnp.concatenate([dox.T, ddx.T], axis=0)))
            spreads.append(dox)
        yield
        grads = []
        for u, w in enumerate(group):
            ds = p_scr[b, w].astype(F32) * diffs[u]
            dbias_ref[s[b], w] += ds
            grads.append(ds.astype(BF16))
        yield
        fulls = []
        dks = []
        dvs = []
        for u, w in enumerate(group):
            fulls.append(dot_tn(grads[u], k_scr[b, w * QW : w * QW + KW]))
            dks.append(dot(grads[u], spread(q_scr[b, w * QW : w * QW + QW])))
            dvs.append(dot(p_scr[b, w], spreads[u]))
        yield
        for u, w in enumerate(group):
            dq = gathered(fulls[u]) * FACTOR
            dvec_ref[2] += jnp.sum(dq.reshape(QW // 8, 8, C), axis=0)
            d4_scr[b, w * QW : w * QW + QW, :C] = dq.astype(BF16)
            seen = KW - QW if w else 0
            for scr, part in ((dk_scr, dks[u]), (dv_scr, dvs[u])):
                if seen:
                    scr[b, w * QW : w * QW + seen] += part[:seen]
                scr[b, w * QW + seen : w * QW + KW] = part[seen:]

    def finish(b, i):
        start = i * tile
        rows = pl.ds(start, tile)
        pad = pl.ds(start + HALO, tile)
        d4_scr[b, rows, 2 * C : 3 * C] = (dk_scr[b, pad] * FACTOR).astype(BF16)
        d4_scr[b, rows, 3 * C :] = dv_scr[b, pad].astype(BF16)
        yield
        d4 = d4_scr[b, rows]
        dwq = dot_tn(ada_scr[b, rows], d4)
        dada = dot(d4, wqt[...])
        yield
        for at, which in enumerate((2, 5, 3, 4)):
            block(which)[...] += dwq[:, at * C : at * C + C]
        normed = n1_scr[b, rows]
        a_s1[s[b], rows] += dada * normed
        a_h1[s[b], rows] += dada
        grad = dx_scr[b, rows] + layer_back(normed, inv_scr[b, rows], dada * t_s1[s[b], rows])
        dx_scr[b, rows] = grad
        grad_ref[b, rows] = grad.astype(BF16)

    def finish_halo(b):
        spans = (slice(0, HALO), slice(HALO + atoms, None))
        dk = jnp.concatenate([dk_scr[b, span] for span in spans], axis=0) * FACTOR
        dv = jnp.concatenate([dv_scr[b, span] for span in spans], axis=0)
        dkv = jnp.concatenate([dk.astype(BF16), dv.astype(BF16)], axis=1)
        yield
        dw = dot_tn(ah_scr[b], dkv)
        dada = dot(dkv, wqt[2 * C :])
        yield
        block(3)[...] += dw[:, :C]
        block(4)[...] += dw[:, C:]
        normed = nh_scr[b]
        a_hs[s[b]] += dada * normed
        a_hh[s[b]] += dada
        rim = layer_back(normed, ih_scr[b], dada * t_hs[s[b]]).astype(BF16)
        rlo_ref[b] = rim[:HALO]
        rhi_ref[b] = rim[HALO:]

    groups = [tuple(range(at, at + unroll)) for at in range(0, windows, unroll)]

    def phases(b):
        return [
            (3, [project_halo(b)] + [project(b, i) for i in range(tiles)]),
            (4, [attend(b, group) for group in groups]),
            (11, [middle(b, i) for i in range(tiles)]),
            (4, [attend_back(b, group) for group in groups]),
            (3, [finish_halo(b)] + [finish(b, i) for i in range(tiles)]),
        ]

    together([phases(b) for b in range(PACK)])

    @pl.when(step == pl.num_programs(0) - 1)
    def _():
        for at in (15, 16):
            block(at)[...] = block(at)[...].T

        def apply(source, normed, parts, weight, blocks, gain):
            joined_parts = jnp.concatenate(parts, axis=1)
            grads = dot_tn(source, joined_parts)
            back = dot_nt(joined_parts, weight) * normed
            for at, which in enumerate(blocks):
                block(which)[...] += grads[:, at * C : at * C + C]
            dvec_ref[gain] += jnp.sum(back.reshape(-1, 8, C), axis=0)

        def bias_sum(at, part):
            dvec_ref[at] += jnp.sum(part.astype(F32).reshape(-1, 8, C), axis=0)

        def pre(total, gate):
            return (total * gate * (1.0 - gate)).astype(BF16)

        def conditioning(st, i):
            rows = pl.ds(i * tile, tile)
            normed, one, two = cond_rows(cond_ref[st, rows])
            first = [
                pre(a_s1[st, rows], t_s1[st, rows]),
                a_h1[st, rows].astype(BF16),
                pre(a_g1[st, rows], t_g1[st, rows]),
            ]
            second = [
                pre(a_s2[st, rows], t_s2[st, rows]),
                a_h2[st, rows].astype(BF16),
                pre(a_g2[st, rows], t_g2[st, rows]),
            ]
            yield
            for at, part in ((1, first[0]), (3, first[2]), (5, second[0]), (6, second[2])):
                bias_sum(at, part)
            apply(one, normed, first, wc1[...], (0, 1, 7), 0)
            apply(two, normed, second, wc2[...], (8, 9, 10), 4)

        def conditioning_halo(st):
            source = jnp.concatenate([joined(clo_ref, st), joined(chi_ref, st)], axis=0)
            normed, one, _ = cond_rows(source)
            parts = [pre(a_hs[st], t_hs[st]), a_hh[st].astype(BF16)]
            yield
            bias_sum(1, parts[0])
            apply(one, normed, parts, wc1[:, : 2 * C], (0, 1), 0)

        items = [conditioning_halo(st) for st in range(structs)]
        items += [conditioning(st, i) for st in range(structs) for i in range(tiles)]
        for _ in pipeline(items):
            pass

        root_copy.wait()
        for at in range(chunks):
            pair_copy(at).wait()
            st, first = divmod(at * chunk, windows)
            lefts = []
            rights = []
            for w in range(chunk):
                lefts.append(
                    pair_scr[at % SLOTS, w * QW : w * QW + QW].reshape(QW * PAIR, KW)
                )
                grad = dbias_ref[st, first + w] * root_ref[st, first + w].astype(F32)
                rights.append(grad.astype(BF16))
            left = jnp.concatenate(lefts, axis=1)
            pair_total[...] += dot(left, jnp.concatenate(rights, axis=0))
            if at + SLOTS < chunks:
                pair_copy(at + SLOTS).start()
        lanes = lax.broadcasted_iota(jnp.int32, (PAIR, C), 1) % QW
        acc = jnp.zeros((PAIR, C), F32)
        for q in range(QW):
            acc = acc + jnp.where(lanes == q, pair_total[q * PAIR : q * PAIR + PAIR], 0.0)
        half = NBLK * C // 2
        side = (lax.axis_index("samp") // 2) % 2
        send = packed_ref[pl.ds(pl.multiple_of((1 - side) * half, 64), half)]
        keep_ref[...] = packed_ref[pl.ds(pl.multiple_of(side * half, 64), half)]
        small = jnp.concatenate(
            [rows_sum(dvec_ref[at]) for at in range(7)]
            + [jnp.zeros((1, C), F32), acc - jnp.mean(acc, axis=0, keepdims=True)],
            axis=0,
        )
        high, low = split_low(small)
        send_ref[:half] = send.astype(BF16)
        send_ref[half:] = jnp.concatenate([high, low], axis=0)


def main_call(
    ids, atoms, low_msg, high_msg, cotangent, bias, root, pair, cond, weights, vectors
):
    samples, rows, _ = atoms.shape
    structs = cond.shape[0]
    windows = rows // QW
    padded = rows + 2 * HALO

    def per_sample(*shape):
        zeros = (0,) * len(shape)
        return pl.BlockSpec((PACK,) + shape, lambda i, _: (i,) + zeros)

    def whole(*shape):
        zeros = (0,) * len(shape)
        return pl.BlockSpec(shape, lambda i, _: zeros, pipeline_mode=pl.Buffered(1))

    def table(count=rows):
        return pltpu.VMEM((structs, count, C), F32)

    cond_part = pl.BlockSpec((2 * structs, HALO, C), lambda i, _: (samples // (2 * structs), 0, 0))
    shape = jax.ShapeDtypeStruct
    return pl.pallas_call(
        main_kernel,
        grid_spec=pltpu.PrefetchScalarGridSpec(
            num_scalar_prefetch=1,
            grid=(samples // PACK,),
            in_specs=[
                per_sample(rows, C),
                per_sample(HALO, C),
                per_sample(HALO, C),
                per_sample(rows, C),
                pl.BlockSpec(memory_space=pl.ANY),
                pl.BlockSpec(memory_space=pl.ANY),
                pl.BlockSpec(memory_space=pl.ANY),
                whole(structs, rows, C),
                cond_part,
                cond_part,
                whole(NBLK, C, C),
                whole(7, C),
            ],
            out_specs=[
                per_sample(rows, C),
                per_sample(rows, C),
                per_sample(HALO, C),
                per_sample(HALO, C),
                whole(NBLK * C // 2 + 2 * (8 + PAIR), C),
                whole(NBLK * C // 2, C),
            ],
            scratch_shapes=[
                pltpu.VMEM((NBLK * C, C), F32),
                pltpu.VMEM((structs, windows, KW, C), F32),
                pltpu.VMEM((structs, windows, KW, C), BF16),
                pltpu.SemaphoreType.DMA((2,)),
                pltpu.VMEM((structs, windows, KW, C), F32),
                pltpu.VMEM((7, 8, C), F32),
                pltpu.VMEM((SLOTS, min(rows, 8 * QW), PAIR, KW), BF16),
                pltpu.SemaphoreType.DMA((SLOTS,)),
                pltpu.VMEM((QW * PAIR, C), F32),
                pltpu.VMEM((C, 4 * C), BF16),
                pltpu.VMEM((C, C), BF16),
                pltpu.VMEM((C, 2 * FF), BF16),
                pltpu.VMEM((FF, C), BF16),
                pltpu.VMEM((4 * C, C), BF16),
                pltpu.VMEM((C, C), BF16),
                pltpu.VMEM((2 * FF, C), BF16),
                pltpu.VMEM((C, FF), BF16),
                pltpu.VMEM((C, 3 * C), BF16),
                pltpu.VMEM((C, 3 * C), BF16),
                pltpu.VMEM((C, C), BF16),
                table(),
                table(),
                table(2 * HALO),
                table(2 * HALO),
                table(),
                table(),
                table(),
                table(),
                table(),
                table(),
                table(),
                table(),
                table(),
                table(),
                table(2 * HALO),
                table(2 * HALO),
                pltpu.VMEM((PACK, 2 * HALO, C), F32),
                pltpu.VMEM((PACK, 2 * HALO, C), F32),
                pltpu.VMEM((PACK, 2 * HALO, C), BF16),
                pltpu.VMEM((PACK, padded, C), BF16),
                pltpu.VMEM((PACK, padded, C), BF16),
                pltpu.VMEM((PACK, rows, C), BF16),
                pltpu.VMEM((PACK, rows, C), F32),
                pltpu.VMEM((PACK, rows, C), BF16),
                pltpu.VMEM((PACK, rows, C), F32),
                pltpu.VMEM((PACK, rows, C), F32),
                pltpu.VMEM((PACK, rows, C), F32),
                pltpu.VMEM((PACK, windows, KW, C), BF16),
                pltpu.VMEM((PACK, rows, C), BF16),
                pltpu.VMEM((PACK, rows, C), BF16),
                pltpu.VMEM((PACK, rows, 4 * C), BF16),
                pltpu.VMEM((PACK, padded, C), F32),
                pltpu.VMEM((PACK, padded, C), F32),
                pltpu.VMEM((PACK, rows, C), F32),
            ],
        ),
        out_shape=[
            shape((samples, rows, C), BF16),
            shape((samples, rows, C), BF16),
            shape((samples, HALO, C), BF16),
            shape((samples, HALO, C), BF16),
            shape((NBLK * C // 2 + 2 * (8 + PAIR), C), BF16),
            shape((NBLK * C // 2, C), F32),
        ],
        compiler_params=pltpu.CompilerParams(vmem_limit_bytes=VMEM_LIMIT),
        name="block",
    )(
        ids,
        atoms,
        low_msg,
        high_msg,
        cotangent,
        bias,
        root,
        pair,
        cond,
        low_msg,
        high_msg,
        weights,
        vectors,
    )


def split_low(values):
    high = values.astype(BF16)
    return high, (values - high.astype(F32)).astype(BF16)


def update_kernel(
    own_ref,
    other_ref,
    small_ref,
    sl_ref,
    sr_ref,
    rl_ref,
    rr_ref,
    w_ref,
    ew_ref,
    vec_ref,
    sv_ref,
    ev_ref,
    pw_ref,
    sp_ref,
    ep_ref,
    rows_ref,
    tv_ref,
    tp_ref,
    left_ref,
    right_ref,
    neww_ref,
    low_ref,
    newv_ref,
    newp_ref,
    nsv_ref,
    nsp_ref,
    neww_ema_ref,
    newv_ema_ref,
    newp_ema_ref,
    turned,
    total_ref,
):
    chunks, size, _ = own_ref.shape
    side = lax.axis_index("samp") % 2
    for at in range(chunks):
        for ref, place in ((own_ref, side), (other_ref, 1 - side)):
            start = pl.multiple_of((2 * at + place) * size, 16)
            total_ref[pl.ds(start, size)] = ref[at].astype(F32)
    count = sl_ref.shape[1]
    own = pl.ds(lax.axis_index("win") * count, count)

    def product(parts, right):
        high, low = split_low(right)
        lefts = [split_low(part) for part in parts]
        tall = jnp.concatenate([a for a, _ in lefts] + [b for _, b in lefts], axis=0)
        size = tall.shape[0] // 2
        first = dot(tall, high)
        return first[:size] + first[size:] + dot(tall[:size], low)

    def one(b):
        block = total_ref[b * C : b * C + C]
        turned[b] = block.T
        pad = jnp.zeros((16 - count, C), F32) if count < 16 else None

        def rows(values):
            return values if pad is None else jnp.concatenate([values, pad], axis=0)

        own_rows = total_ref[pl.ds(b * C + lax.axis_index("win") * count, count)]
        rows_ref[b] = own_rows
        yield
        own_cols = turned[b, own]
        both = product([rows(own_cols), rows(rl_ref[b])], block)
        left = product([rows(own_rows)], turned[b])
        size = max(count, 16)
        yield
        step = product([both[size:]], rr_ref[b])
        right_ref[b] = stat_decay * sr_ref[b] + (1.0 - stat_decay) * both[:count]
        left_ref[b] = stat_decay * sl_ref[b] + (1.0 - stat_decay) * left[:count]
        yield
        new = w_ref[b, own] - matrix_rate * step[:count]
        neww_ref[b] = new
        low_ref[b] = new.astype(BF16)
        neww_ema_ref[b] = ema_decay * ew_ref[b] + (1.0 - ema_decay) * new

    for _ in pipeline([beside([one(b) for b in range(at, min(at + 6, NBLK))]) for at in range(0, NBLK, 6)]):
        pass
    sums = small_ref[8:]
    pair_total = lax.dot_general(
        head_lanes(),
        sums,
        (((1,), (1,)), ((), ())),
        precision=lax.Precision.HIGHEST,
        preferred_element_type=F32,
    )
    for total, param, stat, ema, out, new_ref, stat_ref, ema_ref in (
        (small_ref[:7], vec_ref, sv_ref, ev_ref, tv_ref, newv_ref, nsv_ref, newv_ema_ref),
        (pair_total, pw_ref, sp_ref, ep_ref, tp_ref, newp_ref, nsp_ref, newp_ema_ref),
    ):
        out[...] = total
        new_stat = stat_decay * stat[...] + (1.0 - stat_decay) * total * total
        stat_ref[...] = new_stat
        new = param[...] - vector_rate * total * lax.rsqrt(new_stat)
        new_ref[...] = new
        ema_ref[...] = ema_decay * ema[...] + (1.0 - ema_decay) * new


def update_call(*args):
    rows = args[3].shape
    vec = args[9].shape
    pw = args[12].shape
    full = pl.BlockSpec(memory_space=pltpu.VMEM)

    def shape(dims, kind=F32):
        return jax.ShapeDtypeStruct(dims, kind)

    def out_block(dims):
        zeros = (0,) * len(dims)
        return pl.BlockSpec(dims, lambda i: zeros)

    outs = [rows, vec, pw, rows, rows, rows, rows, vec, pw, vec, pw, rows, vec, pw]
    return pl.pallas_call(
        update_kernel,
        grid=(1,),
        in_specs=[full] * len(args),
        out_specs=[out_block(dims) for dims in outs],
        out_shape=[
            shape(dims, BF16 if at == 6 else F32) for at, dims in enumerate(outs)
        ],
        scratch_shapes=[pltpu.VMEM((NBLK, C, C), F32), pltpu.VMEM((NBLK * C, C), F32)],
        compiler_params=pltpu.CompilerParams(vmem_limit_bytes=VMEM_LIMIT),
        name="update",
    )(*args)


def passed(shard, by):
    devices = lax.axis_size("win")
    pairs = [(i, i + by) for i in range(devices) if 0 <= i + by < devices]
    return lax.ppermute(shard, "win", pairs)


def rounded(values):
    return lax.reduce_precision(values, exponent_bits=8, mantissa_bits=7)


def partner(values, axis, bit):
    devices = lax.axis_size(axis)
    return lax.ppermute(values, axis, [(i, i ^ bit) for i in range(devices)])


def bits(axis):
    devices = lax.axis_size(axis)
    return [(axis, 1 << at) for at in range((devices - 1).bit_length())]


def exchange(part, small, axis, bit):
    size = part.shape[0]
    high = rounded(small)
    rest = rounded(small - high)
    message = [part.astype(BF16), high.astype(BF16), rest.astype(BF16)]
    got = partner(jnp.concatenate(message, axis=0), axis, bit)
    return got[:size].astype(F32), joined_terms(got[size:]) + (high + rest)


def joined_terms(terms):
    count = terms.shape[0] // 2
    wide = terms.astype(F32)
    return wide[:count] + wide[count:]


def summed(send, keep, edges):
    last, *halvings = bits("samp")
    size = keep.shape[0]
    for at, (axis, bit) in enumerate(halvings):
        if at == 0:
            got, edges = lax.optimization_barrier((partner(send, axis, bit), edges))
            values = keep + got[:size].astype(F32)
            small = joined_terms(send[size:]) + joined_terms(got[size:])
        else:
            side = (lax.axis_index(axis) // bit) % 2
            size = values.shape[0] // 2
            kept = lax.dynamic_slice_in_dim(values, side * size, size)
            part = lax.dynamic_slice_in_dim(values, (1 - side) * size, size)
            got, small = exchange(part, small, axis, bit)
            values = kept + got
    axis, bit = last
    side = (lax.axis_index(axis) // bit) % 2
    size = values.shape[0] // 2
    kept = lax.dynamic_slice_in_dim(values, side * size, size)
    part = lax.dynamic_slice_in_dim(values, (1 - side) * size, size)
    got = partner(jnp.concatenate([part, small], axis=0), axis, bit)
    values = kept + got[:size]
    small = small + got[size:]
    for axis, bit in bits("win"):
        values = rounded(values)
        got, small = exchange(values, small, axis, bit)
        values = values + got
    values = values.astype(BF16)[None]
    for axis, bit in reversed(halvings):
        side = (lax.axis_index(axis) // bit) % 2
        other = partner(values, axis, bit)
        values = jnp.where(
            side == 0,
            jnp.concatenate([values, other]),
            jnp.concatenate([other, values]),
        )
    return values, partner(values, *last), small, edges


def body(
    atoms,
    cond,
    pair,
    struct_ids,
    cotangent,
    weights,
    vectors,
    pair_weight,
    stat_left,
    stat_right,
    root_left,
    root_right,
    stat_vectors,
    stat_pair,
    ema_weights,
    ema_vectors,
    ema_pair,
):
    rows = atoms.shape[1]
    messages = []
    for span in (slice(0, HALO), slice(rows - HALO, rows)):
        high = rounded(cond[:, span])
        rest = cond[:, span] - high
        parts = [atoms[:, span], high.astype(BF16), rest.astype(BF16)]
        messages.append(jnp.concatenate(parts, axis=0))
    first, last = messages
    low_msg, high_msg = passed(last, 1), passed(first, -1)
    bias, root = bias_table(pair, pair_weight.T)
    result, grad_atoms, rim_low, rim_high, send, keep = main_call(
        struct_ids, atoms, low_msg, high_msg, cotangent, bias, root, pair, cond, weights, vectors
    )
    edges = (passed(rim_high, 1), passed(rim_low, -1))
    own, other, small, (below, above) = summed(send, keep, edges)
    for span, part in ((slice(0, HALO), below), (slice(rows - HALO, rows), above)):
        edge = grad_atoms[:, span].astype(F32) + part.astype(F32)
        grad_atoms = grad_atoms.at[:, span].set(edge.astype(BF16))
    outs = list(
        update_call(
            own,
            other,
            small,
            stat_left,
            stat_right,
            root_left,
            root_right,
            weights,
            ema_weights,
            vectors,
            stat_vectors,
            ema_vectors,
            pair_weight.T,
            stat_pair.T,
            ema_pair.T,
        )
    )
    for at in (2, 8, 10, 13):
        outs[at] = outs[at].T
    return (result, grad_atoms, *outs)


def solution(mesh):
    placed = (
        P("samp", "win", None),
        P("samp", "win", None),
        P("samp", "win", None, None),
        P("samp"),
        P("samp", "win", None),
        P(),
        P(),
        P(),
        P(None, "win", None),
        P(None, "win", None),
        P(None, "win", None),
        P(),
        P(),
        P(),
        P(None, "win", None),
        P(),
        P(),
    )
    return jax.shard_map(
        body,
        mesh=mesh,
        in_specs=placed,
        out_specs=(
            P("samp", "win", None),
            P("samp", "win", None),
            P(None, "win", None),
            P(),
            P(),
            P(None, "win", None),
            P(None, "win", None),
            P(None, "win", None),
            P(None, "win", None),
            P(),
            P(),
            P(),
            P(),
            P(None, "win", None),
            P(),
            P(),
        ),
        check_vma=False,
    )
```

```python
import functools
import math

import jax
import jax.numpy as jnp
from jax import lax
from jax.experimental import pallas as pl
from jax.experimental.pallas import tpu as pltpu
from jax.sharding import PartitionSpec as P

HEADS = 4
FF = 256
QW = 32
HALO = 48
KW = 128
C = 128
PAIR = 16
NBLK = 17
UNROLL = 16
PACK = 2
BACK = 8
SLOTS = 3
TILE = 512

stat_decay = 0.5
ema_decay = 0.8
matrix_rate = 1.0
vector_rate = 0.2

F32 = jnp.float32
BF16 = jnp.bfloat16
LOG2E = math.log2(math.e)
FACTOR = 1.0 / math.sqrt(C // HEADS)
INVALID = -1000000000.0
VMEM_LIMIT = 60 * 1024 * 1024


def dot(left, right):
    return lax.dot_general(left, right, (((1,), (0,)), ((), ())), preferred_element_type=F32)


def dot_nt(left, right):
    return lax.dot_general(left, right, (((1,), (1,)), ((), ())), preferred_element_type=F32)


def dot_tn(left, right):
    return lax.dot_general(left, right, (((0,), (0,)), ((), ())), preferred_element_type=F32)


def layer_stats(values):
    center = values - jnp.mean(values, axis=-1, keepdims=True)
    inverse = lax.rsqrt(jnp.mean(center * center, axis=-1, keepdims=True) + 1e-05)
    return (center * inverse, inverse)


def layer_back(normed, inverse, grad_norm):
    return inverse * (
        grad_norm
        - jnp.mean(grad_norm, axis=-1, keepdims=True)
        - normed * jnp.mean(grad_norm * normed, axis=-1, keepdims=True)
    )


def pipeline(stages):
    waiting = list(stages)
    active = []
    while waiting or active:
        if waiting:
            active.append(waiting.pop(0))
        active = [item for item in active if next(item, active) is None]
        yield


def beside(items):
    active = list(items)
    while active:
        active = [item for item in active if next(item, active) is None]
        yield


def together(streams):
    count = len(streams[0])
    for at in range(count + len(streams) - 1):
        pipes = []
        for behind, phases in enumerate(streams):
            if 0 <= at - behind < count:
                depth, stages = phases[at - behind]
                pipes.append([pipeline(stages), depth + len(stages), 0])
        longest = max(length for _, length, _ in pipes)
        for tick in range(1, longest + 1):
            for item in pipes:
                while item[2] * longest < tick * item[1]:
                    item[2] += 1
                    next(item[0], None)
        for pipe, _, _ in pipes:
            for _ in pipe:
                pass


def rows_sum(values):
    return jnp.sum(values, axis=0, keepdims=True)


def bias_kernel(pair_ref, pw_ref, bias_ref, root_ref, expand, flat):
    group = pl.program_id(1)
    per_step = bias_ref.shape[1]
    atoms = pl.num_programs(1) * per_step * QW
    span = QW * PAIR

    @pl.when((pl.program_id(0) == 0) & (group == 0))
    def _():
        rows = lax.broadcasted_iota(jnp.int32, (span, C), 0) // PAIR
        lanes = lax.broadcasted_iota(jnp.int32, (span, C), 1) % QW
        wide = lax.dot_general(
            pw_ref[...],
            head_lanes(),
            (((0,), (0,)), ((), ())),
            precision=lax.Precision.HIGHEST,
            preferred_element_type=F32,
        )
        weight = wide - jnp.mean(wide, axis=0, keepdims=True)
        full = jnp.where(rows == lanes, jnp.concatenate([weight] * QW, axis=0), 0.0)
        high = full.astype(BF16)
        expand[:, :C] = high
        expand[:, C:] = (full - high.astype(F32)).astype(BF16)

    def one(w):
        low = pair_ref[0, w * QW : w * QW + QW].reshape(span, KW)
        flat[w * span : w * span + span] = low.astype(F32)
        yield
        out = dot_tn(low, expand[...])
        roots = []
        for part in range(QW // 8):
            start = w * span + part * 8 * PAIR
            channels = [flat[pl.ds(start + c, 8, stride=PAIR), :] for c in range(PAIR)]
            mean = sum(channels[1:], channels[0]) * (1.0 / PAIR)
            center = [channel - mean for channel in channels]
            squares = [value * value for value in center]
            spread = sum(squares[1:], squares[0]) * (1.0 / PAIR)
            roots.append(lax.rsqrt(spread + 1e-05))
        yield
        root = jnp.concatenate(roots * HEADS, axis=0).T
        value = (out[:, :C] + out[:, C:]) * (root * LOG2E)
        start = lax.axis_index("win") * atoms + (group * per_step + w) * QW - HALO
        position = start + lax.broadcasted_iota(jnp.int32, (KW, C), 0)
        valid = (position >= 0) & (position < lax.axis_size("win") * atoms)
        bias_ref[0, w] = jnp.where(valid, value, INVALID * LOG2E)
        root_ref[0, w] = root.astype(BF16)

    for _ in pipeline([one(w) for w in range(per_step)]):
        pass


def head_lanes():
    rows = lax.broadcasted_iota(jnp.int32, (HEADS, C), 0)
    lanes = lax.broadcasted_iota(jnp.int32, (HEADS, C), 1) // QW
    return jnp.where(rows == lanes, 1.0, 0.0)


def bias_table(pair, turned_weight):
    structs, atoms = pair.shape[:2]
    count = min(8, atoms // QW)
    rows = count * QW
    table = pl.BlockSpec((1, count, KW, C), lambda s, i: (s, i, 0, 0))
    return pl.pallas_call(
        bias_kernel,
        grid=(structs, atoms // rows),
        in_specs=[
            pl.BlockSpec((1, rows, PAIR, KW), lambda s, i: (s, i, 0, 0)),
            pl.BlockSpec((HEADS, PAIR), lambda s, i: (0, 0)),
        ],
        out_specs=[table, table],
        scratch_shapes=[
            pltpu.VMEM((QW * PAIR, 2 * C), BF16),
            pltpu.VMEM((rows * PAIR, KW), F32),
        ],
        out_shape=[
            jax.ShapeDtypeStruct((structs, atoms // QW, KW, C), F32),
            jax.ShapeDtypeStruct((structs, atoms // QW, KW, C), BF16),
        ],
        compiler_params=pltpu.CompilerParams(vmem_limit_bytes=VMEM_LIMIT),
        cost_estimate=pl.CostEstimate(flops=10**9, bytes_accessed=15 * 2**20, transcendentals=0),
        name="pair_bias",
    )(pair, turned_weight)


def main_kernel(
    ids_ref,
    x_ref,
    xlo_ref,
    xhi_ref,
    g_ref,
    bias_hbm,
    root_hbm,
    pair_ref,
    cond_ref,
    clo_ref,
    chi_ref,
    w_ref,
    vec_ref,
    out_ref,
    grad_ref,
    rlo_ref,
    rhi_ref,
    send_ref,
    keep_ref,
    packed_ref,
    bias_ref,
    root_ref,
    table_sem,
    dbias_ref,
    dvec_ref,
    pair_scr,
    pair_sem,
    pair_total,
    wq,
    w6,
    win,
    wo,
    wqt,
    w6t,
    wint,
    wot,
    wc1,
    wc2,
    mask,
    t_s1,
    t_h1,
    t_hs,
    t_hh,
    t_g1,
    t_s2,
    t_h2,
    t_g2,
    a_s1,
    a_h1,
    a_g1,
    a_s2,
    a_h2,
    a_g2,
    a_hs,
    a_hh,
    nh_scr,
    ih_scr,
    ah_scr,
    k_scr,
    v_scr,
    q_scr,
    gate_scr,
    ada_scr,
    n1_scr,
    inv_scr,
    o_scr,
    p_scr,
    do_scr,
    dd_scr,
    d4_scr,
    dk_scr,
    dv_scr,
    dx_scr,
):
    step = pl.program_id(0)
    structs, atoms, _ = cond_ref.shape
    windows = atoms // QW
    unroll = min(UNROLL, windows)
    tile = min(TILE, atoms)
    tiles = atoms // tile
    s = [lax.rem(ids_ref[step * PACK + b], structs) for b in range(PACK)]

    def cond_rows(source):
        normed, _ = layer_stats(source)
        one = (normed * vec_ref[0:1]).astype(BF16)
        two = (normed * vec_ref[4:5]).astype(BF16)
        return normed, one, two

    def block(at):
        return packed_ref.at[at * C : at * C + C]

    def joined(ref, st):
        return ref[st].astype(F32) + ref[structs + st].astype(F32)

    bias_copy = pltpu.make_async_copy(bias_hbm, bias_ref, table_sem.at[0])
    root_copy = pltpu.make_async_copy(root_hbm, root_ref, table_sem.at[1])
    chunk = min(8, windows)
    chunks = structs * windows // chunk

    def pair_copy(at):
        st, first = divmod(at * chunk, windows)
        return pltpu.make_async_copy(
            pair_ref.at[st, pl.ds(first * QW, chunk * QW)],
            pair_scr.at[at % SLOTS],
            pair_sem.at[at % SLOTS],
        )

    @pl.when(step == 0)
    def _():
        bias_copy.start()
        root_copy.start()
        for at in range(min(SLOTS, chunks)):
            pair_copy(at).start()

        def low(b):
            return w_ref[b].astype(BF16)

        for at, b in enumerate((2, 5, 3, 4)):
            wq[:, at * C : at * C + C] = low(b)
        w6[...] = low(6)
        for at in range(4):
            win[:, at * C : at * C + C] = low(11 + at)
        for at in range(2):
            wo[at * C : at * C + C, :] = low(15 + at)
        for source, turned in ((wq, wqt), (w6, w6t), (win, wint), (wo, wot)):
            turned[...] = source[...].T
        for at, b in enumerate((0, 1, 7)):
            wc1[:, at * C : at * C + C] = low(b)
        for at, b in enumerate((8, 9, 10)):
            wc2[:, at * C : at * C + C] = low(b)
        rows_head = lax.broadcasted_iota(jnp.int32, (C, C), 0) // QW
        lane_head = lax.broadcasted_iota(jnp.int32, (C, C), 1) // (C // HEADS)
        mask[...] = jnp.where(rows_head == lane_head, 1.0, 0.0).astype(BF16)
        for acc in (a_s1, a_h1, a_g1, a_s2, a_h2, a_g2, a_hs, a_hh, packed_ref, dvec_ref):
            acc[...] = jnp.zeros_like(acc)
        dbias_ref[...] = jnp.zeros_like(dbias_ref)
        pair_total[...] = jnp.zeros_like(pair_total)

        def table(st, i):
            rows = pl.ds(i * tile, tile)
            _, one, two = cond_rows(cond_ref[st, rows])
            yield
            first = dot(one, wc1[...])
            second = dot(two, wc2[...])
            yield
            t_s1[st, rows] = jax.nn.sigmoid(first[:, :C] + vec_ref[1:2])
            t_h1[st, rows] = first[:, C : 2 * C]
            t_g1[st, rows] = jax.nn.sigmoid(first[:, 2 * C :] + vec_ref[3:4])
            t_s2[st, rows] = jax.nn.sigmoid(second[:, :C] + vec_ref[5:6])
            t_h2[st, rows] = second[:, C : 2 * C]
            t_g2[st, rows] = jax.nn.sigmoid(second[:, 2 * C :] + vec_ref[6:7])

        def table_halo(st):
            source = jnp.concatenate([joined(clo_ref, st), joined(chi_ref, st)], axis=0)
            _, one, _ = cond_rows(source)
            yield
            first = dot(one, wc1[:, : 2 * C])
            yield
            t_hs[st] = jax.nn.sigmoid(first[:, :C] + vec_ref[1:2])
            t_hh[st] = first[:, C:]

        items = [table_halo(st) for st in range(structs)]
        items += [table(st, i) for st in range(structs) for i in range(tiles)]
        for _ in pipeline(items):
            pass

    @pl.when(step == 0)
    def _():
        bias_copy.wait()

    def project(b, i):
        start = i * tile
        rows = pl.ds(start, tile)
        pad = pl.ds(start + HALO, tile)
        normed, inverse = layer_stats(x_ref[b, rows].astype(F32))
        n1_scr[b, rows] = normed
        inv_scr[b, rows] = jnp.broadcast_to(inverse, (tile, C))
        ada = (t_s1[s[b], rows] * normed + t_h1[s[b], rows]).astype(BF16)
        ada_scr[b, rows] = ada
        yield
        out = dot(ada, wq[...])
        yield
        q_scr[b, rows] = (out[:, :C] + vec_ref[2:3]).astype(BF16)
        gate_scr[b, rows] = jax.nn.sigmoid(out[:, C : 2 * C])
        k_scr[b, pad] = out[:, 2 * C : 3 * C].astype(BF16)
        v_scr[b, pad] = out[:, 3 * C :].astype(BF16)

    def project_halo(b):
        halo = jnp.concatenate([xlo_ref[b], xhi_ref[b]], axis=0).astype(F32)
        normed, inverse = layer_stats(halo)
        ada = (t_hs[s[b]] * normed + t_hh[s[b]]).astype(BF16)
        nh_scr[b] = normed
        ih_scr[b] = jnp.broadcast_to(inverse, (2 * HALO, C))
        ah_scr[b] = ada
        yield
        out = dot(ada, wq[:, 2 * C :])
        yield
        k_scr[b, :HALO] = out[:HALO, :C].astype(BF16)
        v_scr[b, :HALO] = out[:HALO, C:].astype(BF16)
        k_scr[b, HALO + atoms :] = out[HALO:, :C].astype(BF16)
        v_scr[b, HALO + atoms :] = out[HALO:, C:].astype(BF16)

    lane_head = lax.broadcasted_iota(jnp.int32, (QW, C), 1) // (C // HEADS)

    def spread(rows):
        return jnp.concatenate([rows] * HEADS, axis=0) * mask[...]

    def gathered(full):
        parts = [full[h * QW : h * QW + QW] for h in range(HEADS)]
        last = parts[HEADS - 1]
        for h in range(HEADS - 2, -1, -1):
            last = jnp.where(lane_head == h, parts[h], last)
        return last

    def attend(b, group):
        scores = []
        for w in group:
            queries = spread(q_scr[b, w * QW : w * QW + QW])
            scores.append(dot(k_scr[b, w * QW : w * QW + KW], queries.T))
        yield
        probs = []
        for u, w in enumerate(group):
            value = scores[u] * (FACTOR * LOG2E) + bias_ref[s[b], w]
            exps = jnp.exp2(value - jnp.max(value, axis=0, keepdims=True))
            prob = (exps * (1.0 / rows_sum(exps))).astype(BF16)
            p_scr[b, w] = prob
            probs.append(prob)
        yield
        fulls = [dot_tn(probs[u], v_scr[b, w * QW : w * QW + KW]) for u, w in enumerate(group)]
        yield
        for u, w in enumerate(group):
            o_scr[b, w * QW : w * QW + QW] = gathered(fulls[u])

    def middle(b, i):
        rows = pl.ds(i * tile, tile)
        gate = gate_scr[b, rows]
        mixed = o_scr[b, rows]
        y = (gate * mixed).astype(BF16)
        yield
        attn = dot(y, w6[...])
        yield
        gate_one = t_g1[s[b], rows]
        x1 = x_ref[b, rows].astype(F32) + gate_one * attn
        normed, inverse = layer_stats(x1)
        scale_two = t_s2[s[b], rows]
        ada = (scale_two * normed + t_h2[s[b], rows]).astype(BF16)
        yield
        expand = dot(ada, win[...])
        yield
        a = expand[:, :FF]
        up = expand[:, FF:]
        sig = jax.nn.sigmoid(a)
        silu = a * sig
        hid = (silu * up).astype(BF16)
        yield
        ff = dot(hid, wo[...])
        gate_two = t_g2[s[b], rows]
        g = g_ref[b, rows].astype(F32)
        dff = (g * gate_two).astype(BF16)
        dhid = dot(dff, wot[...])
        yield
        out_ref[b, rows] = (x1 + gate_two * ff).astype(BF16)
        a_g2[s[b], rows] += g * ff
        da = (dhid * up * (sig + silu * (1.0 - sig))).astype(BF16)
        db = (dhid * silu).astype(BF16)
        dab = jnp.concatenate([da, db], axis=1)
        yield
        dada = dot(dab, wint[...])
        yield
        a_s2[s[b], rows] += dada * normed
        a_h2[s[b], rows] += dada
        dx1 = g + layer_back(normed, inverse, dada * scale_two)
        dx_scr[b, rows] = dx1
        a_g1[s[b], rows] += dx1 * attn
        dattn = (dx1 * gate_one).astype(BF16)
        yield
        dy = dot(dattn, w6t[...])
        dwo = dot_tn(dff, hid)
        dwin = dot_tn(ada, dab)
        dw6 = dot_tn(y, dattn)
        yield
        do = (dy * gate).astype(BF16)
        do_scr[b, rows] = do
        dd_scr[b, rows] = (do.astype(F32) * mixed * -1.0).astype(BF16)
        d4_scr[b, rows, C : 2 * C] = (dy * mixed * gate * (1.0 - gate)).astype(BF16)
        block(15)[...] += dwo[:, :C]
        block(16)[...] += dwo[:, C:]
        for at in range(4):
            block(11 + at)[...] += dwin[:, at * C : at * C + C]
        block(6)[...] += dw6

    ones = jnp.ones((KW, C), BF16)

    def attend_back(b, group):
        diffs = []
        spreads = []
        for w in group:
            dox = spread(do_scr[b, w * QW : w * QW + QW])
            ddx = spread(dd_scr[b, w * QW : w * QW + QW])
            values = jnp.concatenate([v_scr[b, w * QW : w * QW + KW], ones], axis=1)
            diffs.append(dot(values, jnp.concatenate([dox.T, ddx.T], axis=0)))
            spreads.append(dox)
        yield
        grads = []
        for u, w in enumerate(group):
            ds = p_scr[b, w].astype(F32) * diffs[u]
            dbias_ref[s[b], w] += ds
            grads.append(ds.astype(BF16))
        yield
        fulls = []
        dks = []
        dvs = []
        for u, w in enumerate(group):
            fulls.append(dot_tn(grads[u], k_scr[b, w * QW : w * QW + KW]))
            dks.append(dot(grads[u], spread(q_scr[b, w * QW : w * QW + QW])))
            dvs.append(dot(p_scr[b, w], spreads[u]))
        yield
        for u, w in enumerate(group):
            dq = gathered(fulls[u]) * FACTOR
            dvec_ref[2] += jnp.sum(dq.reshape(QW // 8, 8, C), axis=0)
            d4_scr[b, w * QW : w * QW + QW, :C] = dq.astype(BF16)
            seen = KW - QW if w else 0
            for scr, part in ((dk_scr, dks[u]), (dv_scr, dvs[u])):
                if seen:
                    scr[b, w * QW : w * QW + seen] += part[:seen]
                scr[b, w * QW + seen : w * QW + KW] = part[seen:]

    def finish(b, i):
        start = i * tile
        rows = pl.ds(start, tile)
        pad = pl.ds(start + HALO, tile)
        d4_scr[b, rows, 2 * C : 3 * C] = (dk_scr[b, pad] * FACTOR).astype(BF16)
        d4_scr[b, rows, 3 * C :] = dv_scr[b, pad].astype(BF16)
        yield
        d4 = d4_scr[b, rows]
        dwq = dot_tn(ada_scr[b, rows], d4)
        dada = dot(d4, wqt[...])
        yield
        for at, which in enumerate((2, 5, 3, 4)):
            block(which)[...] += dwq[:, at * C : at * C + C]
        normed = n1_scr[b, rows]
        a_s1[s[b], rows] += dada * normed
        a_h1[s[b], rows] += dada
        grad = dx_scr[b, rows] + layer_back(normed, inv_scr[b, rows], dada * t_s1[s[b], rows])
        dx_scr[b, rows] = grad
        grad_ref[b, rows] = grad.astype(BF16)

    def finish_halo(b):
        spans = (slice(0, HALO), slice(HALO + atoms, None))
        dk = jnp.concatenate([dk_scr[b, span] for span in spans], axis=0) * FACTOR
        dv = jnp.concatenate([dv_scr[b, span] for span in spans], axis=0)
        dkv = jnp.concatenate([dk.astype(BF16), dv.astype(BF16)], axis=1)
        yield
        dw = dot_tn(ah_scr[b], dkv)
        dada = dot(dkv, wqt[2 * C :])
        yield
        block(3)[...] += dw[:, :C]
        block(4)[...] += dw[:, C:]
        normed = nh_scr[b]
        a_hs[s[b]] += dada * normed
        a_hh[s[b]] += dada
        rim = layer_back(normed, ih_scr[b], dada * t_hs[s[b]]).astype(BF16)
        rlo_ref[b] = rim[:HALO]
        rhi_ref[b] = rim[HALO:]

    groups = [tuple(range(at, at + unroll)) for at in range(0, windows, unroll)]
    width = min(BACK, windows)
    backs = [tuple(range(at, at + width)) for at in range(0, windows, width)]

    def phases(b):
        return [
            (3, [project_halo(b)] + [project(b, i) for i in range(tiles)]),
            (4, [attend(b, group) for group in groups]),
            (11, [middle(b, i) for i in range(tiles)]),
            (4, [attend_back(b, group) for group in backs]),
            (3, [finish_halo(b)] + [finish(b, i) for i in range(tiles)]),
        ]

    together([phases(b) for b in range(PACK)])

    @pl.when(step == pl.num_programs(0) - 1)
    def _():
        for at in (15, 16):
            block(at)[...] = block(at)[...].T

        def apply(source, normed, parts, weight, blocks, gain):
            joined_parts = jnp.concatenate(parts, axis=1)
            grads = dot_tn(source, joined_parts)
            back = dot_nt(joined_parts, weight) * normed
            for at, which in enumerate(blocks):
                block(which)[...] += grads[:, at * C : at * C + C]
            dvec_ref[gain] += jnp.sum(back.reshape(-1, 8, C), axis=0)

        def bias_sum(at, part):
            dvec_ref[at] += jnp.sum(part.astype(F32).reshape(-1, 8, C), axis=0)

        def pre(total, gate):
            return (total * gate * (1.0 - gate)).astype(BF16)

        def conditioning(st, i):
            rows = pl.ds(i * tile, tile)
            normed, one, two = cond_rows(cond_ref[st, rows])
            first = [
                pre(a_s1[st, rows], t_s1[st, rows]),
                a_h1[st, rows].astype(BF16),
                pre(a_g1[st, rows], t_g1[st, rows]),
            ]
            second = [
                pre(a_s2[st, rows], t_s2[st, rows]),
                a_h2[st, rows].astype(BF16),
                pre(a_g2[st, rows], t_g2[st, rows]),
            ]
            yield
            for at, part in ((1, first[0]), (3, first[2]), (5, second[0]), (6, second[2])):
                bias_sum(at, part)
            apply(one, normed, first, wc1[...], (0, 1, 7), 0)
            apply(two, normed, second, wc2[...], (8, 9, 10), 4)

        def conditioning_halo(st):
            source = jnp.concatenate([joined(clo_ref, st), joined(chi_ref, st)], axis=0)
            normed, one, _ = cond_rows(source)
            parts = [pre(a_hs[st], t_hs[st]), a_hh[st].astype(BF16)]
            yield
            bias_sum(1, parts[0])
            apply(one, normed, parts, wc1[:, : 2 * C], (0, 1), 0)

        items = [conditioning_halo(st) for st in range(structs)]
        items += [conditioning(st, i) for st in range(structs) for i in range(tiles)]
        for _ in pipeline(items):
            pass

        root_copy.wait()
        for at in range(chunks):
            pair_copy(at).wait()
            st, first = divmod(at * chunk, windows)
            lefts = []
            rights = []
            for w in range(chunk):
                lefts.append(
                    pair_scr[at % SLOTS, w * QW : w * QW + QW].reshape(QW * PAIR, KW)
                )
                grad = dbias_ref[st, first + w] * root_ref[st, first + w].astype(F32)
                rights.append(grad.astype(BF16))
            left = jnp.concatenate(lefts, axis=1)
            pair_total[...] += dot(left, jnp.concatenate(rights, axis=0))
            if at + SLOTS < chunks:
                pair_copy(at + SLOTS).start()
        lanes = lax.broadcasted_iota(jnp.int32, (PAIR, C), 1) % QW
        acc = jnp.zeros((PAIR, C), F32)
        for q in range(QW):
            acc = acc + jnp.where(lanes == q, pair_total[q * PAIR : q * PAIR + PAIR], 0.0)
        half = NBLK * C // 2
        side = (lax.axis_index("samp") // 2) % 2
        send = packed_ref[pl.ds(pl.multiple_of((1 - side) * half, 64), half)]
        keep_ref[...] = packed_ref[pl.ds(pl.multiple_of(side * half, 64), half)]
        small = jnp.concatenate(
            [rows_sum(dvec_ref[at]) for at in range(7)]
            + [jnp.zeros((1, C), F32), acc - jnp.mean(acc, axis=0, keepdims=True)],
            axis=0,
        )
        high, low = split_low(small)
        send_ref[:half] = send.astype(BF16)
        send_ref[half:] = jnp.concatenate([high, low], axis=0)


def main_call(
    ids, atoms, low_msg, high_msg, cotangent, bias, root, pair, cond, weights, vectors
):
    samples, rows, _ = atoms.shape
    structs = cond.shape[0]
    windows = rows // QW
    padded = rows + 2 * HALO

    def per_sample(*shape):
        zeros = (0,) * len(shape)
        return pl.BlockSpec((PACK,) + shape, lambda i, _: (i,) + zeros)

    def whole(*shape):
        zeros = (0,) * len(shape)
        return pl.BlockSpec(shape, lambda i, _: zeros, pipeline_mode=pl.Buffered(1))

    def table(count=rows):
        return pltpu.VMEM((structs, count, C), F32)

    cond_part = pl.BlockSpec((2 * structs, HALO, C), lambda i, _: (samples // (2 * structs), 0, 0))
    shape = jax.ShapeDtypeStruct
    return pl.pallas_call(
        main_kernel,
        grid_spec=pltpu.PrefetchScalarGridSpec(
            num_scalar_prefetch=1,
            grid=(samples // PACK,),
            in_specs=[
                per_sample(rows, C),
                per_sample(HALO, C),
                per_sample(HALO, C),
                per_sample(rows, C),
                pl.BlockSpec(memory_space=pl.ANY),
                pl.BlockSpec(memory_space=pl.ANY),
                pl.BlockSpec(memory_space=pl.ANY),
                whole(structs, rows, C),
                cond_part,
                cond_part,
                whole(NBLK, C, C),
                whole(7, C),
            ],
            out_specs=[
                per_sample(rows, C),
                per_sample(rows, C),
                per_sample(HALO, C),
                per_sample(HALO, C),
                whole(NBLK * C // 2 + 2 * (8 + PAIR), C),
                whole(NBLK * C // 2, C),
            ],
            scratch_shapes=[
                pltpu.VMEM((NBLK * C, C), F32),
                pltpu.VMEM((structs, windows, KW, C), F32),
                pltpu.VMEM((structs, windows, KW, C), BF16),
                pltpu.SemaphoreType.DMA((2,)),
                pltpu.VMEM((structs, windows, KW, C), F32),
                pltpu.VMEM((7, 8, C), F32),
                pltpu.VMEM((SLOTS, min(rows, 8 * QW), PAIR, KW), BF16),
                pltpu.SemaphoreType.DMA((SLOTS,)),
                pltpu.VMEM((QW * PAIR, C), F32),
                pltpu.VMEM((C, 4 * C), BF16),
                pltpu.VMEM((C, C), BF16),
                pltpu.VMEM((C, 2 * FF), BF16),
                pltpu.VMEM((FF, C), BF16),
                pltpu.VMEM((4 * C, C), BF16),
                pltpu.VMEM((C, C), BF16),
                pltpu.VMEM((2 * FF, C), BF16),
                pltpu.VMEM((C, FF), BF16),
                pltpu.VMEM((C, 3 * C), BF16),
                pltpu.VMEM((C, 3 * C), BF16),
                pltpu.VMEM((C, C), BF16),
                table(),
                table(),
                table(2 * HALO),
                table(2 * HALO),
                table(),
                table(),
                table(),
                table(),
                table(),
                table(),
                table(),
                table(),
                table(),
                table(),
                table(2 * HALO),
                table(2 * HALO),
                pltpu.VMEM((PACK, 2 * HALO, C), F32),
                pltpu.VMEM((PACK, 2 * HALO, C), F32),
                pltpu.VMEM((PACK, 2 * HALO, C), BF16),
                pltpu.VMEM((PACK, padded, C), BF16),
                pltpu.VMEM((PACK, padded, C), BF16),
                pltpu.VMEM((PACK, rows, C), BF16),
                pltpu.VMEM((PACK, rows, C), F32),
                pltpu.VMEM((PACK, rows, C), BF16),
                pltpu.VMEM((PACK, rows, C), F32),
                pltpu.VMEM((PACK, rows, C), F32),
                pltpu.VMEM((PACK, rows, C), F32),
                pltpu.VMEM((PACK, windows, KW, C), BF16),
                pltpu.VMEM((PACK, rows, C), BF16),
                pltpu.VMEM((PACK, rows, C), BF16),
                pltpu.VMEM((PACK, rows, 4 * C), BF16),
                pltpu.VMEM((PACK, padded, C), F32),
                pltpu.VMEM((PACK, padded, C), F32),
                pltpu.VMEM((PACK, rows, C), F32),
            ],
        ),
        out_shape=[
            shape((samples, rows, C), BF16),
            shape((samples, rows, C), BF16),
            shape((samples, HALO, C), BF16),
            shape((samples, HALO, C), BF16),
            shape((NBLK * C // 2 + 2 * (8 + PAIR), C), BF16),
            shape((NBLK * C // 2, C), F32),
        ],
        compiler_params=pltpu.CompilerParams(vmem_limit_bytes=VMEM_LIMIT),
        name="block",
    )(
        ids,
        atoms,
        low_msg,
        high_msg,
        cotangent,
        bias,
        root,
        pair,
        cond,
        low_msg,
        high_msg,
        weights,
        vectors,
    )


def split_low(values):
    high = values.astype(BF16)
    return high, (values - high.astype(F32)).astype(BF16)


def update_kernel(
    own_ref,
    other_ref,
    small_ref,
    sl_ref,
    sr_ref,
    rl_ref,
    rr_ref,
    w_ref,
    ew_ref,
    vec_ref,
    sv_ref,
    ev_ref,
    pw_ref,
    sp_ref,
    ep_ref,
    rows_ref,
    tv_ref,
    tp_ref,
    left_ref,
    right_ref,
    neww_ref,
    low_ref,
    newv_ref,
    newp_ref,
    nsv_ref,
    nsp_ref,
    neww_ema_ref,
    newv_ema_ref,
    newp_ema_ref,
    turned,
    total_ref,
):
    chunks, size, _ = own_ref.shape
    side = lax.axis_index("samp") % 2
    for at in range(chunks):
        for ref, place in ((own_ref, side), (other_ref, 1 - side)):
            start = pl.multiple_of((2 * at + place) * size, 16)
            total_ref[pl.ds(start, size)] = ref[at].astype(F32)
    count = sl_ref.shape[1]
    own = pl.ds(lax.axis_index("win") * count, count)

    def product(parts, right):
        high, low = split_low(right)
        lefts = [split_low(part) for part in parts]
        tall = jnp.concatenate([a for a, _ in lefts] + [b for _, b in lefts], axis=0)
        size = tall.shape[0] // 2
        first = dot(tall, high)
        return first[:size] + first[size:] + dot(tall[:size], low)

    def one(b):
        block = total_ref[b * C : b * C + C]
        turned[b] = block.T
        pad = jnp.zeros((16 - count, C), F32) if count < 16 else None

        def rows(values):
            return values if pad is None else jnp.concatenate([values, pad], axis=0)

        own_rows = total_ref[pl.ds(b * C + lax.axis_index("win") * count, count)]
        rows_ref[b] = own_rows
        yield
        own_cols = turned[b, own]
        both = product([rows(own_cols), rows(rl_ref[b])], block)
        left = product([rows(own_rows)], turned[b])
        size = max(count, 16)
        yield
        step = product([both[size:]], rr_ref[b])
        right_ref[b] = stat_decay * sr_ref[b] + (1.0 - stat_decay) * both[:count]
        left_ref[b] = stat_decay * sl_ref[b] + (1.0 - stat_decay) * left[:count]
        yield
        new = w_ref[b, own] - matrix_rate * step[:count]
        neww_ref[b] = new
        low_ref[b] = new.astype(BF16)
        neww_ema_ref[b] = ema_decay * ew_ref[b] + (1.0 - ema_decay) * new

    for _ in pipeline([beside([one(b) for b in range(at, min(at + 6, NBLK))]) for at in range(0, NBLK, 6)]):
        pass
    sums = small_ref[8:]
    pair_total = lax.dot_general(
        head_lanes(),
        sums,
        (((1,), (1,)), ((), ())),
        precision=lax.Precision.HIGHEST,
        preferred_element_type=F32,
    )
    for total, param, stat, ema, out, new_ref, stat_ref, ema_ref in (
        (small_ref[:7], vec_ref, sv_ref, ev_ref, tv_ref, newv_ref, nsv_ref, newv_ema_ref),
        (pair_total, pw_ref, sp_ref, ep_ref, tp_ref, newp_ref, nsp_ref, newp_ema_ref),
    ):
        out[...] = total
        new_stat = stat_decay * stat[...] + (1.0 - stat_decay) * total * total
        stat_ref[...] = new_stat
        new = param[...] - vector_rate * total * lax.rsqrt(new_stat)
        new_ref[...] = new
        ema_ref[...] = ema_decay * ema[...] + (1.0 - ema_decay) * new


def update_call(*args):
    rows = args[3].shape
    vec = args[9].shape
    pw = args[12].shape
    full = pl.BlockSpec(memory_space=pltpu.VMEM)

    def shape(dims, kind=F32):
        return jax.ShapeDtypeStruct(dims, kind)

    def out_block(dims):
        zeros = (0,) * len(dims)
        return pl.BlockSpec(dims, lambda i: zeros)

    outs = [rows, vec, pw, rows, rows, rows, rows, vec, pw, vec, pw, rows, vec, pw]
    return pl.pallas_call(
        update_kernel,
        grid=(1,),
        in_specs=[full] * len(args),
        out_specs=[out_block(dims) for dims in outs],
        out_shape=[
            shape(dims, BF16 if at == 6 else F32) for at, dims in enumerate(outs)
        ],
        scratch_shapes=[pltpu.VMEM((NBLK, C, C), F32), pltpu.VMEM((NBLK * C, C), F32)],
        compiler_params=pltpu.CompilerParams(vmem_limit_bytes=VMEM_LIMIT),
        name="update",
    )(*args)


def passed(shard, by):
    devices = lax.axis_size("win")
    pairs = [(i, i + by) for i in range(devices) if 0 <= i + by < devices]
    return lax.ppermute(shard, "win", pairs)


def rounded(values):
    return lax.reduce_precision(values, exponent_bits=8, mantissa_bits=7)


def partner(values, axis, bit):
    devices = lax.axis_size(axis)
    return lax.ppermute(values, axis, [(i, i ^ bit) for i in range(devices)])


def bits(axis):
    devices = lax.axis_size(axis)
    return [(axis, 1 << at) for at in range((devices - 1).bit_length())]


def exchange(part, small, axis, bit):
    size = part.shape[0]
    high = rounded(small)
    rest = rounded(small - high)
    message = [part.astype(BF16), high.astype(BF16), rest.astype(BF16)]
    got = partner(jnp.concatenate(message, axis=0), axis, bit)
    return got[:size].astype(F32), joined_terms(got[size:]) + (high + rest)


def joined_terms(terms):
    count = terms.shape[0] // 2
    wide = terms.astype(F32)
    return wide[:count] + wide[count:]


def summed(send, keep, edges):
    last, *halvings = bits("samp")
    size = keep.shape[0]
    for at, (axis, bit) in enumerate(halvings):
        if at == 0:
            got, edges = lax.optimization_barrier((partner(send, axis, bit), edges))
            values = keep + got[:size].astype(F32)
            small = joined_terms(send[size:]) + joined_terms(got[size:])
        else:
            side = (lax.axis_index(axis) // bit) % 2
            size = values.shape[0] // 2
            kept = lax.dynamic_slice_in_dim(values, side * size, size)
            part = lax.dynamic_slice_in_dim(values, (1 - side) * size, size)
            got, small = exchange(part, small, axis, bit)
            values = kept + got
    axis, bit = last
    side = (lax.axis_index(axis) // bit) % 2
    size = values.shape[0] // 2
    kept = lax.dynamic_slice_in_dim(values, side * size, size)
    part = lax.dynamic_slice_in_dim(values, (1 - side) * size, size)
    got = partner(jnp.concatenate([part, small], axis=0), axis, bit)
    values = kept + got[:size]
    small = small + got[size:]
    for axis, bit in bits("win"):
        values = rounded(values)
        got, small = exchange(values, small, axis, bit)
        values = values + got
    values = values.astype(BF16)[None]
    for axis, bit in reversed(halvings):
        side = (lax.axis_index(axis) // bit) % 2
        other = partner(values, axis, bit)
        values = jnp.where(
            side == 0,
            jnp.concatenate([values, other]),
            jnp.concatenate([other, values]),
        )
    return values, partner(values, *last), small, edges


def body(
    atoms,
    cond,
    pair,
    struct_ids,
    cotangent,
    weights,
    vectors,
    pair_weight,
    stat_left,
    stat_right,
    root_left,
    root_right,
    stat_vectors,
    stat_pair,
    ema_weights,
    ema_vectors,
    ema_pair,
):
    rows = atoms.shape[1]
    messages = []
    for span in (slice(0, HALO), slice(rows - HALO, rows)):
        high = rounded(cond[:, span])
        rest = cond[:, span] - high
        parts = [atoms[:, span], high.astype(BF16), rest.astype(BF16)]
        messages.append(jnp.concatenate(parts, axis=0))
    first, last = messages
    low_msg, high_msg = passed(last, 1), passed(first, -1)
    bias, root = bias_table(pair, pair_weight.T)
    result, grad_atoms, rim_low, rim_high, send, keep = main_call(
        struct_ids, atoms, low_msg, high_msg, cotangent, bias, root, pair, cond, weights, vectors
    )
    edges = (passed(rim_high, 1), passed(rim_low, -1))
    own, other, small, (below, above) = summed(send, keep, edges)
    for span, part in ((slice(0, HALO), below), (slice(rows - HALO, rows), above)):
        edge = grad_atoms[:, span].astype(F32) + part.astype(F32)
        grad_atoms = grad_atoms.at[:, span].set(edge.astype(BF16))
    outs = list(
        update_call(
            own,
            other,
            small,
            stat_left,
            stat_right,
            root_left,
            root_right,
            weights,
            ema_weights,
            vectors,
            stat_vectors,
            ema_vectors,
            pair_weight.T,
            stat_pair.T,
            ema_pair.T,
        )
    )
    for at in (2, 8, 10, 13):
        outs[at] = outs[at].T
    return (result, grad_atoms, *outs)


def solution(mesh):
    placed = (
        P("samp", "win", None),
        P("samp", "win", None),
        P("samp", "win", None, None),
        P("samp"),
        P("samp", "win", None),
        P(),
        P(),
        P(),
        P(None, "win", None),
        P(None, "win", None),
        P(None, "win", None),
        P(),
        P(),
        P(),
        P(None, "win", None),
        P(),
        P(),
    )
    return jax.shard_map(
        body,
        mesh=mesh,
        in_specs=placed,
        out_specs=(
            P("samp", "win", None),
            P("samp", "win", None),
            P(None, "win", None),
            P(),
            P(),
            P(None, "win", None),
            P(None, "win", None),
            P(None, "win", None),
            P(None, "win", None),
            P(),
            P(),
            P(),
            P(),
            P(None, "win", None),
            P(),
            P(),
        ),
        check_vma=False,
    )
```

```python
import functools
import math

import jax
import jax.numpy as jnp
from jax import lax
from jax.experimental import pallas as pl
from jax.experimental.pallas import tpu as pltpu
from jax.sharding import PartitionSpec as P

HEADS = 4
FF = 256
QW = 32
HALO = 48
KW = 128
C = 128
PAIR = 16
NBLK = 17
UNROLL = 16
PACK = 2
BACK = 8
SLOTS = 3
TILE = 512

stat_decay = 0.5
ema_decay = 0.8
matrix_rate = 1.0
vector_rate = 0.2

F32 = jnp.float32
BF16 = jnp.bfloat16
LOG2E = math.log2(math.e)
FACTOR = 1.0 / math.sqrt(C // HEADS)
INVALID = -1000000000.0
VMEM_LIMIT = 60 * 1024 * 1024


def dot(left, right):
    return lax.dot_general(left, right, (((1,), (0,)), ((), ())), preferred_element_type=F32)


def dot_nt(left, right):
    return lax.dot_general(left, right, (((1,), (1,)), ((), ())), preferred_element_type=F32)


def dot_tn(left, right):
    return lax.dot_general(left, right, (((0,), (0,)), ((), ())), preferred_element_type=F32)


def layer_stats(values):
    center = values - jnp.mean(values, axis=-1, keepdims=True)
    inverse = lax.rsqrt(jnp.mean(center * center, axis=-1, keepdims=True) + 1e-05)
    return (center * inverse, inverse)


def layer_back(normed, inverse, grad_norm):
    return inverse * (
        grad_norm
        - jnp.mean(grad_norm, axis=-1, keepdims=True)
        - normed * jnp.mean(grad_norm * normed, axis=-1, keepdims=True)
    )


def pipeline(stages):
    waiting = list(stages)
    active = []
    while waiting or active:
        if waiting:
            active.append(waiting.pop(0))
        active = [item for item in active if next(item, active) is None]
        yield


def beside(items):
    active = list(items)
    while active:
        active = [item for item in active if next(item, active) is None]
        yield


def together(streams):
    count = len(streams[0])
    for at in range(count + len(streams) - 1):
        pipes = []
        for behind, phases in enumerate(streams):
            if 0 <= at - behind < count:
                depth, stages = phases[at - behind]
                pipes.append([pipeline(stages), depth + len(stages), 0])
        longest = max(length for _, length, _ in pipes)
        for tick in range(1, longest + 1):
            for item in pipes:
                while item[2] * longest < tick * item[1]:
                    item[2] += 1
                    next(item[0], None)
        for pipe, _, _ in pipes:
            for _ in pipe:
                pass


def rows_sum(values):
    return jnp.sum(values, axis=0, keepdims=True)


def bias_kernel(pair_ref, pw_ref, bias_ref, root_ref, expand, flat):
    group = pl.program_id(1)
    per_step = bias_ref.shape[1]
    atoms = pl.num_programs(1) * per_step * QW
    span = QW * PAIR

    @pl.when((pl.program_id(0) == 0) & (group == 0))
    def _():
        rows = lax.broadcasted_iota(jnp.int32, (span, C), 0) // PAIR
        lanes = lax.broadcasted_iota(jnp.int32, (span, C), 1) % QW
        wide = lax.dot_general(
            pw_ref[...],
            head_lanes(),
            (((0,), (0,)), ((), ())),
            precision=lax.Precision.HIGHEST,
            preferred_element_type=F32,
        )
        weight = wide - jnp.mean(wide, axis=0, keepdims=True)
        full = jnp.where(rows == lanes, jnp.concatenate([weight] * QW, axis=0), 0.0)
        high = full.astype(BF16)
        expand[:, :C] = high
        expand[:, C:] = (full - high.astype(F32)).astype(BF16)

    def one(w):
        low = pair_ref[0, w * QW : w * QW + QW].reshape(span, KW)
        flat[w * span : w * span + span] = low.astype(F32)
        yield
        out = dot_tn(low, expand[...])
        roots = []
        for part in range(QW // 8):
            start = w * span + part * 8 * PAIR
            channels = [flat[pl.ds(start + c, 8, stride=PAIR), :] for c in range(PAIR)]
            mean = sum(channels[1:], channels[0]) * (1.0 / PAIR)
            center = [channel - mean for channel in channels]
            squares = [value * value for value in center]
            spread = sum(squares[1:], squares[0]) * (1.0 / PAIR)
            roots.append(lax.rsqrt(spread + 1e-05))
        yield
        root = jnp.concatenate(roots * HEADS, axis=0).T
        value = (out[:, :C] + out[:, C:]) * (root * LOG2E)
        start = lax.axis_index("win") * atoms + (group * per_step + w) * QW - HALO
        position = start + lax.broadcasted_iota(jnp.int32, (KW, C), 0)
        valid = (position >= 0) & (position < lax.axis_size("win") * atoms)
        bias_ref[0, w] = jnp.where(valid, value, INVALID * LOG2E)
        root_ref[0, w] = root.astype(BF16)

    for _ in pipeline([one(w) for w in range(per_step)]):
        pass


def head_lanes():
    rows = lax.broadcasted_iota(jnp.int32, (HEADS, C), 0)
    lanes = lax.broadcasted_iota(jnp.int32, (HEADS, C), 1) // QW
    return jnp.where(rows == lanes, 1.0, 0.0)


def bias_table(pair, turned_weight):
    structs, atoms = pair.shape[:2]
    count = min(16, atoms // QW)
    rows = count * QW
    table = pl.BlockSpec((1, count, KW, C), lambda s, i: (s, i, 0, 0))
    return pl.pallas_call(
        bias_kernel,
        grid=(structs, atoms // rows),
        in_specs=[
            pl.BlockSpec((1, rows, PAIR, KW), lambda s, i: (s, i, 0, 0)),
            pl.BlockSpec((HEADS, PAIR), lambda s, i: (0, 0)),
        ],
        out_specs=[table, table],
        scratch_shapes=[
            pltpu.VMEM((QW * PAIR, 2 * C), BF16),
            pltpu.VMEM((rows * PAIR, KW), F32),
        ],
        out_shape=[
            jax.ShapeDtypeStruct((structs, atoms // QW, KW, C), F32),
            jax.ShapeDtypeStruct((structs, atoms // QW, KW, C), BF16),
        ],
        compiler_params=pltpu.CompilerParams(vmem_limit_bytes=VMEM_LIMIT),
        cost_estimate=pl.CostEstimate(flops=10**9, bytes_accessed=15 * 2**20, transcendentals=0),
        name="pair_bias",
    )(pair, turned_weight)


def main_kernel(
    ids_ref,
    x_ref,
    xlo_ref,
    xhi_ref,
    g_ref,
    bias_hbm,
    root_hbm,
    pair_ref,
    cond_ref,
    clo_ref,
    chi_ref,
    w_ref,
    vec_ref,
    out_ref,
    grad_ref,
    rlo_ref,
    rhi_ref,
    send_ref,
    keep_ref,
    packed_ref,
    bias_ref,
    root_ref,
    table_sem,
    dbias_ref,
    dvec_ref,
    pair_scr,
    pair_sem,
    pair_total,
    wq,
    w6,
    win,
    wo,
    wqt,
    w6t,
    wint,
    wot,
    wc1,
    wc2,
    mask,
    t_s1,
    t_h1,
    t_hs,
    t_hh,
    t_g1,
    t_s2,
    t_h2,
    t_g2,
    a_s1,
    a_h1,
    a_g1,
    a_s2,
    a_h2,
    a_g2,
    a_hs,
    a_hh,
    nh_scr,
    ih_scr,
    ah_scr,
    k_scr,
    v_scr,
    q_scr,
    gate_scr,
    ada_scr,
    n1_scr,
    inv_scr,
    o_scr,
    p_scr,
    do_scr,
    dd_scr,
    d4_scr,
    dk_scr,
    dv_scr,
    dx_scr,
):
    step = pl.program_id(0)
    structs, atoms, _ = cond_ref.shape
    windows = atoms // QW
    unroll = min(UNROLL, windows)
    tile = min(TILE, atoms)
    tiles = atoms // tile
    s = [lax.rem(ids_ref[step * PACK + b], structs) for b in range(PACK)]

    def cond_rows(source):
        normed, _ = layer_stats(source)
        one = (normed * vec_ref[0:1]).astype(BF16)
        two = (normed * vec_ref[4:5]).astype(BF16)
        return normed, one, two

    def block(at):
        return packed_ref.at[at * C : at * C + C]

    def joined(ref, st):
        return ref[st].astype(F32) + ref[structs + st].astype(F32)

    bias_copy = pltpu.make_async_copy(bias_hbm, bias_ref, table_sem.at[0])
    root_copy = pltpu.make_async_copy(root_hbm, root_ref, table_sem.at[1])
    chunk = min(8, windows)
    chunks = structs * windows // chunk

    def pair_copy(at):
        st, first = divmod(at * chunk, windows)
        return pltpu.make_async_copy(
            pair_ref.at[st, pl.ds(first * QW, chunk * QW)],
            pair_scr.at[at % SLOTS],
            pair_sem.at[at % SLOTS],
        )

    @pl.when(step == 0)
    def _():
        bias_copy.start()
        root_copy.start()
        for at in range(min(SLOTS, chunks)):
            pair_copy(at).start()

        def low(b):
            return w_ref[b].astype(BF16)

        for at, b in enumerate((2, 5, 3, 4)):
            wq[:, at * C : at * C + C] = low(b)
        w6[...] = low(6)
        for at in range(4):
            win[:, at * C : at * C + C] = low(11 + at)
        for at in range(2):
            wo[at * C : at * C + C, :] = low(15 + at)
        for source, turned in ((wq, wqt), (w6, w6t), (win, wint), (wo, wot)):
            turned[...] = source[...].T
        for at, b in enumerate((0, 1, 7)):
            wc1[:, at * C : at * C + C] = low(b)
        for at, b in enumerate((8, 9, 10)):
            wc2[:, at * C : at * C + C] = low(b)
        rows_head = lax.broadcasted_iota(jnp.int32, (C, C), 0) // QW
        lane_head = lax.broadcasted_iota(jnp.int32, (C, C), 1) // (C // HEADS)
        mask[...] = jnp.where(rows_head == lane_head, 1.0, 0.0).astype(BF16)
        for acc in (a_s1, a_h1, a_g1, a_s2, a_h2, a_g2, a_hs, a_hh, packed_ref, dvec_ref):
            acc[...] = jnp.zeros_like(acc)
        dbias_ref[...] = jnp.zeros_like(dbias_ref)
        pair_total[...] = jnp.zeros_like(pair_total)

        def table(st, i):
            rows = pl.ds(i * tile, tile)
            _, one, two = cond_rows(cond_ref[st, rows])
            yield
            first = dot(one, wc1[...])
            second = dot(two, wc2[...])
            yield
            t_s1[st, rows] = jax.nn.sigmoid(first[:, :C] + vec_ref[1:2])
            t_h1[st, rows] = first[:, C : 2 * C]
            t_g1[st, rows] = jax.nn.sigmoid(first[:, 2 * C :] + vec_ref[3:4])
            t_s2[st, rows] = jax.nn.sigmoid(second[:, :C] + vec_ref[5:6])
            t_h2[st, rows] = second[:, C : 2 * C]
            t_g2[st, rows] = jax.nn.sigmoid(second[:, 2 * C :] + vec_ref[6:7])

        def table_halo(st):
            source = jnp.concatenate([joined(clo_ref, st), joined(chi_ref, st)], axis=0)
            _, one, _ = cond_rows(source)
            yield
            first = dot(one, wc1[:, : 2 * C])
            yield
            t_hs[st] = jax.nn.sigmoid(first[:, :C] + vec_ref[1:2])
            t_hh[st] = first[:, C:]

        items = [table_halo(st) for st in range(structs)]
        items += [table(st, i) for st in range(structs) for i in range(tiles)]
        for _ in pipeline(items):
            pass

    @pl.when(step == 0)
    def _():
        bias_copy.wait()

    def project(b, i):
        start = i * tile
        rows = pl.ds(start, tile)
        pad = pl.ds(start + HALO, tile)
        normed, inverse = layer_stats(x_ref[b, rows].astype(F32))
        n1_scr[b, rows] = normed
        inv_scr[b, rows] = jnp.broadcast_to(inverse, (tile, C))
        ada = (t_s1[s[b], rows] * normed + t_h1[s[b], rows]).astype(BF16)
        ada_scr[b, rows] = ada
        yield
        out = dot(ada, wq[...])
        yield
        q_scr[b, rows] = (out[:, :C] + vec_ref[2:3]).astype(BF16)
        gate_scr[b, rows] = jax.nn.sigmoid(out[:, C : 2 * C])
        k_scr[b, pad] = out[:, 2 * C : 3 * C].astype(BF16)
        v_scr[b, pad] = out[:, 3 * C :].astype(BF16)

    def project_halo(b):
        halo = jnp.concatenate([xlo_ref[b], xhi_ref[b]], axis=0).astype(F32)
        normed, inverse = layer_stats(halo)
        ada = (t_hs[s[b]] * normed + t_hh[s[b]]).astype(BF16)
        nh_scr[b] = normed
        ih_scr[b] = jnp.broadcast_to(inverse, (2 * HALO, C))
        ah_scr[b] = ada
        yield
        out = dot(ada, wq[:, 2 * C :])
        yield
        k_scr[b, :HALO] = out[:HALO, :C].astype(BF16)
        v_scr[b, :HALO] = out[:HALO, C:].astype(BF16)
        k_scr[b, HALO + atoms :] = out[HALO:, :C].astype(BF16)
        v_scr[b, HALO + atoms :] = out[HALO:, C:].astype(BF16)

    lane_head = lax.broadcasted_iota(jnp.int32, (QW, C), 1) // (C // HEADS)

    def spread(rows):
        return jnp.concatenate([rows] * HEADS, axis=0) * mask[...]

    def gathered(full):
        parts = [full[h * QW : h * QW + QW] for h in range(HEADS)]
        last = parts[HEADS - 1]
        for h in range(HEADS - 2, -1, -1):
            last = jnp.where(lane_head == h, parts[h], last)
        return last

    def attend(b, group):
        scores = []
        for w in group:
            queries = spread(q_scr[b, w * QW : w * QW + QW])
            scores.append(dot(k_scr[b, w * QW : w * QW + KW], queries.T))
        yield
        probs = []
        for u, w in enumerate(group):
            value = scores[u] * (FACTOR * LOG2E) + bias_ref[s[b], w]
            exps = jnp.exp2(value - jnp.max(value, axis=0, keepdims=True))
            prob = (exps * (1.0 / rows_sum(exps))).astype(BF16)
            p_scr[b, w] = prob
            probs.append(prob)
        yield
        fulls = [dot_tn(probs[u], v_scr[b, w * QW : w * QW + KW]) for u, w in enumerate(group)]
        yield
        for u, w in enumerate(group):
            o_scr[b, w * QW : w * QW + QW] = gathered(fulls[u])

    def middle(b, i):
        rows = pl.ds(i * tile, tile)
        gate = gate_scr[b, rows]
        mixed = o_scr[b, rows]
        y = (gate * mixed).astype(BF16)
        yield
        attn = dot(y, w6[...])
        yield
        gate_one = t_g1[s[b], rows]
        x1 = x_ref[b, rows].astype(F32) + gate_one * attn
        normed, inverse = layer_stats(x1)
        scale_two = t_s2[s[b], rows]
        ada = (scale_two * normed + t_h2[s[b], rows]).astype(BF16)
        yield
        expand = dot(ada, win[...])
        yield
        a = expand[:, :FF]
        up = expand[:, FF:]
        sig = jax.nn.sigmoid(a)
        silu = a * sig
        hid = (silu * up).astype(BF16)
        yield
        ff = dot(hid, wo[...])
        gate_two = t_g2[s[b], rows]
        g = g_ref[b, rows].astype(F32)
        dff = (g * gate_two).astype(BF16)
        dhid = dot(dff, wot[...])
        yield
        out_ref[b, rows] = (x1 + gate_two * ff).astype(BF16)
        a_g2[s[b], rows] += g * ff
        da = (dhid * up * (sig + silu * (1.0 - sig))).astype(BF16)
        db = (dhid * silu).astype(BF16)
        dab = jnp.concatenate([da, db], axis=1)
        yield
        dada = dot(dab, wint[...])
        yield
        a_s2[s[b], rows] += dada * normed
        a_h2[s[b], rows] += dada
        dx1 = g + layer_back(normed, inverse, dada * scale_two)
        dx_scr[b, rows] = dx1
        a_g1[s[b], rows] += dx1 * attn
        dattn = (dx1 * gate_one).astype(BF16)
        yield
        dy = dot(dattn, w6t[...])
        dwo = dot_tn(dff, hid)
        dwin = dot_tn(ada, dab)
        dw6 = dot_tn(y, dattn)
        yield
        do = (dy * gate).astype(BF16)
        do_scr[b, rows] = do
        dd_scr[b, rows] = (do.astype(F32) * mixed * -1.0).astype(BF16)
        d4_scr[b, rows, C : 2 * C] = (dy * mixed * gate * (1.0 - gate)).astype(BF16)
        block(15)[...] += dwo[:, :C]
        block(16)[...] += dwo[:, C:]
        for at in range(4):
            block(11 + at)[...] += dwin[:, at * C : at * C + C]
        block(6)[...] += dw6

    ones = jnp.ones((KW, C), BF16)

    def attend_back(b, group):
        diffs = []
        spreads = []
        for w in group:
            dox = spread(do_scr[b, w * QW : w * QW + QW])
            ddx = spread(dd_scr[b, w * QW : w * QW + QW])
            values = jnp.concatenate([v_scr[b, w * QW : w * QW + KW], ones], axis=1)
            diffs.append(dot(values, jnp.concatenate([dox.T, ddx.T], axis=0)))
            spreads.append(dox)
        yield
        grads = []
        for u, w in enumerate(group):
            ds = p_scr[b, w].astype(F32) * diffs[u]
            dbias_ref[s[b], w] += ds
            grads.append(ds.astype(BF16))
        yield
        fulls = []
        dks = []
        dvs = []
        for u, w in enumerate(group):
            fulls.append(dot_tn(grads[u], k_scr[b, w * QW : w * QW + KW]))
            dks.append(dot(grads[u], spread(q_scr[b, w * QW : w * QW + QW])))
            dvs.append(dot(p_scr[b, w], spreads[u]))
        yield
        for u, w in enumerate(group):
            dq = gathered(fulls[u]) * FACTOR
            dvec_ref[2] += jnp.sum(dq.reshape(QW // 8, 8, C), axis=0)
            d4_scr[b, w * QW : w * QW + QW, :C] = dq.astype(BF16)
            seen = KW - QW if w else 0
            for scr, part in ((dk_scr, dks[u]), (dv_scr, dvs[u])):
                if seen:
                    scr[b, w * QW : w * QW + seen] += part[:seen]
                scr[b, w * QW + seen : w * QW + KW] = part[seen:]

    def finish(b, i):
        start = i * tile
        rows = pl.ds(start, tile)
        pad = pl.ds(start + HALO, tile)
        d4_scr[b, rows, 2 * C : 3 * C] = (dk_scr[b, pad] * FACTOR).astype(BF16)
        d4_scr[b, rows, 3 * C :] = dv_scr[b, pad].astype(BF16)
        yield
        d4 = d4_scr[b, rows]
        dwq = dot_tn(ada_scr[b, rows], d4)
        dada = dot(d4, wqt[...])
        yield
        for at, which in enumerate((2, 5, 3, 4)):
            block(which)[...] += dwq[:, at * C : at * C + C]
        normed = n1_scr[b, rows]
        a_s1[s[b], rows] += dada * normed
        a_h1[s[b], rows] += dada
        grad = dx_scr[b, rows] + layer_back(normed, inv_scr[b, rows], dada * t_s1[s[b], rows])
        dx_scr[b, rows] = grad
        grad_ref[b, rows] = grad.astype(BF16)

    def finish_halo(b):
        spans = (slice(0, HALO), slice(HALO + atoms, None))
        dk = jnp.concatenate([dk_scr[b, span] for span in spans], axis=0) * FACTOR
        dv = jnp.concatenate([dv_scr[b, span] for span in spans], axis=0)
        dkv = jnp.concatenate([dk.astype(BF16), dv.astype(BF16)], axis=1)
        yield
        dw = dot_tn(ah_scr[b], dkv)
        dada = dot(dkv, wqt[2 * C :])
        yield
        block(3)[...] += dw[:, :C]
        block(4)[...] += dw[:, C:]
        normed = nh_scr[b]
        a_hs[s[b]] += dada * normed
        a_hh[s[b]] += dada
        rim = layer_back(normed, ih_scr[b], dada * t_hs[s[b]]).astype(BF16)
        rlo_ref[b] = rim[:HALO]
        rhi_ref[b] = rim[HALO:]

    groups = [tuple(range(at, at + unroll)) for at in range(0, windows, unroll)]
    width = min(BACK, windows)
    backs = [tuple(range(at, at + width)) for at in range(0, windows, width)]

    def phases(b):
        return [
            (3, [project_halo(b)] + [project(b, i) for i in range(tiles)]),
            (4, [attend(b, group) for group in groups]),
            (11, [middle(b, i) for i in range(tiles)]),
            (4, [attend_back(b, group) for group in backs]),
            (3, [finish_halo(b)] + [finish(b, i) for i in range(tiles)]),
        ]

    together([phases(b) for b in range(PACK)])

    @pl.when(step == pl.num_programs(0) - 1)
    def _():
        for at in (15, 16):
            block(at)[...] = block(at)[...].T

        def apply(source, normed, parts, weight, blocks, gain):
            joined_parts = jnp.concatenate(parts, axis=1)
            grads = dot_tn(source, joined_parts)
            back = dot_nt(joined_parts, weight) * normed
            for at, which in enumerate(blocks):
                block(which)[...] += grads[:, at * C : at * C + C]
            dvec_ref[gain] += jnp.sum(back.reshape(-1, 8, C), axis=0)

        def bias_sum(at, part):
            dvec_ref[at] += jnp.sum(part.astype(F32).reshape(-1, 8, C), axis=0)

        def pre(total, gate):
            return (total * gate * (1.0 - gate)).astype(BF16)

        def conditioning(st, i):
            rows = pl.ds(i * tile, tile)
            normed, one, two = cond_rows(cond_ref[st, rows])
            first = [
                pre(a_s1[st, rows], t_s1[st, rows]),
                a_h1[st, rows].astype(BF16),
                pre(a_g1[st, rows], t_g1[st, rows]),
            ]
            second = [
                pre(a_s2[st, rows], t_s2[st, rows]),
                a_h2[st, rows].astype(BF16),
                pre(a_g2[st, rows], t_g2[st, rows]),
            ]
            yield
            for at, part in ((1, first[0]), (3, first[2]), (5, second[0]), (6, second[2])):
                bias_sum(at, part)
            apply(one, normed, first, wc1[...], (0, 1, 7), 0)
            apply(two, normed, second, wc2[...], (8, 9, 10), 4)

        def conditioning_halo(st):
            source = jnp.concatenate([joined(clo_ref, st), joined(chi_ref, st)], axis=0)
            normed, one, _ = cond_rows(source)
            parts = [pre(a_hs[st], t_hs[st]), a_hh[st].astype(BF16)]
            yield
            bias_sum(1, parts[0])
            apply(one, normed, parts, wc1[:, : 2 * C], (0, 1), 0)

        items = [conditioning_halo(st) for st in range(structs)]
        items += [conditioning(st, i) for st in range(structs) for i in range(tiles)]
        for _ in pipeline(items):
            pass

        root_copy.wait()
        for at in range(chunks):
            pair_copy(at).wait()
            st, first = divmod(at * chunk, windows)
            lefts = []
            rights = []
            for w in range(chunk):
                lefts.append(
                    pair_scr[at % SLOTS, w * QW : w * QW + QW].reshape(QW * PAIR, KW)
                )
                grad = dbias_ref[st, first + w] * root_ref[st, first + w].astype(F32)
                rights.append(grad.astype(BF16))
            left = jnp.concatenate(lefts, axis=1)
            pair_total[...] += dot(left, jnp.concatenate(rights, axis=0))
            if at + SLOTS < chunks:
                pair_copy(at + SLOTS).start()
        lanes = lax.broadcasted_iota(jnp.int32, (PAIR, C), 1) % QW
        acc = jnp.zeros((PAIR, C), F32)
        for q in range(QW):
            acc = acc + jnp.where(lanes == q, pair_total[q * PAIR : q * PAIR + PAIR], 0.0)
        half = NBLK * C // 2
        side = (lax.axis_index("samp") // 2) % 2
        send = packed_ref[pl.ds(pl.multiple_of((1 - side) * half, 64), half)]
        keep_ref[...] = packed_ref[pl.ds(pl.multiple_of(side * half, 64), half)]
        small = jnp.concatenate(
            [rows_sum(dvec_ref[at]) for at in range(7)]
            + [jnp.zeros((1, C), F32), acc - jnp.mean(acc, axis=0, keepdims=True)],
            axis=0,
        )
        high, low = split_low(small)
        send_ref[:half] = send.astype(BF16)
        send_ref[half:] = jnp.concatenate([high, low], axis=0)


def main_call(
    ids, atoms, low_msg, high_msg, cotangent, bias, root, pair, cond, weights, vectors
):
    samples, rows, _ = atoms.shape
    structs = cond.shape[0]
    windows = rows // QW
    padded = rows + 2 * HALO

    def per_sample(*shape):
        zeros = (0,) * len(shape)
        return pl.BlockSpec((PACK,) + shape, lambda i, _: (i,) + zeros)

    def whole(*shape):
        zeros = (0,) * len(shape)
        return pl.BlockSpec(shape, lambda i, _: zeros, pipeline_mode=pl.Buffered(1))

    def table(count=rows):
        return pltpu.VMEM((structs, count, C), F32)

    cond_part = pl.BlockSpec((2 * structs, HALO, C), lambda i, _: (samples // (2 * structs), 0, 0))
    shape = jax.ShapeDtypeStruct
    return pl.pallas_call(
        main_kernel,
        grid_spec=pltpu.PrefetchScalarGridSpec(
            num_scalar_prefetch=1,
            grid=(samples // PACK,),
            in_specs=[
                per_sample(rows, C),
                per_sample(HALO, C),
                per_sample(HALO, C),
                per_sample(rows, C),
                pl.BlockSpec(memory_space=pl.ANY),
                pl.BlockSpec(memory_space=pl.ANY),
                pl.BlockSpec(memory_space=pl.ANY),
                whole(structs, rows, C),
                cond_part,
                cond_part,
                whole(NBLK, C, C),
                whole(7, C),
            ],
            out_specs=[
                per_sample(rows, C),
                per_sample(rows, C),
                per_sample(HALO, C),
                per_sample(HALO, C),
                whole(NBLK * C // 2 + 2 * (8 + PAIR), C),
                whole(NBLK * C // 2, C),
            ],
            scratch_shapes=[
                pltpu.VMEM((NBLK * C, C), F32),
                pltpu.VMEM((structs, windows, KW, C), F32),
                pltpu.VMEM((structs, windows, KW, C), BF16),
                pltpu.SemaphoreType.DMA((2,)),
                pltpu.VMEM((structs, windows, KW, C), F32),
                pltpu.VMEM((7, 8, C), F32),
                pltpu.VMEM((SLOTS, min(rows, 8 * QW), PAIR, KW), BF16),
                pltpu.SemaphoreType.DMA((SLOTS,)),
                pltpu.VMEM((QW * PAIR, C), F32),
                pltpu.VMEM((C, 4 * C), BF16),
                pltpu.VMEM((C, C), BF16),
                pltpu.VMEM((C, 2 * FF), BF16),
                pltpu.VMEM((FF, C), BF16),
                pltpu.VMEM((4 * C, C), BF16),
                pltpu.VMEM((C, C), BF16),
                pltpu.VMEM((2 * FF, C), BF16),
                pltpu.VMEM((C, FF), BF16),
                pltpu.VMEM((C, 3 * C), BF16),
                pltpu.VMEM((C, 3 * C), BF16),
                pltpu.VMEM((C, C), BF16),
                table(),
                table(),
                table(2 * HALO),
                table(2 * HALO),
                table(),
                table(),
                table(),
                table(),
                table(),
                table(),
                table(),
                table(),
                table(),
                table(),
                table(2 * HALO),
                table(2 * HALO),
                pltpu.VMEM((PACK, 2 * HALO, C), F32),
                pltpu.VMEM((PACK, 2 * HALO, C), F32),
                pltpu.VMEM((PACK, 2 * HALO, C), BF16),
                pltpu.VMEM((PACK, padded, C), BF16),
                pltpu.VMEM((PACK, padded, C), BF16),
                pltpu.VMEM((PACK, rows, C), BF16),
                pltpu.VMEM((PACK, rows, C), F32),
                pltpu.VMEM((PACK, rows, C), BF16),
                pltpu.VMEM((PACK, rows, C), F32),
                pltpu.VMEM((PACK, rows, C), F32),
                pltpu.VMEM((PACK, rows, C), F32),
                pltpu.VMEM((PACK, windows, KW, C), BF16),
                pltpu.VMEM((PACK, rows, C), BF16),
                pltpu.VMEM((PACK, rows, C), BF16),
                pltpu.VMEM((PACK, rows, 4 * C), BF16),
                pltpu.VMEM((PACK, padded, C), F32),
                pltpu.VMEM((PACK, padded, C), F32),
                pltpu.VMEM((PACK, rows, C), F32),
            ],
        ),
        out_shape=[
            shape((samples, rows, C), BF16),
            shape((samples, rows, C), BF16),
            shape((samples, HALO, C), BF16),
            shape((samples, HALO, C), BF16),
            shape((NBLK * C // 2 + 2 * (8 + PAIR), C), BF16),
            shape((NBLK * C // 2, C), F32),
        ],
        compiler_params=pltpu.CompilerParams(vmem_limit_bytes=VMEM_LIMIT),
        name="block",
    )(
        ids,
        atoms,
        low_msg,
        high_msg,
        cotangent,
        bias,
        root,
        pair,
        cond,
        low_msg,
        high_msg,
        weights,
        vectors,
    )


def split_low(values):
    high = values.astype(BF16)
    return high, (values - high.astype(F32)).astype(BF16)


def update_kernel(
    own_ref,
    other_ref,
    small_ref,
    sl_ref,
    sr_ref,
    rl_ref,
    rr_ref,
    w_ref,
    ew_ref,
    vec_ref,
    sv_ref,
    ev_ref,
    pw_ref,
    sp_ref,
    ep_ref,
    rows_ref,
    tv_ref,
    tp_ref,
    left_ref,
    right_ref,
    neww_ref,
    low_ref,
    newv_ref,
    newp_ref,
    nsv_ref,
    nsp_ref,
    neww_ema_ref,
    newv_ema_ref,
    newp_ema_ref,
    turned,
    total_ref,
):
    chunks, size, _ = own_ref.shape
    side = lax.axis_index("samp") % 2
    for at in range(chunks):
        for ref, place in ((own_ref, side), (other_ref, 1 - side)):
            start = pl.multiple_of((2 * at + place) * size, 16)
            total_ref[pl.ds(start, size)] = ref[at].astype(F32)
    count = sl_ref.shape[1]
    own = pl.ds(lax.axis_index("win") * count, count)

    def product(parts, right):
        high, low = split_low(right)
        lefts = [split_low(part) for part in parts]
        tall = jnp.concatenate([a for a, _ in lefts] + [b for _, b in lefts], axis=0)
        size = tall.shape[0] // 2
        first = dot(tall, high)
        return first[:size] + first[size:] + dot(tall[:size], low)

    def one(b):
        block = total_ref[b * C : b * C + C]
        turned[b] = block.T
        pad = jnp.zeros((16 - count, C), F32) if count < 16 else None

        def rows(values):
            return values if pad is None else jnp.concatenate([values, pad], axis=0)

        own_rows = total_ref[pl.ds(b * C + lax.axis_index("win") * count, count)]
        rows_ref[b] = own_rows
        yield
        own_cols = turned[b, own]
        both = product([rows(own_cols), rows(rl_ref[b])], block)
        left = product([rows(own_rows)], turned[b])
        size = max(count, 16)
        yield
        step = product([both[size:]], rr_ref[b])
        right_ref[b] = stat_decay * sr_ref[b] + (1.0 - stat_decay) * both[:count]
        left_ref[b] = stat_decay * sl_ref[b] + (1.0 - stat_decay) * left[:count]
        yield
        new = w_ref[b, own] - matrix_rate * step[:count]
        neww_ref[b] = new
        low_ref[b] = new.astype(BF16)
        neww_ema_ref[b] = ema_decay * ew_ref[b] + (1.0 - ema_decay) * new

    for _ in pipeline([beside([one(b) for b in range(at, min(at + 9, NBLK))]) for at in range(0, NBLK, 9)]):
        pass
    sums = small_ref[8:]
    pair_total = lax.dot_general(
        head_lanes(),
        sums,
        (((1,), (1,)), ((), ())),
        precision=lax.Precision.HIGHEST,
        preferred_element_type=F32,
    )
    for total, param, stat, ema, out, new_ref, stat_ref, ema_ref in (
        (small_ref[:7], vec_ref, sv_ref, ev_ref, tv_ref, newv_ref, nsv_ref, newv_ema_ref),
        (pair_total, pw_ref, sp_ref, ep_ref, tp_ref, newp_ref, nsp_ref, newp_ema_ref),
    ):
        out[...] = total
        new_stat = stat_decay * stat[...] + (1.0 - stat_decay) * total * total
        stat_ref[...] = new_stat
        new = param[...] - vector_rate * total * lax.rsqrt(new_stat)
        new_ref[...] = new
        ema_ref[...] = ema_decay * ema[...] + (1.0 - ema_decay) * new


def update_call(*args):
    rows = args[3].shape
    vec = args[9].shape
    pw = args[12].shape
    full = pl.BlockSpec(memory_space=pltpu.VMEM)

    def shape(dims, kind=F32):
        return jax.ShapeDtypeStruct(dims, kind)

    def out_block(dims):
        zeros = (0,) * len(dims)
        return pl.BlockSpec(dims, lambda i: zeros)

    outs = [rows, vec, pw, rows, rows, rows, rows, vec, pw, vec, pw, rows, vec, pw]
    return pl.pallas_call(
        update_kernel,
        grid=(1,),
        in_specs=[full] * len(args),
        out_specs=[out_block(dims) for dims in outs],
        out_shape=[
            shape(dims, BF16 if at == 6 else F32) for at, dims in enumerate(outs)
        ],
        scratch_shapes=[pltpu.VMEM((NBLK, C, C), F32), pltpu.VMEM((NBLK * C, C), F32)],
        compiler_params=pltpu.CompilerParams(vmem_limit_bytes=VMEM_LIMIT),
        name="update",
    )(*args)


def passed(shard, by):
    devices = lax.axis_size("win")
    pairs = [(i, i + by) for i in range(devices) if 0 <= i + by < devices]
    return lax.ppermute(shard, "win", pairs)


def rounded(values):
    return lax.reduce_precision(values, exponent_bits=8, mantissa_bits=7)


def partner(values, axis, bit):
    devices = lax.axis_size(axis)
    return lax.ppermute(values, axis, [(i, i ^ bit) for i in range(devices)])


def bits(axis):
    devices = lax.axis_size(axis)
    return [(axis, 1 << at) for at in range((devices - 1).bit_length())]


def exchange(part, small, axis, bit):
    size = part.shape[0]
    high = rounded(small)
    rest = rounded(small - high)
    message = [part.astype(BF16), high.astype(BF16), rest.astype(BF16)]
    got = partner(jnp.concatenate(message, axis=0), axis, bit)
    return got[:size].astype(F32), joined_terms(got[size:]) + (high + rest)


def joined_terms(terms):
    count = terms.shape[0] // 2
    wide = terms.astype(F32)
    return wide[:count] + wide[count:]


def summed(send, keep, edges):
    last, *halvings = bits("samp")
    size = keep.shape[0]
    for at, (axis, bit) in enumerate(halvings):
        if at == 0:
            got, edges = lax.optimization_barrier((partner(send, axis, bit), edges))
            values = keep + got[:size].astype(F32)
            small = joined_terms(send[size:]) + joined_terms(got[size:])
        else:
            side = (lax.axis_index(axis) // bit) % 2
            size = values.shape[0] // 2
            kept = lax.dynamic_slice_in_dim(values, side * size, size)
            part = lax.dynamic_slice_in_dim(values, (1 - side) * size, size)
            got, small = exchange(part, small, axis, bit)
            values = kept + got
    axis, bit = last
    side = (lax.axis_index(axis) // bit) % 2
    size = values.shape[0] // 2
    kept = lax.dynamic_slice_in_dim(values, side * size, size)
    part = lax.dynamic_slice_in_dim(values, (1 - side) * size, size)
    got = partner(jnp.concatenate([part, small], axis=0), axis, bit)
    values = kept + got[:size]
    small = small + got[size:]
    for axis, bit in bits("win"):
        values = rounded(values)
        got, small = exchange(values, small, axis, bit)
        values = values + got
    values = values.astype(BF16)[None]
    for axis, bit in reversed(halvings):
        side = (lax.axis_index(axis) // bit) % 2
        other = partner(values, axis, bit)
        values = jnp.where(
            side == 0,
            jnp.concatenate([values, other]),
            jnp.concatenate([other, values]),
        )
    return values, partner(values, *last), small, edges


def body(
    atoms,
    cond,
    pair,
    struct_ids,
    cotangent,
    weights,
    vectors,
    pair_weight,
    stat_left,
    stat_right,
    root_left,
    root_right,
    stat_vectors,
    stat_pair,
    ema_weights,
    ema_vectors,
    ema_pair,
):
    rows = atoms.shape[1]
    messages = []
    for span in (slice(0, HALO), slice(rows - HALO, rows)):
        high = rounded(cond[:, span])
        rest = cond[:, span] - high
        parts = [atoms[:, span], high.astype(BF16), rest.astype(BF16)]
        messages.append(jnp.concatenate(parts, axis=0))
    first, last = messages
    low_msg, high_msg = passed(last, 1), passed(first, -1)
    bias, root = bias_table(pair, pair_weight.T)
    result, grad_atoms, rim_low, rim_high, send, keep = main_call(
        struct_ids, atoms, low_msg, high_msg, cotangent, bias, root, pair, cond, weights, vectors
    )
    edges = (passed(rim_high, 1), passed(rim_low, -1))
    own, other, small, (below, above) = summed(send, keep, edges)
    for span, part in ((slice(0, HALO), below), (slice(rows - HALO, rows), above)):
        edge = grad_atoms[:, span].astype(F32) + part.astype(F32)
        grad_atoms = grad_atoms.at[:, span].set(edge.astype(BF16))
    outs = list(
        update_call(
            own,
            other,
            small,
            stat_left,
            stat_right,
            root_left,
            root_right,
            weights,
            ema_weights,
            vectors,
            stat_vectors,
            ema_vectors,
            pair_weight.T,
            stat_pair.T,
            ema_pair.T,
        )
    )
    for at in (2, 8, 10, 13):
        outs[at] = outs[at].T
    return (result, grad_atoms, *outs)


def solution(mesh):
    placed = (
        P("samp", "win", None),
        P("samp", "win", None),
        P("samp", "win", None, None),
        P("samp"),
        P("samp", "win", None),
        P(),
        P(),
        P(),
        P(None, "win", None),
        P(None, "win", None),
        P(None, "win", None),
        P(),
        P(),
        P(),
        P(None, "win", None),
        P(),
        P(),
    )
    return jax.shard_map(
        body,
        mesh=mesh,
        in_specs=placed,
        out_specs=(
            P("samp", "win", None),
            P("samp", "win", None),
            P(None, "win", None),
            P(),
            P(),
            P(None, "win", None),
            P(None, "win", None),
            P(None, "win", None),
            P(None, "win", None),
            P(),
            P(),
            P(),
            P(),
            P(None, "win", None),
            P(),
            P(),
        ),
        check_vma=False,
    )
```
